128 devices in a mesh: row: 8 (over z_lo, y), col: 16 (over x, z_hi, core).
Axes of the slice: x: 4, y: 4, z: 4 (z_hi: 2, z_lo: 2; z = z_hi * 2 + z_lo), core: 2. Of those that a mesh axis runs over, the one named last changes fastest.
Arguments:
- dst_embed: bfloat16 [16384, 64], P(('row', 'col')), may hold values from -24 to 24
- src_embed: bfloat16 [16384, 64], P(('row', 'col')), may hold values from -24 to 24
- series: bfloat16 [16384, 384], P(('row', 'col')), may hold values from -6 to 6
- w_self: bfloat16 [32, 32], replicated, may hold values from -1 to 1
- w_hop1: bfloat16 [32, 32], replicated, may hold values from -2.390625 to 2.390625
- w_hop2: bfloat16 [32, 32], replicated, may hold values from -9 to 9
- cotangent: bfloat16 [16384, 384], P(('row', 'col')), may hold values from -6 to 6
Outputs:
- output: bfloat16 [16384, 384], P(('row', 'col'))
- d_dst: float32 [16384, 64], P(('row', 'col'))
- d_src: float32 [16384, 64], P(('row', 'col'))
The draws below stay inside these ranges and needn't reach their ends.
All inputs are finite; a program needn't handle non-finite values.
Results may differ from the reference program's by a relative error of at most 0.006.
Values may be sent and summed in bfloat16 or wider, within the bound.
No kernel may reach another device: no remote copies, remote signals or barrier semaphores. Data moves between devices by JAX's collectives and lax.ppermute only.
A program may use at most 128 MiB of HBM per device.

```python
import jax
import jax.numpy as jnp
from jax import lax

RANK = 64
CHAN = 32
FEAT = 384
NODES = 16384


def draw_dst_embed(key, part):
    key = jax.random.fold_in(key, 11)
    values = 0.6 * jax.random.normal(key, (NODES, RANK), jnp.float32)
    return jnp.clip(values, -24.0, 24.0).astype(jnp.bfloat16)


def draw_src_embed(key, part):
    key = jax.random.fold_in(key, 23)
    values = 0.6 * jax.random.normal(key, (NODES, RANK), jnp.float32)
    return jnp.clip(values, -24.0, 24.0).astype(jnp.bfloat16)


def steps_of(stream_key, extent, pieces, low, high):
    level = 1.0
    for dim, shards_of in pieces:
        steps = jax.random.uniform(jax.random.fold_in(jax.random.fold_in(stream_key, 6), dim), (shards_of,), jnp.float32, low / len(pieces), high / len(pieces))
        level = level * jnp.repeat(jnp.exp(steps), extent[dim] // shards_of).reshape((-1,) + (1,) * (len(extent) - 1 - dim))
    return level


def scatter_about(rng, dims, spread, most, shards=(), held_as=jnp.bfloat16):
    values = jax.random.normal(rng, dims, jnp.float32) * spread
    if len(shards) > 0:
        values = steps_of(rng, dims, shards, -0.22, 0.18) * values
    return jnp.clip(values, min=-most, max=most).astype(held_as)


def setup_inputs(seed: int = 0) -> dict:
    seeds = jax.random.split(jax.random.key(seed), 8)
    return {
        "dst_embed": draw_dst_embed(jax.random.fold_in(seeds[7], 71), 0),
        "src_embed": draw_src_embed(jax.random.fold_in(seeds[7], 71), 0),
        "series": scatter_about(seeds[2], (NODES, FEAT), 1.0, 6.0, ((0, 128),)),
        "w_self": scatter_about(seeds[3], (CHAN, CHAN), CHAN ** -0.5, 1.0),
        "w_hop1": scatter_about(seeds[4], (CHAN, CHAN), 0.4, 2.390625),
        "w_hop2": scatter_about(seeds[5], (CHAN, CHAN), 1.5, 9.0),
        "cotangent": scatter_about(seeds[6], (NODES, FEAT), 1.0, 6.0, ((0, 128),)),
    }


def mix_forward(values, weight):
    count_rows = values.shape[0]
    grouped = values.astype(jnp.float32).reshape(count_rows, -1, CHAN)
    return jnp.einsum("nsc,cd->nsd", grouped, weight.astype(jnp.float32)).reshape(count_rows, -1)


def mix_backward(values, weight):
    count_rows = values.shape[0]
    grouped = values.astype(jnp.float32).reshape(count_rows, -1, CHAN)
    return jnp.einsum("nsd,cd->nsc", grouped, weight.astype(jnp.float32)).reshape(count_rows, -1)


def contract_rows(left_op, right_op):
    return lax.dot_general(left_op, right_op, (((0,), (0,)), ((), ())), preferred_element_type=jnp.float32)


def contract_cols(left_op, right_op):
    return lax.dot_general(left_op, right_op, (((1,), (1,)), ((), ())), preferred_element_type=jnp.float32)


def reference(dst_embed, src_embed, series, w_self, w_hop1, w_hop2, cotangent):
    block_count = 16
    block_len = NODES // block_count
    dst_blocks = dst_embed.reshape(block_count, block_len, RANK)

    def adjacency_rows(row_block):
        scores = contract_cols(row_block, src_embed)
        lifted = jnp.maximum(scores, 0.0)
        row_peak = jnp.max(lifted, axis=1, keepdims=True)
        exponent = jnp.exp(lifted - row_peak)
        weights = exponent / jnp.sum(exponent, axis=1, keepdims=True)
        return scores, weights

    def diffuse(features):
        def per_block(row_block):
            weights = adjacency_rows(row_block)[1]
            return jnp.dot(weights.astype(jnp.bfloat16), features, preferred_element_type=jnp.float32).astype(jnp.bfloat16)
        return lax.map(per_block, dst_blocks).reshape(NODES, FEAT)

    hop_first = diffuse(series)
    hop_second = diffuse(hop_first)
    output = (mix_forward(series, w_self) + mix_forward(hop_first, w_hop1) + mix_forward(hop_second, w_hop2)).astype(jnp.bfloat16)

    grad_second = mix_backward(cotangent, w_hop2).astype(jnp.bfloat16)
    second_blocks = grad_second.reshape(block_count, block_len, FEAT)

    def carry_back(running, block_pair):
        row_block, grad_rows = block_pair
        weights = adjacency_rows(row_block)[1].astype(jnp.bfloat16)
        return running + contract_rows(weights, grad_rows), None

    carried, _ = lax.scan(carry_back, jnp.zeros((NODES, FEAT), jnp.float32), (dst_blocks, second_blocks))
    grad_first = (mix_backward(cotangent, w_hop1) + carried).astype(jnp.bfloat16)
    first_blocks = grad_first.reshape(block_count, block_len, FEAT)

    def embed_grads(running, block_triple):
        row_block, grad_two, grad_one = block_triple
        scores, weights = adjacency_rows(row_block)
        adj_grad = contract_cols(grad_two, hop_first) + contract_cols(grad_one, series)
        inner_sum = jnp.sum(weights * adj_grad, axis=1, keepdims=True)
        score_grad = jnp.where(scores > 0.0, weights * (adj_grad - inner_sum), 0.0).astype(jnp.bfloat16)
        d_rows = jnp.dot(score_grad, src_embed, preferred_element_type=jnp.float32)
        return running + contract_rows(score_grad, row_block), d_rows

    d_src, d_dst = lax.scan(embed_grads, jnp.zeros((NODES, RANK), jnp.float32), (dst_blocks, second_blocks, first_blocks))
    return output, d_dst.reshape(NODES, RANK), d_src
```

```python
import jax
import jax.numpy as jnp
from jax import lax
from jax.experimental import pallas as pl
from jax.experimental.pallas import tpu as pltpu
from jax.sharding import PartitionSpec as P

BF16 = jnp.bfloat16
F32 = jnp.float32
GROUP = 8
STEP = 256
VMEM_BYTES = 40 * 1024 * 1024

SAME_CORE = [[2 * chip + core for chip in range(8)] for core in range(2)]
OTHER_CORE = [(i, i ^ 1) for i in range(16)]


def dot_nn(a, b):
    return lax.dot_general(a, b, (((1,), (0,)), ((), ())), preferred_element_type=F32)


def dot_nt(a, b):
    return lax.dot_general(a, b, (((1,), (1,)), ((), ())), preferred_element_type=F32)


def dot_tn(a, b):
    return lax.dot_general(a, b, (((0,), (0,)), ((), ())), preferred_element_type=F32)


def exchange_dst(blocks):
    return lax.all_to_all(blocks, "row", 0, 0)


def exchange_src(blocks):
    return lax.all_to_all(blocks, "col", 0, 0, axis_index_groups=SAME_CORE)


def swap_cores(blocks):
    return lax.ppermute(blocks, "col", OTHER_CORE)


def whole(shape):
    return pl.BlockSpec(shape, lambda *_: (0,) * len(shape))


def call(kernel, steps, ins, in_specs, outs, out_specs, scratch=(), flops=0, exps=0):
    sizes = [a.size * a.dtype.itemsize for a in list(ins) + list(outs)]
    return pl.pallas_call(
        kernel,
        grid=(steps,),
        in_specs=in_specs,
        out_specs=out_specs,
        out_shape=outs,
        scratch_shapes=scratch,
        compiler_params=pltpu.CompilerParams(vmem_limit_bytes=VMEM_BYTES),
        cost_estimate=pl.CostEstimate(flops=flops, bytes_accessed=sum(sizes), transcendentals=exps),
    )(*ins)


def array(shape, dtype):
    return jax.ShapeDtypeStruct(shape, dtype)


HALF = GROUP * 128 // STEP


def first_half(*block):
    return pl.BlockSpec(block, lambda i: (jnp.minimum(i, HALF - 1),) + (0,) * (len(block) - 1))


def second_half(*block):
    return pl.BlockSpec(block, lambda i: (jnp.maximum(i - HALF, 0),) + (0,) * (len(block) - 1))


def by_step(*block):
    return pl.BlockSpec(block, lambda i: (i,) + (0,) * (len(block) - 1))


def pick(own_ref, other_ref):
    return jnp.where(pl.program_id(0) < HALF, own_ref[...], other_ref[...])


def put(own_ref, other_ref, value):
    value = value.astype(own_ref.dtype).reshape(own_ref.shape)

    @pl.when(pl.program_id(0) < HALF)
    def _():
        own_ref[...] = value

    @pl.when(pl.program_id(0) >= HALF)
    def _():
        other_ref[...] = value


def at_step(step):
    return pl.when(pl.program_id(0) == step)


def accumulate(total, part):
    @at_step(0)
    def _():
        total[...] = part

    @pl.when(pl.program_id(0) > 0)
    def _():
        total[...] += part


def mixing(weight):
    size, chan = 384, weight.shape[0]
    place = lax.broadcasted_iota(jnp.int32, (size, chan), 0) % chan
    repeat = jnp.where(place == lax.broadcasted_iota(jnp.int32, (size, chan), 1), 1.0, 0.0).astype(BF16)
    tiled = dot_nt(dot_nn(repeat, weight).astype(BF16), repeat)
    rows = lax.broadcasted_iota(jnp.int32, (size, size), 0) // chan
    cols = lax.broadcasted_iota(jnp.int32, (size, size), 1) // chan
    return jnp.where(rows == cols, tiled, 0.0).astype(BF16)


def prepare_kernel(
    dst_ref, src_ref, series_ref, self_ref, hop1_ref, hop2_ref, cotangent_ref,
    dst_out, src_out, first_out, base_out, mix1_out, mix2_out,
):
    mix1, mix2 = mixing(hop1_ref[...]), mixing(hop2_ref[...])
    cotangent = cotangent_ref[...]
    second = dot_nt(cotangent, mix2).astype(BF16)
    for block in range(GROUP):
        dst_out[block, :, 0:384] = second
        dst_out[block, :, 384:448] = dst_ref[...]
        src_out[block, :, 0:384] = series_ref[...]
        src_out[block, :, 384:448] = src_ref[...]
    first_out[...] = dot_nt(cotangent, mix1)
    base_out[...] = dot_nn(series_ref[...], mixing(self_ref[...]))
    mix1_out[...] = mix1
    mix2_out[...] = mix2


def prepare(*ins):
    outs = [
        array((GROUP, 128, 448), BF16),
        array((GROUP, 128, 448), BF16),
        array((128, 384), F32),
        array((128, 384), F32),
        array((384, 384), BF16),
        array((384, 384), BF16),
    ]
    specs = [whole(a.shape) for a in ins], [whole(a.shape) for a in outs]
    return call(prepare_kernel, 1, ins, specs[0], outs, specs[1], flops=3 * 2 * 128 * 384 * 384)


def stats_kernel(packed_ref, dst_ref, before_ref, out_ref, state):
    lifted = jnp.maximum(dot_nt(packed_ref[:, 384:448], dst_ref[:, 384:448]), 0.0)
    peak = jnp.max(lifted, axis=0, keepdims=True)

    @at_step(0)
    def _():
        state[...] = before_ref[...]

    old = state[0:1, :]
    new = jnp.maximum(old, peak)
    total = jnp.sum(jnp.exp(lifted - new), axis=0, keepdims=True)
    state[1:2, :] = state[1:2, :] * jnp.exp(old - new) + total
    state[0:1, :] = new

    @at_step(pl.num_programs(0) - 1)
    def _():
        out_ref[...] = jnp.broadcast_to(state[...].reshape(out_ref.shape[-2:]), out_ref.shape)


def softmax_stats(packed, dst, before, out_shape):
    rows, src = dst.shape[0], packed.shape[0]
    return call(
        stats_kernel,
        src // STEP,
        (packed, dst, before),
        [by_step(STEP, 448), whole(dst.shape), whole(before.shape)],
        [array(out_shape, F32)],
        [whole(out_shape)],
        [pltpu.VMEM((2, rows), F32)],
        2 * src * rows * 64,
        src * rows,
    )[0]


def weights_of(packed, dst_ref, norm_ref):
    scores = dot_nt(packed[:, 384:448], dst_ref[:, 384:448])
    weights = jnp.exp(jnp.maximum(scores, 0.0) - norm_ref[0:1, :]) * norm_ref[1:2, :]
    return scores, weights


def first_kernel(
    own_ref, other_ref, dst_ref, stats_ref, adj_ref, hop_ref, norm_ref, own_out, other_out, total
):
    @at_step(0)
    def _():
        peak = stats_ref[0, 0:1, :]
        for d in range(1, GROUP):
            peak = jnp.maximum(peak, stats_ref[d, 0:1, :])
        row_sum = jnp.zeros_like(peak)
        for d in range(GROUP):
            row_sum += stats_ref[d, 1:2, :] * jnp.exp(stats_ref[d, 0:1, :] - peak)
        norm_ref[0:1, :] = peak
        norm_ref[1:2, :] = 1.0 / row_sum

    packed = pick(own_ref, other_ref)
    adjacency = weights_of(packed, dst_ref, norm_ref)[1].astype(BF16)
    adj_ref[...] = adjacency
    accumulate(total, dot_tn(packed[:, 0:384], adjacency))
    put(own_out, other_out, dot_nn(adjacency, dst_ref[:, 0:384]))

    @at_step(pl.num_programs(0) - 1)
    def _():
        for block in range(GROUP):
            hop_ref[block] = total[:, 128 * block : 128 * block + 128].astype(BF16)


def adjacency_and_hops(own, other, dst, stats):
    rows, src = dst.shape[0], 2 * own.shape[0]
    outs = [
        array((src, rows), BF16),
        array((GROUP, 384, 128), BF16),
        array((2, rows), F32),
        array((GROUP, 128, 384), BF16),
        array((GROUP, 128, 384), BF16),
    ]
    return call(
        first_kernel,
        2 * HALF,
        (own, other, dst, stats),
        [first_half(STEP, 448), second_half(STEP, 448), whole(dst.shape), whole(stats.shape)],
        outs,
        [
            by_step(STEP, rows),
            whole(outs[1].shape),
            whole(outs[2].shape),
            first_half(STEP // 128, 128, 384),
            second_half(STEP // 128, 128, 384),
        ],
        [pltpu.VMEM((384, rows), F32)],
        2 * src * rows * 832,
        src * rows,
    )


def join_kernel(hop_ref, own_ref, other_ref, pack_ref, hop_out):
    hop = hop_ref[0].astype(F32)
    for d in range(1, GROUP):
        hop += hop_ref[d].astype(F32)
    hop = hop.T.astype(BF16)
    hop_out[...] = hop
    for block in range(GROUP):
        carried = own_ref[block].astype(F32) + other_ref[block].astype(F32)
        pack_ref[block, :, 0:384] = carried.astype(BF16)
        pack_ref[block, :, 384:768] = hop


def join(*ins):
    outs = [array((GROUP, 128, 768), BF16), array((128, 384), BF16)]
    specs = [whole(a.shape) for a in ins], [whole(a.shape) for a in outs]
    return call(join_kernel, 1, ins, specs[0], outs, specs[1])


def split_kernel(pack_ref, first_ref, first_out, hop_out):
    first = first_ref[...]
    for d in range(GROUP):
        first += pack_ref[d, :, 0:384].astype(F32)
        hop_out[128 * d : 128 * d + 128, :] = pack_ref[d, :, 384:768]
    first = first.astype(BF16)
    for block in range(GROUP):
        first_out[block] = first


def split(*ins):
    outs = [array((GROUP, 128, 384), BF16), array((GROUP * 128, 384), BF16)]
    specs = [whole(a.shape) for a in ins], [whole(a.shape) for a in outs]
    return call(split_kernel, 1, ins, specs[0], outs, specs[1])


def second_kernel(adj_ref, own_ref, other_ref, out_ref, total):
    accumulate(total, dot_tn(pick(own_ref, other_ref), adj_ref[...]))

    @at_step(pl.num_programs(0) - 1)
    def _():
        for block in range(GROUP):
            out_ref[block] = total[:, 128 * block : 128 * block + 128].astype(BF16)


def second_hop(adjacency, own, other):
    src, rows = adjacency.shape
    return call(
        second_kernel,
        2 * HALF,
        (adjacency, own, other),
        [by_step(STEP, rows), first_half(STEP, 384), second_half(STEP, 384)],
        [array((GROUP, 384, 128), BF16)],
        [whole((GROUP, 384, 128))],
        [pltpu.VMEM((384, rows), F32)],
        2 * src * rows * 384,
    )[0]


def grad_kernel(
    own_ref, other_ref, hop_own_ref, hop_other_ref, dst_ref, norm_ref, first_ref, second_ref,
    adj_ref, pack_ref, inner,
):
    packed, hop = pick(own_ref, other_ref), pick(hop_own_ref, hop_other_ref)
    weights = weights_of(packed, dst_ref, norm_ref)[1]
    adj_grad = dot_nt(hop, dst_ref[:, 0:384]) + dot_nt(packed[:, 0:384], first_ref[...])
    adj_ref[...] = adj_grad
    accumulate(inner, jnp.sum(weights * adj_grad, axis=0, keepdims=True))

    @at_step(pl.num_programs(0) - 1)
    def _():
        high = inner[...].astype(BF16).astype(F32)
        rest = inner[...] - high
        middle = rest.astype(BF16).astype(F32)
        rows = [
            term[:, 128 * block : 128 * block + 128]
            for term in (high, middle, rest - middle)
            for block in range(GROUP)
        ]
        terms = jnp.concatenate(rows + [jnp.zeros((8, 128), F32)], axis=0).astype(BF16)
        for block in range(GROUP):
            pack_ref[block, 0:384, :] = second_ref[block]
            pack_ref[block, 384:416, :] = terms


def adjacency_grad(own, other, hop_own, hop_other, dst, norm, first, second):
    rows, src = dst.shape[0], 2 * own.shape[0]
    outs = [array((src, rows), F32), array((GROUP, 416, 128), BF16)]
    return call(
        grad_kernel,
        2 * HALF,
        (own, other, hop_own, hop_other, dst, norm, first, second),
        [
            first_half(STEP, 448),
            second_half(STEP, 448),
            first_half(STEP, 384),
            second_half(STEP, 384),
            whole(dst.shape),
            whole(norm.shape),
            whole(first.shape),
            whole(second.shape),
        ],
        outs,
        [by_step(STEP, rows), whole(outs[1].shape)],
        [pltpu.VMEM((1, rows), F32)],
        2 * src * rows * 832,
        src * rows,
    )


def embed_kernel(
    own_ref, other_ref, adj_ref, dst_ref, norm_ref, pack_ref, ddst_ref, own_out, other_out, inner, total
):
    @at_step(0)
    def _():
        terms = pack_ref[0, 384:416, :].astype(F32)
        for d in range(1, GROUP):
            terms += pack_ref[d, 384:416, :].astype(F32)
        rows = terms[0:8] + (terms[8:16] + terms[16:24])
        for block in range(GROUP):
            inner[0:1, 128 * block : 128 * block + 128] = rows[block : block + 1, :]

    packed = pick(own_ref, other_ref)
    scores, weights = weights_of(packed, dst_ref, norm_ref)
    graded = jnp.where(scores > 0.0, weights * (adj_ref[...] - inner[...]), 0.0).astype(BF16)
    accumulate(total, dot_tn(packed[:, 384:448], graded))
    put(own_out, other_out, dot_nn(graded, dst_ref[:, 384:448]))

    @at_step(pl.num_programs(0) - 1)
    def _():
        for block in range(GROUP):
            ddst_ref[block] = total[:, 128 * block : 128 * block + 128]


def embed_grads(own, other, adj_grad, dst, norm, pack):
    src, rows = adj_grad.shape
    outs = [
        array((GROUP, 64, 128), F32),
        array((GROUP, 128, 64), F32),
        array((GROUP, 128, 64), F32),
    ]
    return call(
        embed_kernel,
        2 * HALF,
        (own, other, adj_grad, dst, norm, pack),
        [
            first_half(STEP, 448),
            second_half(STEP, 448),
            by_step(STEP, rows),
            whole(dst.shape),
            whole(norm.shape),
            whole(pack.shape),
        ],
        outs,
        [
            whole(outs[0].shape),
            first_half(STEP // 128, 128, 64),
            second_half(STEP // 128, 128, 64),
        ],
        [pltpu.VMEM((1, rows), F32), pltpu.VMEM((64, rows), F32)],
        6 * src * rows * 64,
        src * rows,
    )


def output_kernel(pack_ref, hop_ref, base_ref, mix1_ref, mix2_ref, out_ref):
    second = pack_ref[0, 0:384, :].astype(F32)
    for d in range(1, GROUP):
        second += pack_ref[d, 0:384, :].astype(F32)
    second = second.T.astype(BF16)
    mixed = base_ref[...] + dot_nn(hop_ref[...], mix1_ref[...]) + dot_nn(second, mix2_ref[...])
    out_ref[...] = mixed.astype(BF16)


def mix_output(*ins):
    outs = [array((128, 384), BF16)]
    return call(
        output_kernel, 1, ins, [whole(a.shape) for a in ins], outs, [whole((128, 384))],
        flops=4 * 128 * 384 * 384,
    )[0]


def local(dst_embed, src_embed, series, w_self, w_hop1, w_hop2, cotangent):
    dst_pack, src_pack, first_mixed, base, mix1, mix2 = prepare(
        dst_embed, src_embed, series, w_self, w_hop1, w_hop2, cotangent
    )
    own = exchange_src(src_pack).reshape(-1, 448)
    other = swap_cores(own)
    dst = exchange_dst(dst_pack).reshape(-1, 448)

    rows = dst.shape[0]
    stats = softmax_stats(own, dst, jnp.zeros((2, rows), F32), (2, rows))
    stats = exchange_dst(softmax_stats(other, dst, stats, (GROUP, 2, rows)))

    adjacency, first_part, norm, carried_own, carried_other = adjacency_and_hops(own, other, dst, stats)
    first_part = exchange_dst(first_part)
    pack, hop_first = join(first_part, carried_own, swap_cores(carried_other))
    first, hop_own = split(exchange_src(pack), first_mixed)
    hop_other = swap_cores(hop_own)
    first = exchange_dst(first).reshape(-1, 384)

    second_part = second_hop(adjacency, hop_own, hop_other)
    adj_grad, pack = adjacency_grad(own, other, hop_own, hop_other, dst, norm, first, second_part)
    pack = exchange_dst(pack)
    d_dst, d_src_own, d_src_other = embed_grads(own, other, adj_grad, dst, norm, pack)
    output = mix_output(pack, hop_first, base, mix1, mix2)
    d_dst = jnp.sum(exchange_dst(d_dst), axis=0).T
    d_src = jnp.sum(exchange_src(d_src_own + swap_cores(d_src_other)), axis=0)
    return output, d_dst, d_src


def solution(mesh):
    blocks = P(("row", "col"), None)
    return jax.shard_map(
        local,
        mesh=mesh,
        in_specs=(blocks, blocks, blocks, P(), P(), P(), blocks),
        out_specs=(blocks, blocks, blocks),
        check_vma=False,
    )
```

```python
import jax
import jax.numpy as jnp
from jax import lax
from jax.experimental import pallas as pl
from jax.experimental.pallas import tpu as pltpu
from jax.sharding import PartitionSpec as P

BF16 = jnp.bfloat16
F32 = jnp.float32
GROUP = 8
STEP = 256
BLOCKS = STEP // 128
VMEM_BYTES = 60 * 1024 * 1024

SAME_CORE = [[2 * chip + core for chip in range(8)] for core in range(2)]
OTHER_CORE = [(i, i ^ 1) for i in range(16)]


def dot_nn(a, b):
    return lax.dot_general(a, b, (((1,), (0,)), ((), ())), preferred_element_type=F32)


def dot_nt(a, b):
    return lax.dot_general(a, b, (((1,), (1,)), ((), ())), preferred_element_type=F32)


def dot_tn(a, b):
    return lax.dot_general(a, b, (((0,), (0,)), ((), ())), preferred_element_type=F32)


def exchange_dst(blocks):
    return lax.all_to_all(blocks, "row", 0, 0)


def exchange_src(blocks):
    return lax.all_to_all(blocks, "col", 0, 0, axis_index_groups=SAME_CORE)


def swap_cores(blocks):
    return lax.ppermute(blocks, "col", OTHER_CORE)


def whole(shape):
    return pl.BlockSpec(shape, lambda *_: (0,) * len(shape))


def call(kernel, steps, ins, in_specs, outs, out_specs, scratch=(), flops=0, exps=0):
    sizes = [a.size * a.dtype.itemsize for a in list(ins) + list(outs)]
    return pl.pallas_call(
        kernel,
        grid=(steps,),
        in_specs=in_specs,
        out_specs=out_specs,
        out_shape=outs,
        scratch_shapes=scratch,
        compiler_params=pltpu.CompilerParams(vmem_limit_bytes=VMEM_BYTES),
        cost_estimate=pl.CostEstimate(flops=flops, bytes_accessed=sum(sizes), transcendentals=exps),
    )(*ins)


def array(shape, dtype):
    return jax.ShapeDtypeStruct(shape, dtype)


HALF = GROUP * 128 // STEP


def first_half(*block):
    return pl.BlockSpec(block, lambda i: (jnp.minimum(i, HALF - 1),) + (0,) * (len(block) - 1))


def second_half(*block):
    return pl.BlockSpec(block, lambda i: (jnp.maximum(i - HALF, 0),) + (0,) * (len(block) - 1))


def by_step(*block):
    return pl.BlockSpec(block, lambda i: (i,) + (0,) * (len(block) - 1))


def pick(own_ref, other_ref):
    return jnp.where(pl.program_id(0) < HALF, own_ref[...], other_ref[...])


def put(own_ref, other_ref, value):
    value = value.astype(own_ref.dtype).reshape(own_ref.shape)

    @pl.when(pl.program_id(0) < HALF)
    def _():
        own_ref[...] = value

    @pl.when(pl.program_id(0) >= HALF)
    def _():
        other_ref[...] = value


def at_step(step):
    return pl.when(pl.program_id(0) == step)


def accumulate(total, part):
    @at_step(0)
    def _():
        total[...] = part

    @pl.when(pl.program_id(0) > 0)
    def _():
        total[...] += part


def mixing(weight):
    size, chan = 384, weight.shape[0]
    place = lax.broadcasted_iota(jnp.int32, (size, chan), 0) % chan
    repeat = jnp.where(place == lax.broadcasted_iota(jnp.int32, (size, chan), 1), 1.0, 0.0).astype(BF16)
    tiled = dot_nt(dot_nn(repeat, weight).astype(BF16), repeat)
    rows = lax.broadcasted_iota(jnp.int32, (size, size), 0) // chan
    cols = lax.broadcasted_iota(jnp.int32, (size, size), 1) // chan
    return jnp.where(rows == cols, tiled, 0.0).astype(BF16)


def pack_block(out, features, embed_t):
    for block in range(GROUP):
        out[block, 0:128, :] = features
        out[block, 128:160, 0:128] = embed_t[0:32]
        out[block, 128:160, 128:256] = embed_t[32:64]
        out[block, 128:160, 256:384] = jnp.zeros((32, 128), BF16)


def rows_of(packed):
    return jnp.concatenate([packed[b, 0:128, :] for b in range(packed.shape[0])], axis=0)


def embeds_of(packed):
    pieces = [
        jnp.concatenate([packed[b, 128:160, 0:128], packed[b, 128:160, 128:256]], axis=0)
        for b in range(packed.shape[0])
    ]
    return jnp.concatenate(pieces, axis=1)


def prepare_kernel(
    dst_ref, src_ref, series_ref, self_ref, hop1_ref, hop2_ref, cotangent_ref,
    dst_out, src_out, first_out, base_out, mix1_out, mix2_out,
):
    mix1, mix2 = mixing(hop1_ref[...]), mixing(hop2_ref[...])
    cotangent = cotangent_ref[...]
    second = dot_nt(cotangent, mix2).astype(BF16)
    pack_block(dst_out, second, dst_ref[...])
    pack_block(src_out, series_ref[...], src_ref[...])
    first_out[...] = dot_nt(cotangent, mix1)
    base_out[...] = dot_nn(series_ref[...], mixing(self_ref[...]))
    mix1_out[...] = mix1
    mix2_out[...] = mix2


def prepare(*ins):
    outs = [
        array((GROUP, 160, 384), BF16),
        array((GROUP, 160, 384), BF16),
        array((128, 384), F32),
        array((128, 384), F32),
        array((384, 384), BF16),
        array((384, 384), BF16),
    ]
    specs = [whole(a.shape) for a in ins], [whole(a.shape) for a in outs]
    return call(prepare_kernel, 1, ins, specs[0], outs, specs[1], flops=3 * 2 * 128 * 384 * 384)


def stats_kernel(packed_ref, dst_ref, before_ref, out_ref, state, dst):
    @at_step(0)
    def _():
        state[...] = before_ref[...]
        dst[...] = embeds_of(dst_ref)

    lifted = jnp.maximum(dot_tn(embeds_of(packed_ref), dst[...]), 0.0)
    old = state[0:1, :]
    new = jnp.maximum(old, jnp.max(lifted, axis=0, keepdims=True))
    total = jnp.sum(jnp.exp(lifted - new), axis=0, keepdims=True)
    state[1:2, :] = state[1:2, :] * jnp.exp(old - new) + total
    state[0:1, :] = new

    @at_step(pl.num_programs(0) - 1)
    def _():
        out_ref[...] = jnp.broadcast_to(state[...].reshape(out_ref.shape[-2:]), out_ref.shape)


def softmax_stats(packed, dst, before, out_shape):
    rows, src = dst.shape[0] * 128, packed.shape[0] * 128
    return call(
        stats_kernel,
        src // STEP,
        (packed, dst, before),
        [by_step(BLOCKS, 160, 384), whole(dst.shape), whole(before.shape)],
        [array(out_shape, F32)],
        [whole(out_shape)],
        [pltpu.VMEM((2, rows), F32), pltpu.VMEM((64, rows), BF16)],
        2 * src * rows * 64,
        src * rows,
    )[0]


def weights_of(packed, dst_ref, norm_ref):
    scores = dot_tn(embeds_of(packed), dst_ref[...])
    weights = jnp.exp(jnp.maximum(scores, 0.0) - norm_ref[0:1, :]) * norm_ref[1:2, :]
    return scores, weights


def first_kernel(
    own_ref, other_ref, dst_ref, stats_ref, adj_ref, hop_ref, norm_ref, own_out, other_out, total, dst, second
):
    @at_step(0)
    def _():
        peak = stats_ref[0, 0:1, :]
        for d in range(1, GROUP):
            peak = jnp.maximum(peak, stats_ref[d, 0:1, :])
        row_sum = jnp.zeros_like(peak)
        for d in range(GROUP):
            row_sum += stats_ref[d, 1:2, :] * jnp.exp(stats_ref[d, 0:1, :] - peak)
        norm_ref[0:1, :] = peak
        norm_ref[1:2, :] = 1.0 / row_sum
        dst[...] = embeds_of(dst_ref)
        second[...] = rows_of(dst_ref)

    packed = pick(own_ref, other_ref)
    adjacency = weights_of(packed, dst, norm_ref)[1].astype(BF16)
    adj_ref[...] = adjacency
    accumulate(total, dot_tn(rows_of(packed), adjacency))
    put(own_out, other_out, dot_nn(adjacency, second[...]))

    @at_step(pl.num_programs(0) - 1)
    def _():
        for block in range(GROUP):
            hop_ref[block] = total[:, 128 * block : 128 * block + 128].astype(BF16)


def adjacency_and_hops(own, other, dst, stats):
    rows, src = dst.shape[0] * 128, 2 * own.shape[0] * 128
    outs = [
        array((src, rows), BF16),
        array((GROUP, 384, 128), BF16),
        array((2, rows), F32),
        array((GROUP, 128, 384), BF16),
        array((GROUP, 128, 384), BF16),
    ]
    return call(
        first_kernel,
        2 * HALF,
        (own, other, dst, stats),
        [first_half(BLOCKS, 160, 384), second_half(BLOCKS, 160, 384), whole(dst.shape), whole(stats.shape)],
        outs,
        [
            by_step(STEP, rows),
            whole(outs[1].shape),
            whole(outs[2].shape),
            first_half(BLOCKS, 128, 384),
            second_half(BLOCKS, 128, 384),
        ],
        [pltpu.VMEM((384, rows), F32), pltpu.VMEM((64, rows), BF16), pltpu.VMEM((rows, 384), BF16)],
        2 * src * rows * 832,
        src * rows,
    )


def join_kernel(hop_ref, own_ref, other_ref, pack_ref, hop_out):
    hop = hop_ref[0].astype(F32)
    for d in range(1, GROUP):
        hop += hop_ref[d].astype(F32)
    hop = hop.T.astype(BF16)
    hop_out[...] = hop
    for block in range(GROUP):
        carried = own_ref[block].astype(F32) + other_ref[block].astype(F32)
        pack_ref[block, :, 0:384] = carried.astype(BF16)
        pack_ref[block, :, 384:768] = hop


def join(*ins):
    outs = [array((GROUP, 128, 768), BF16), array((128, 384), BF16)]
    specs = [whole(a.shape) for a in ins], [whole(a.shape) for a in outs]
    return call(join_kernel, 1, ins, specs[0], outs, specs[1])


def split_kernel(pack_ref, first_ref, first_out, hop_out):
    first = first_ref[...]
    for d in range(GROUP):
        first += pack_ref[d, :, 0:384].astype(F32)
        hop_out[128 * d : 128 * d + 128, :] = pack_ref[d, :, 384:768]
    first = first.astype(BF16)
    for block in range(GROUP):
        first_out[block] = first


def split(*ins):
    outs = [array((GROUP, 128, 384), BF16), array((GROUP * 128, 384), BF16)]
    specs = [whole(a.shape) for a in ins], [whole(a.shape) for a in outs]
    return call(split_kernel, 1, ins, specs[0], outs, specs[1])


def second_kernel(adj_ref, own_ref, other_ref, out_ref, total):
    accumulate(total, dot_tn(pick(own_ref, other_ref), adj_ref[...]))

    @at_step(pl.num_programs(0) - 1)
    def _():
        for block in range(GROUP):
            out_ref[block] = total[:, 128 * block : 128 * block + 128].astype(BF16)


def second_hop(adjacency, own, other):
    src, rows = adjacency.shape
    return call(
        second_kernel,
        2 * HALF,
        (adjacency, own, other),
        [by_step(STEP, rows), first_half(STEP, 384), second_half(STEP, 384)],
        [array((GROUP, 384, 128), BF16)],
        [whole((GROUP, 384, 128))],
        [pltpu.VMEM((384, rows), F32)],
        2 * src * rows * 384,
    )[0]


def grad_kernel(
    own_ref, other_ref, hop_own_ref, hop_other_ref, dst_ref, norm_ref, first_ref, second_ref,
    adj_ref, pack_ref, inner, dst, grads,
):
    @at_step(0)
    def _():
        dst[...] = embeds_of(dst_ref)
        grads[:, 0:384] = rows_of(dst_ref)
        grads[:, 384:768] = first_ref[...]

    packed, hop = pick(own_ref, other_ref), pick(hop_own_ref, hop_other_ref)
    weights = weights_of(packed, dst, norm_ref)[1]
    adj_grad = dot_nt(jnp.concatenate([hop, rows_of(packed)], axis=1), grads[...])
    adj_ref[...] = adj_grad
    accumulate(inner, jnp.sum(weights * adj_grad, axis=0, keepdims=True))

    @at_step(pl.num_programs(0) - 1)
    def _():
        high = inner[...].astype(BF16).astype(F32)
        rest = inner[...] - high
        middle = rest.astype(BF16).astype(F32)
        rows = [
            term[:, 128 * block : 128 * block + 128]
            for term in (high, middle, rest - middle)
            for block in range(GROUP)
        ]
        terms = jnp.concatenate(rows + [jnp.zeros((8, 128), F32)], axis=0).astype(BF16)
        for block in range(GROUP):
            pack_ref[block, 0:384, :] = second_ref[block]
            pack_ref[block, 384:416, :] = terms


def adjacency_grad(own, other, hop_own, hop_other, dst, norm, first, second):
    rows, src = dst.shape[0] * 128, 2 * own.shape[0] * 128
    outs = [array((src, rows), F32), array((GROUP, 416, 128), BF16)]
    return call(
        grad_kernel,
        2 * HALF,
        (own, other, hop_own, hop_other, dst, norm, first, second),
        [
            first_half(BLOCKS, 160, 384),
            second_half(BLOCKS, 160, 384),
            first_half(STEP, 384),
            second_half(STEP, 384),
            whole(dst.shape),
            whole(norm.shape),
            whole(first.shape),
            whole(second.shape),
        ],
        outs,
        [by_step(STEP, rows), whole(outs[1].shape)],
        [pltpu.VMEM((1, rows), F32), pltpu.VMEM((64, rows), BF16), pltpu.VMEM((rows, 768), BF16)],
        2 * src * rows * 832,
        src * rows,
    )


def embed_kernel(
    own_ref, other_ref, adj_ref, dst_ref, norm_ref, pack_ref, ddst_ref, own_out, other_out, inner, total, dst
):
    @at_step(0)
    def _():
        terms = pack_ref[0, 384:416, :].astype(F32)
        for d in range(1, GROUP):
            terms += pack_ref[d, 384:416, :].astype(F32)
        rows = terms[0:8] + (terms[8:16] + terms[16:24])
        for block in range(GROUP):
            inner[0:1, 128 * block : 128 * block + 128] = rows[block : block + 1, :]
        dst[...] = embeds_of(dst_ref)

    packed = pick(own_ref, other_ref)
    scores, weights = weights_of(packed, dst, norm_ref)
    graded = jnp.where(scores > 0.0, weights * (adj_ref[...] - inner[...]), 0.0).astype(BF16)
    accumulate(total, dot_nn(embeds_of(packed), graded))
    d_src = dot_nt(dst[...], graded)
    d_src = jnp.stack([d_src[:, 128 * b : 128 * b + 128] for b in range(BLOCKS)])
    put(own_out, other_out, d_src)

    @at_step(pl.num_programs(0) - 1)
    def _():
        for block in range(GROUP):
            ddst_ref[block] = total[:, 128 * block : 128 * block + 128]


def embed_grads(own, other, adj_grad, dst, norm, pack):
    src, rows = adj_grad.shape
    outs = [array((GROUP, 64, 128), F32)] * 3
    return call(
        embed_kernel,
        2 * HALF,
        (own, other, adj_grad, dst, norm, pack),
        [
            first_half(BLOCKS, 160, 384),
            second_half(BLOCKS, 160, 384),
            by_step(STEP, rows),
            whole(dst.shape),
            whole(norm.shape),
            whole(pack.shape),
        ],
        outs,
        [
            whole(outs[0].shape),
            first_half(BLOCKS, 64, 128),
            second_half(BLOCKS, 64, 128),
        ],
        [pltpu.VMEM((1, rows), F32), pltpu.VMEM((64, rows), F32), pltpu.VMEM((64, rows), BF16)],
        6 * src * rows * 64,
        src * rows,
    )


def output_kernel(pack_ref, hop_ref, base_ref, mix1_ref, mix2_ref, out_ref):
    second = pack_ref[0, 0:384, :].astype(F32)
    for d in range(1, GROUP):
        second += pack_ref[d, 0:384, :].astype(F32)
    second = second.T.astype(BF16)
    mixed = base_ref[...] + dot_nn(hop_ref[...], mix1_ref[...]) + dot_nn(second, mix2_ref[...])
    out_ref[...] = mixed.astype(BF16)


def mix_output(*ins):
    outs = [array((128, 384), BF16)]
    return call(
        output_kernel, 1, ins, [whole(a.shape) for a in ins], outs, [whole((128, 384))],
        flops=4 * 128 * 384 * 384,
    )[0]


def local(dst_embed, src_embed, series, w_self, w_hop1, w_hop2, cotangent):
    dst_pack, src_pack, first_mixed, base, mix1, mix2 = prepare(
        dst_embed.T, src_embed.T, series, w_self, w_hop1, w_hop2, cotangent
    )
    own = exchange_src(src_pack)
    other = swap_cores(own)
    dst = exchange_dst(dst_pack)

    rows = dst.shape[0] * 128
    stats = softmax_stats(own, dst, jnp.zeros((2, rows), F32), (2, rows))
    stats = exchange_dst(softmax_stats(other, dst, stats, (GROUP, 2, rows)))

    adjacency, first_part, norm, carried_own, carried_other = adjacency_and_hops(own, other, dst, stats)
    first_part = exchange_dst(first_part)
    pack, hop_first = join(first_part, carried_own, swap_cores(carried_other))
    first, hop_own = split(exchange_src(pack), first_mixed)
    hop_other = swap_cores(hop_own)
    first = exchange_dst(first).reshape(-1, 384)

    second_part = second_hop(adjacency, hop_own, hop_other)
    adj_grad, pack = adjacency_grad(own, other, hop_own, hop_other, dst, norm, first, second_part)
    pack = exchange_dst(pack)
    d_dst, d_src_own, d_src_other = embed_grads(own, other, adj_grad, dst, norm, pack)
    output = mix_output(pack, hop_first, base, mix1, mix2)
    d_dst = jnp.sum(exchange_dst(d_dst), axis=0).T
    d_src = jnp.sum(exchange_src(d_src_own + swap_cores(d_src_other)), axis=0).T
    return output, d_dst, d_src


def solution(mesh):
    blocks = P(("row", "col"), None)
    return jax.shard_map(
        local,
        mesh=mesh,
        in_specs=(blocks, blocks, blocks, P(), P(), P(), blocks),
        out_specs=(blocks, blocks, blocks),
        check_vma=False,
    )
```

```python
import jax
import jax.numpy as jnp
from jax import lax
from jax.experimental import pallas as pl
from jax.experimental.pallas import tpu as pltpu
from jax.sharding import PartitionSpec as P

BF16 = jnp.bfloat16
F32 = jnp.float32
GROUP = 8
STEP = 1024
BLOCKS = STEP // 128
VMEM_BYTES = 28 * 1024 * 1024

SAME_CORE = [[2 * chip + core for chip in range(8)] for core in range(2)]
OTHER_CORE = [(i, i ^ 1) for i in range(16)]


def dot_nn(a, b):
    return lax.dot_general(a, b, (((1,), (0,)), ((), ())), preferred_element_type=F32)


def dot_nt(a, b):
    return lax.dot_general(a, b, (((1,), (1,)), ((), ())), preferred_element_type=F32)


def dot_tn(a, b):
    return lax.dot_general(a, b, (((0,), (0,)), ((), ())), preferred_element_type=F32)


def exchange_dst(blocks):
    return lax.all_to_all(blocks, "row", 0, 0)


def exchange_src(blocks):
    return lax.all_to_all(blocks, "col", 0, 0, axis_index_groups=SAME_CORE)


def swap_cores(blocks):
    return lax.ppermute(blocks, "col", OTHER_CORE)


def whole(shape):
    return pl.BlockSpec(shape, lambda *_: (0,) * len(shape))


def call(kernel, steps, ins, in_specs, outs, out_specs, scratch=(), flops=0, exps=0):
    sizes = [a.size * a.dtype.itemsize for a in list(ins) + list(outs)]
    return pl.pallas_call(
        kernel,
        grid=(steps,),
        in_specs=in_specs,
        out_specs=out_specs,
        out_shape=outs,
        scratch_shapes=scratch,
        compiler_params=pltpu.CompilerParams(vmem_limit_bytes=VMEM_BYTES),
        cost_estimate=pl.CostEstimate(flops=flops, bytes_accessed=sum(sizes), transcendentals=exps),
    )(*ins)


def array(shape, dtype):
    return jax.ShapeDtypeStruct(shape, dtype)


HALF = GROUP * 128 // STEP


def first_half(*block):
    return pl.BlockSpec(block, lambda i: (jnp.minimum(i, HALF - 1),) + (0,) * (len(block) - 1))


def second_half(*block):
    return pl.BlockSpec(block, lambda i: (jnp.maximum(i - HALF, 0),) + (0,) * (len(block) - 1))


def by_step(*block):
    return pl.BlockSpec(block, lambda i: (i,) + (0,) * (len(block) - 1))


def pick(own_ref, other_ref):
    return jnp.where(pl.program_id(0) < HALF, own_ref[...], other_ref[...])


def put(own_ref, other_ref, value):
    value = value.astype(own_ref.dtype).reshape(own_ref.shape)

    @pl.when(pl.program_id(0) < HALF)
    def _():
        own_ref[...] = value

    @pl.when(pl.program_id(0) >= HALF)
    def _():
        other_ref[...] = value


def at_step(step):
    return pl.when(pl.program_id(0) == step)


def accumulate(total, part):
    @at_step(0)
    def _():
        total[...] = part

    @pl.when(pl.program_id(0) > 0)
    def _():
        total[...] += part


def mixing(weight):
    size, chan = 384, weight.shape[0]
    place = lax.broadcasted_iota(jnp.int32, (size, chan), 0) % chan
    repeat = jnp.where(place == lax.broadcasted_iota(jnp.int32, (size, chan), 1), 1.0, 0.0).astype(BF16)
    tiled = dot_nt(dot_nn(repeat, weight).astype(BF16), repeat)
    rows = lax.broadcasted_iota(jnp.int32, (size, size), 0) // chan
    cols = lax.broadcasted_iota(jnp.int32, (size, size), 1) // chan
    return jnp.where(rows == cols, tiled, 0.0).astype(BF16)


def pack_block(out, features, embed_t):
    for block in range(GROUP):
        out[block, 0:128, :] = features
        out[block, 128:160, 0:128] = embed_t[0:32]
        out[block, 128:160, 128:256] = embed_t[32:64]
        out[block, 128:160, 256:384] = jnp.zeros((32, 128), BF16)


def rows_of(packed):
    return jnp.concatenate([packed[b, 0:128, :] for b in range(packed.shape[0])], axis=0)


def embeds_of(packed):
    pieces = [
        jnp.concatenate([packed[b, 128:160, 0:128], packed[b, 128:160, 128:256]], axis=0)
        for b in range(packed.shape[0])
    ]
    return jnp.concatenate(pieces, axis=1)


def prepare_kernel(
    dst_ref, src_ref, series_ref, self_ref, hop1_ref, hop2_ref, cotangent_ref,
    dst_out, src_out, first_out, base_out, mix1_out, mix2_out,
):
    mix1, mix2 = mixing(hop1_ref[...]), mixing(hop2_ref[...])
    cotangent = cotangent_ref[...]
    second = dot_nt(cotangent, mix2).astype(BF16)
    pack_block(dst_out, second, dst_ref[...])
    pack_block(src_out, series_ref[...], src_ref[...])
    first_out[...] = dot_nt(cotangent, mix1)
    base_out[...] = dot_nn(series_ref[...], mixing(self_ref[...]))
    mix1_out[...] = mix1
    mix2_out[...] = mix2


def prepare(*ins):
    outs = [
        array((GROUP, 160, 384), BF16),
        array((GROUP, 160, 384), BF16),
        array((128, 384), F32),
        array((128, 384), F32),
        array((384, 384), BF16),
        array((384, 384), BF16),
    ]
    specs = [whole(a.shape) for a in ins], [whole(a.shape) for a in outs]
    return call(prepare_kernel, 1, ins, specs[0], outs, specs[1], flops=3 * 2 * 128 * 384 * 384)


def stats_kernel(packed_ref, dst_ref, before_ref, out_ref, state, dst):
    @at_step(0)
    def _():
        state[...] = before_ref[...]
        dst[...] = embeds_of(dst_ref)

    lifted = jnp.maximum(dot_tn(embeds_of(packed_ref), dst[...]), 0.0)
    old = state[0:1, :]
    new = jnp.maximum(old, jnp.max(lifted, axis=0, keepdims=True))
    total = jnp.sum(jnp.exp(lifted - new), axis=0, keepdims=True)
    state[1:2, :] = state[1:2, :] * jnp.exp(old - new) + total
    state[0:1, :] = new

    @at_step(pl.num_programs(0) - 1)
    def _():
        out_ref[...] = jnp.broadcast_to(state[...].reshape(out_ref.shape[-2:]), out_ref.shape)


def softmax_stats(packed, dst, before, out_shape):
    rows, src = dst.shape[0] * 128, packed.shape[0] * 128
    return call(
        stats_kernel,
        src // STEP,
        (packed, dst, before),
        [by_step(BLOCKS, 160, 384), whole(dst.shape), whole(before.shape)],
        [array(out_shape, F32)],
        [whole(out_shape)],
        [pltpu.VMEM((2, rows), F32), pltpu.VMEM((64, rows), BF16)],
        2 * src * rows * 64,
        src * rows,
    )[0]


def weights_of(packed, dst_ref, norm_ref):
    scores = dot_tn(embeds_of(packed), dst_ref[...])
    weights = jnp.exp(jnp.maximum(scores, 0.0) - norm_ref[0:1, :]) * norm_ref[1:2, :]
    return scores, weights


def first_kernel(
    own_ref, other_ref, dst_ref, stats_ref, adj_ref, hop_ref, norm_ref, own_out, other_out, total, dst, second
):
    @at_step(0)
    def _():
        peak = stats_ref[0, 0:1, :]
        for d in range(1, GROUP):
            peak = jnp.maximum(peak, stats_ref[d, 0:1, :])
        row_sum = jnp.zeros_like(peak)
        for d in range(GROUP):
            row_sum += stats_ref[d, 1:2, :] * jnp.exp(stats_ref[d, 0:1, :] - peak)
        norm_ref[0:1, :] = peak
        norm_ref[1:2, :] = 1.0 / row_sum
        dst[...] = embeds_of(dst_ref)
        second[...] = rows_of(dst_ref)

    packed = pick(own_ref, other_ref)
    adjacency = weights_of(packed, dst, norm_ref)[1].astype(BF16)
    adj_ref[...] = adjacency
    accumulate(total, dot_tn(rows_of(packed), adjacency))
    put(own_out, other_out, dot_nn(adjacency, second[...]))

    @at_step(pl.num_programs(0) - 1)
    def _():
        for block in range(GROUP):
            hop_ref[block] = total[:, 128 * block : 128 * block + 128].astype(BF16)


def adjacency_and_hops(own, other, dst, stats):
    rows, src = dst.shape[0] * 128, 2 * own.shape[0] * 128
    outs = [
        array((src, rows), BF16),
        array((GROUP, 384, 128), BF16),
        array((2, rows), F32),
        array((GROUP, 128, 384), BF16),
        array((GROUP, 128, 384), BF16),
    ]
    return call(
        first_kernel,
        2 * HALF,
        (own, other, dst, stats),
        [first_half(BLOCKS, 160, 384), second_half(BLOCKS, 160, 384), whole(dst.shape), whole(stats.shape)],
        outs,
        [
            by_step(STEP, rows),
            whole(outs[1].shape),
            whole(outs[2].shape),
            first_half(BLOCKS, 128, 384),
            second_half(BLOCKS, 128, 384),
        ],
        [pltpu.VMEM((384, rows), F32), pltpu.VMEM((64, rows), BF16), pltpu.VMEM((rows, 384), BF16)],
        2 * src * rows * 832,
        src * rows,
    )


def join_kernel(hop_ref, own_ref, other_ref, pack_ref, hop_out):
    hop = hop_ref[0].astype(F32)
    for d in range(1, GROUP):
        hop += hop_ref[d].astype(F32)
    hop = hop.T.astype(BF16)
    hop_out[...] = hop
    for block in range(GROUP):
        carried = own_ref[block].astype(F32) + other_ref[block].astype(F32)
        pack_ref[block, :, 0:384] = carried.astype(BF16)
        pack_ref[block, :, 384:768] = hop


def join(*ins):
    outs = [array((GROUP, 128, 768), BF16), array((128, 384), BF16)]
    specs = [whole(a.shape) for a in ins], [whole(a.shape) for a in outs]
    return call(join_kernel, 1, ins, specs[0], outs, specs[1])


def split_kernel(pack_ref, first_ref, first_out, hop_out):
    first = first_ref[...]
    for d in range(GROUP):
        first += pack_ref[d, :, 0:384].astype(F32)
        hop_out[128 * d : 128 * d + 128, :] = pack_ref[d, :, 384:768]
    first = first.astype(BF16)
    for block in range(GROUP):
        first_out[block] = first


def split(*ins):
    outs = [array((GROUP, 128, 384), BF16), array((GROUP * 128, 384), BF16)]
    specs = [whole(a.shape) for a in ins], [whole(a.shape) for a in outs]
    return call(split_kernel, 1, ins, specs[0], outs, specs[1])


def second_kernel(adj_ref, own_ref, other_ref, out_ref, total):
    accumulate(total, dot_tn(pick(own_ref, other_ref), adj_ref[...]))

    @at_step(pl.num_programs(0) - 1)
    def _():
        for block in range(GROUP):
            out_ref[block] = total[:, 128 * block : 128 * block + 128].astype(BF16)


def second_hop(adjacency, own, other):
    src, rows = adjacency.shape
    return call(
        second_kernel,
        2 * HALF,
        (adjacency, own, other),
        [by_step(STEP, rows), first_half(STEP, 384), second_half(STEP, 384)],
        [array((GROUP, 384, 128), BF16)],
        [whole((GROUP, 384, 128))],
        [pltpu.VMEM((384, rows), F32)],
        2 * src * rows * 384,
    )[0]


def grad_kernel(
    own_ref, other_ref, hop_own_ref, hop_other_ref, dst_ref, norm_ref, first_ref, second_ref,
    adj_ref, pack_ref, inner, dst, grads,
):
    @at_step(0)
    def _():
        dst[...] = embeds_of(dst_ref)
        grads[:, 0:384] = rows_of(dst_ref)
        grads[:, 384:768] = first_ref[...]

    packed, hop = pick(own_ref, other_ref), pick(hop_own_ref, hop_other_ref)
    weights = weights_of(packed, dst, norm_ref)[1]
    adj_grad = dot_nt(jnp.concatenate([hop, rows_of(packed)], axis=1), grads[...])
    adj_ref[...] = adj_grad
    accumulate(inner, jnp.sum(weights * adj_grad, axis=0, keepdims=True))

    @at_step(pl.num_programs(0) - 1)
    def _():
        high = inner[...].astype(BF16).astype(F32)
        rest = inner[...] - high
        middle = rest.astype(BF16).astype(F32)
        rows = [
            term[:, 128 * block : 128 * block + 128]
            for term in (high, middle, rest - middle)
            for block in range(GROUP)
        ]
        terms = jnp.concatenate(rows + [jnp.zeros((8, 128), F32)], axis=0).astype(BF16)
        for block in range(GROUP):
            pack_ref[block, 0:384, :] = second_ref[block]
            pack_ref[block, 384:416, :] = terms


def adjacency_grad(own, other, hop_own, hop_other, dst, norm, first, second):
    rows, src = dst.shape[0] * 128, 2 * own.shape[0] * 128
    outs = [array((src, rows), F32), array((GROUP, 416, 128), BF16)]
    return call(
        grad_kernel,
        2 * HALF,
        (own, other, hop_own, hop_other, dst, norm, first, second),
        [
            first_half(BLOCKS, 160, 384),
            second_half(BLOCKS, 160, 384),
            first_half(STEP, 384),
            second_half(STEP, 384),
            whole(dst.shape),
            whole(norm.shape),
            whole(first.shape),
            whole(second.shape),
        ],
        outs,
        [by_step(STEP, rows), whole(outs[1].shape)],
        [pltpu.VMEM((1, rows), F32), pltpu.VMEM((64, rows), BF16), pltpu.VMEM((rows, 768), BF16)],
        2 * src * rows * 832,
        src * rows,
    )


def embed_kernel(
    own_ref, other_ref, adj_ref, dst_ref, norm_ref, pack_ref, ddst_ref, own_out, other_out, inner, total, dst
):
    @at_step(0)
    def _():
        terms = pack_ref[0, 384:416, :].astype(F32)
        for d in range(1, GROUP):
            terms += pack_ref[d, 384:416, :].astype(F32)
        rows = terms[0:8] + (terms[8:16] + terms[16:24])
        for block in range(GROUP):
            inner[0:1, 128 * block : 128 * block + 128] = rows[block : block + 1, :]
        dst[...] = embeds_of(dst_ref)

    packed = pick(own_ref, other_ref)
    scores, weights = weights_of(packed, dst, norm_ref)
    graded = jnp.where(scores > 0.0, weights * (adj_ref[...] - inner[...]), 0.0).astype(BF16)
    accumulate(total, dot_nn(embeds_of(packed), graded))
    d_src = dot_nt(dst[...], graded)
    d_src = jnp.stack([d_src[:, 128 * b : 128 * b + 128] for b in range(BLOCKS)])
    put(own_out, other_out, d_src)

    @at_step(pl.num_programs(0) - 1)
    def _():
        for block in range(GROUP):
            ddst_ref[block] = total[:, 128 * block : 128 * block + 128]


def embed_grads(own, other, adj_grad, dst, norm, pack):
    src, rows = adj_grad.shape
    outs = [array((GROUP, 64, 128), F32)] * 3
    return call(
        embed_kernel,
        2 * HALF,
        (own, other, adj_grad, dst, norm, pack),
        [
            first_half(BLOCKS, 160, 384),
            second_half(BLOCKS, 160, 384),
            by_step(STEP, rows),
            whole(dst.shape),
            whole(norm.shape),
            whole(pack.shape),
        ],
        outs,
        [
            whole(outs[0].shape),
            first_half(BLOCKS, 64, 128),
            second_half(BLOCKS, 64, 128),
        ],
        [pltpu.VMEM((1, rows), F32), pltpu.VMEM((64, rows), F32), pltpu.VMEM((64, rows), BF16)],
        6 * src * rows * 64,
        src * rows,
    )


def output_kernel(pack_ref, hop_ref, base_ref, mix1_ref, mix2_ref, out_ref):
    second = pack_ref[0, 0:384, :].astype(F32)
    for d in range(1, GROUP):
        second += pack_ref[d, 0:384, :].astype(F32)
    second = second.T.astype(BF16)
    mixed = base_ref[...] + dot_nn(hop_ref[...], mix1_ref[...]) + dot_nn(second, mix2_ref[...])
    out_ref[...] = mixed.astype(BF16)


def mix_output(*ins):
    outs = [array((128, 384), BF16)]
    return call(
        output_kernel, 1, ins, [whole(a.shape) for a in ins], outs, [whole((128, 384))],
        flops=4 * 128 * 384 * 384,
    )[0]


def local(dst_embed, src_embed, series, w_self, w_hop1, w_hop2, cotangent):
    dst_pack, src_pack, first_mixed, base, mix1, mix2 = prepare(
        dst_embed.T, src_embed.T, series, w_self, w_hop1, w_hop2, cotangent
    )
    own = exchange_src(src_pack)
    other = swap_cores(own)
    dst = exchange_dst(dst_pack)

    rows = dst.shape[0] * 128
    stats = softmax_stats(own, dst, jnp.zeros((2, rows), F32), (2, rows))
    stats = exchange_dst(softmax_stats(other, dst, stats, (GROUP, 2, rows)))

    adjacency, first_part, norm, carried_own, carried_other = adjacency_and_hops(own, other, dst, stats)
    first_part = exchange_dst(first_part)
    pack, hop_first = join(first_part, carried_own, swap_cores(carried_other))
    first, hop_own = split(exchange_src(pack), first_mixed)
    hop_other = swap_cores(hop_own)
    first = exchange_dst(first).reshape(-1, 384)

    second_part = second_hop(adjacency, hop_own, hop_other)
    adj_grad, pack = adjacency_grad(own, other, hop_own, hop_other, dst, norm, first, second_part)
    pack = exchange_dst(pack)
    d_dst, d_src_own, d_src_other = embed_grads(own, other, adj_grad, dst, norm, pack)
    output = mix_output(pack, hop_first, base, mix1, mix2)
    d_dst = jnp.sum(exchange_dst(d_dst), axis=0).T
    d_src = jnp.sum(exchange_src(d_src_own + swap_cores(d_src_other)), axis=0).T
    return output, d_dst, d_src


def solution(mesh):
    blocks = P(("row", "col"), None)
    return jax.shard_map(
        local,
        mesh=mesh,
        in_specs=(blocks, blocks, blocks, P(), P(), P(), blocks),
        out_specs=(blocks, blocks, blocks),
        check_vma=False,
    )
```

```python
import jax
import jax.numpy as jnp
from jax import lax
from jax.experimental import pallas as pl
from jax.experimental.pallas import tpu as pltpu
from jax.sharding import PartitionSpec as P

BF16 = jnp.bfloat16
F32 = jnp.float32
GROUP = 8
MIB = 1024 * 1024
VMEM_BYTES = 28 * MIB

SAME_CORE = [[2 * chip + core for chip in range(8)] for core in range(2)]
OTHER_CORE = [(i, i ^ 1) for i in range(16)]


def dot_nn(a, b):
    return lax.dot_general(a, b, (((1,), (0,)), ((), ())), preferred_element_type=F32)


def dot_nt(a, b):
    return lax.dot_general(a, b, (((1,), (1,)), ((), ())), preferred_element_type=F32)


def dot_tn(a, b):
    return lax.dot_general(a, b, (((0,), (0,)), ((), ())), preferred_element_type=F32)


def exchange_dst(blocks):
    return lax.all_to_all(blocks, "row", 0, 0)


def exchange_src(blocks):
    return lax.all_to_all(blocks, "col", 0, 0, axis_index_groups=SAME_CORE)


def swap_cores(blocks):
    return lax.ppermute(blocks, "col", OTHER_CORE)


def array(*shape, dtype=BF16):
    return jax.ShapeDtypeStruct(shape, dtype)


def whole(a):
    return pl.BlockSpec(a.shape, lambda *_: (0,) * len(a.shape))


def by_step(a):
    return pl.BlockSpec((a.shape[0] // 2,) + a.shape[1:], lambda i, *_: (i,) + (0,) * (len(a.shape) - 1))


def by_core(a):
    return pl.BlockSpec((GROUP, 1) + a.shape[2:], lambda i, core: (0, (core[0] + i) % 2) + (0,) * (len(a.shape) - 2))


def call(kernel, steps, ins, outs, scratch=(), flops=0, exps=0, core=None, kinds=None, vmem=VMEM_BYTES):
    kinds = kinds or {}
    sizes = [a.size * a.dtype.itemsize for a in list(ins) + list(outs)]
    specs = [kinds.get(i, whole)(a) for i, a in enumerate(list(ins) + list(outs))]
    return pl.pallas_call(
        kernel,
        grid_spec=pltpu.PrefetchScalarGridSpec(
            num_scalar_prefetch=0 if core is None else 1,
            grid=(steps,),
            in_specs=specs[: len(ins)],
            out_specs=specs[len(ins) :],
            scratch_shapes=scratch,
        ),
        out_shape=outs,
        compiler_params=pltpu.CompilerParams(vmem_limit_bytes=vmem),
        cost_estimate=pl.CostEstimate(flops=flops, bytes_accessed=sum(sizes), transcendentals=exps),
    )(*(() if core is None else (core,)), *ins)


def at_step(step):
    return pl.when(pl.program_id(0) == step)


def pick(own_ref, other_ref):
    return jnp.where(pl.program_id(0) == 0, own_ref[...], other_ref[...])


def put(own_ref, other_ref, block, value):
    @at_step(0)
    def _():
        own_ref[block] = value

    @at_step(1)
    def _():
        other_ref[block] = value


def accumulate(total, part):
    @at_step(0)
    def _():
        total[...] = part

    @at_step(1)
    def _():
        total[...] += part


def side_by_side(blocks):
    return jnp.concatenate([blocks[b] for b in range(GROUP)], axis=1)


def nodes(block):
    return slice(128 * block, 128 * block + 128)


def mixing(weight):
    size, chan = 384, weight.shape[0]
    place = lax.broadcasted_iota(jnp.int32, (size, chan), 0) % chan
    repeat = jnp.where(place == lax.broadcasted_iota(jnp.int32, (size, chan), 1), 1.0, 0.0).astype(BF16)
    tiled = dot_nt(dot_nn(repeat, weight).astype(BF16), repeat)
    rows = lax.broadcasted_iota(jnp.int32, (size, size), 0) // chan
    cols = lax.broadcasted_iota(jnp.int32, (size, size), 1) // chan
    return jnp.where(rows == cols, tiled, 0.0).astype(BF16)


def prepare_kernel(
    dst_ref, src_ref, series_ref, self_ref, hop1_ref, hop2_ref, cotangent_ref,
    src_out, dst_out, first_out, base_out, mix1_out, mix2_out,
):
    mix1, mix2 = mixing(hop1_ref[...]), mixing(hop2_ref[...])
    cotangent = cotangent_ref[...]
    second = dot_nt(mix2, cotangent).astype(BF16)
    for block in range(GROUP):
        src_out[block] = src_ref[...]
        dst_out[block, 0:384, :] = second
        dst_out[block, 384:448, :] = dst_ref[...]
    first_out[...] = dot_nt(mix1, cotangent)
    base_out[...] = dot_nn(series_ref[...], mixing(self_ref[...]))
    mix1_out[...] = mix1
    mix2_out[...] = mix2


def prepare(*ins):
    outs = [
        array(GROUP, 64, 128),
        array(GROUP, 448, 128),
        array(384, 128, dtype=F32),
        array(128, 384, dtype=F32),
        array(384, 384),
        array(384, 384),
    ]
    return call(prepare_kernel, 1, ins, outs, flops=3 * 2 * 128 * 384 * 384, vmem=60 * MIB)


def stats_kernel(own_ref, other_ref, dst_ref, out_ref, state, dst):
    @at_step(0)
    def _():
        state[...] = jnp.zeros_like(state)
        dst[...] = side_by_side(dst_ref[:, 384:448, :])

    lifted = jnp.maximum(dot_tn(side_by_side(pick(own_ref, other_ref)), dst[...]), 0.0)
    old = state[0:1, :]
    new = jnp.maximum(old, jnp.max(lifted, axis=0, keepdims=True))
    total = jnp.sum(jnp.exp(lifted - new), axis=0, keepdims=True)
    state[1:2, :] = state[1:2, :] * jnp.exp(old - new) + total
    state[0:1, :] = new

    @at_step(1)
    def _():
        out_ref[...] = jnp.broadcast_to(state[...][None], out_ref.shape)


def softmax_stats(own, other, dst):
    rows = dst.shape[0] * 128
    scratch = [pltpu.VMEM((2, rows), F32), pltpu.VMEM((64, rows), BF16)]
    outs = [array(GROUP, 2, rows, dtype=F32)]
    size = 2 * rows * rows
    return call(stats_kernel, 2, (own, other, dst), outs, scratch, 128 * size, size)[0]


def weights_of(src, dst, norm_ref):
    scores = dot_tn(src, dst)
    weights = jnp.exp(jnp.maximum(scores, 0.0) - norm_ref[0:1, :]) * norm_ref[1:2, :]
    return scores, weights


def adjacency_kernel(
    own_ref, other_ref, dst_ref, stats_ref, adj_ref, norm_ref, own_out, other_out, dst, second
):
    @at_step(0)
    def _():
        peak = stats_ref[0, 0:1, :]
        for d in range(1, GROUP):
            peak = jnp.maximum(peak, stats_ref[d, 0:1, :])
        row_sum = jnp.zeros_like(peak)
        for d in range(GROUP):
            row_sum += stats_ref[d, 1:2, :] * jnp.exp(stats_ref[d, 0:1, :] - peak)
        norm_ref[0:1, :] = peak
        norm_ref[1:2, :] = 1.0 / row_sum
        second[...] = side_by_side(dst_ref[:, 0:384, :])
        dst[...] = side_by_side(dst_ref[:, 384:448, :])

    src = side_by_side(pick(own_ref, other_ref))
    adjacency = weights_of(src, dst[...], norm_ref)[1].astype(BF16)
    adj_ref[...] = adjacency
    carried = dot_nt(second[...], adjacency).astype(BF16)
    for block in range(GROUP):
        put(own_out, other_out, block, carried[:, nodes(block)])


def adjacency_and_carried(own, other, dst, stats):
    rows = dst.shape[0] * 128
    outs = [
        array(2 * rows, rows),
        array(2, rows, dtype=F32),
        array(GROUP, 384, 128),
        array(GROUP, 384, 128),
    ]
    scratch = [pltpu.VMEM((64, rows), BF16), pltpu.VMEM((384, rows), BF16)]
    size = 2 * rows * rows
    return call(
        adjacency_kernel, 2, (own, other, dst, stats), outs, scratch, 896 * size, size, kinds={4: by_step}
    )


def first_kernel(core_ref, adj_ref, series_ref, out_ref, total):
    del core_ref
    accumulate(total, dot_tn(series_ref[...].reshape(GROUP * 128, 384), adj_ref[...]))

    @at_step(1)
    def _():
        for block in range(GROUP):
            out_ref[block] = total[:, nodes(block)].astype(BF16)


def first_hop(core, adjacency, series):
    rows = adjacency.shape[1]
    return call(
        first_kernel, 2, (adjacency, series), [array(GROUP, 384, 128)], [pltpu.VMEM((384, rows), F32)],
        2 * adjacency.size * 384, core=core, kinds={0: by_step, 1: by_core},
    )[0]


def sum_of(pack_ref, start, stop):
    total = pack_ref[0, start:stop, :].astype(F32)
    for d in range(1, GROUP):
        total += pack_ref[d, start:stop, :].astype(F32)
    return total


def add_kernel(own_ref, other_ref, out_ref):
    out_ref[...] = (own_ref[...].astype(F32) + other_ref[...].astype(F32)).astype(BF16)


def first_grad_kernel(carried_ref, mixed_ref, hop_ref, out_ref):
    grad = (mixed_ref[...] + sum_of(carried_ref, 0, 384)).astype(BF16)
    for block in range(GROUP):
        out_ref[block, 0:384, :] = hop_ref[block]
        out_ref[block, 384:768, :] = grad


def join_kernel(pack_ref, hop_out, spread_out):
    hop = sum_of(pack_ref, 0, 384).T.astype(BF16)
    hop_out[...] = hop
    for block in range(GROUP):
        spread_out[nodes(block), :] = hop


def second_kernel(adj_ref, own_ref, other_ref, out_ref, total):
    accumulate(total, dot_tn(pick(own_ref, other_ref), adj_ref[...]))

    @at_step(1)
    def _():
        for block in range(GROUP):
            out_ref[block] = total[:, nodes(block)].astype(BF16)


def second_hop(adjacency, own, other):
    rows = adjacency.shape[1]
    return call(
        second_kernel, 2, (adjacency, own, other), [array(GROUP, 384, 128)], [pltpu.VMEM((384, rows), F32)],
        2 * adjacency.size * 384, kinds={0: by_step},
    )[0]


def grad_kernel(
    core_ref, own_ref, other_ref, series_ref, hop_own_ref, hop_other_ref, dst_ref, norm_ref, pack_ref,
    adj_ref, inner_ref, inner, dst, grads,
):
    del core_ref

    @at_step(0)
    def _():
        dst[...] = side_by_side(dst_ref[:, 384:448, :])
        grads[0:384, :] = side_by_side(dst_ref[:, 0:384, :])
        grads[384:768, :] = side_by_side(pack_ref[:, 384:768, :])

    weights = weights_of(side_by_side(pick(own_ref, other_ref)), dst[...], norm_ref)[1]
    series = series_ref[...].reshape(GROUP * 128, 384)
    adj_grad = dot_nn(jnp.concatenate([pick(hop_own_ref, hop_other_ref), series], axis=1), grads[...])
    adj_ref[...] = adj_grad
    accumulate(inner, jnp.sum(weights * adj_grad, axis=0, keepdims=True))

    @at_step(1)
    def _():
        rows = jnp.concatenate([inner[:, nodes(block)] for block in range(GROUP)], axis=0)
        inner_ref[...] = jnp.broadcast_to(rows[None], inner_ref.shape)


def adjacency_grad(core, *ins):
    rows = ins[5].shape[0] * 128
    outs = [array(2 * rows, rows, dtype=F32), array(GROUP, GROUP, 128, dtype=F32)]
    scratch = [pltpu.VMEM((1, rows), F32), pltpu.VMEM((64, rows), BF16), pltpu.VMEM((768, rows), BF16)]
    size = 2 * rows * rows
    return call(
        grad_kernel, 2, ins, outs, scratch, 2 * 832 * size, size, core=core, kinds={2: by_core, 8: by_step}
    )


def embed_kernel(
    own_ref, other_ref, adj_ref, dst_ref, norm_ref, inner_ref, second_ref,
    pack_ref, own_out, other_out, inner, total, dst,
):
    @at_step(0)
    def _():
        rows = inner_ref[0]
        for d in range(1, GROUP):
            rows += inner_ref[d]
        for block in range(GROUP):
            inner[0:1, nodes(block)] = rows[block : block + 1, :]
        dst[...] = side_by_side(dst_ref[:, 384:448, :])

    src = side_by_side(pick(own_ref, other_ref))
    scores, weights = weights_of(src, dst[...], norm_ref)
    graded = jnp.where(scores > 0.0, weights * (adj_ref[...] - inner[...]), 0.0).astype(BF16)
    accumulate(total, dot_nn(src, graded))
    d_src = dot_nt(dst[...], graded)
    for block in range(GROUP):
        put(own_out, other_out, block, d_src[:, nodes(block)])

    @at_step(1)
    def _():
        high = total[...].astype(BF16)
        low = (total[...] - high.astype(F32)).astype(BF16)
        for block in range(GROUP):
            pack_ref[block, 0:384, :] = second_ref[block]
            pack_ref[block, 384:448, :] = high[:, nodes(block)]
            pack_ref[block, 448:512, :] = low[:, nodes(block)]


def embed_grads(*ins):
    src, rows = ins[2].shape
    outs = [array(GROUP, 512, 128), array(GROUP, 64, 128, dtype=F32), array(GROUP, 64, 128, dtype=F32)]
    scratch = [pltpu.VMEM((1, rows), F32), pltpu.VMEM((64, rows), F32), pltpu.VMEM((64, rows), BF16)]
    return call(embed_kernel, 2, ins, outs, scratch, 384 * src * rows, src * rows, kinds={2: by_step})


def output_kernel(pack_ref, hop_ref, base_ref, mix1_ref, mix2_ref, out_ref, d_dst_ref):
    second = sum_of(pack_ref, 0, 384).T.astype(BF16)
    mixed = base_ref[...] + dot_nn(hop_ref[...], mix1_ref[...]) + dot_nn(second, mix2_ref[...])
    out_ref[...] = mixed.astype(BF16)
    d_dst_ref[...] = sum_of(pack_ref, 384, 448) + sum_of(pack_ref, 448, 512)


def local(dst_embed, src_embed, series, w_self, w_hop1, w_hop2, cotangent):
    core = jnp.reshape(lax.axis_index("col") % 2, (1,)).astype(jnp.int32)
    all_series = lax.all_gather(series, "col", axis=0).reshape(GROUP, 2, 128, 384)
    src_own, dst, first_mixed, base, mix1, mix2 = prepare(
        dst_embed.T, src_embed.T, series, w_self, w_hop1, w_hop2, cotangent
    )
    src_own = exchange_src(src_own)
    src_other = swap_cores(src_own)
    dst = exchange_dst(dst)
    stats = exchange_dst(softmax_stats(src_own, src_other, dst))

    adjacency, norm, own, other = adjacency_and_carried(src_own, src_other, dst, stats)
    carried = call(add_kernel, 1, (own, swap_cores(other)), [array(GROUP, 384, 128)])[0]
    hop_part = first_hop(core, adjacency, all_series)
    carried = exchange_src(carried)
    pack = call(first_grad_kernel, 1, (carried, first_mixed, hop_part), [array(GROUP, 768, 128)])[0]
    pack = exchange_dst(pack)
    hop, hop_own = call(join_kernel, 1, (pack,), [array(128, 384), array(GROUP * 128, 384)])
    hop_own = exchange_src(hop_own.reshape(GROUP, 128, 384)).reshape(-1, 384)
    hop_other = swap_cores(hop_own)

    adj_grad, inner = adjacency_grad(
        core, src_own, src_other, all_series, hop_own, hop_other, dst, norm, pack
    )
    inner = exchange_dst(inner)
    second_part = second_hop(adjacency, hop_own, hop_other)
    pack, own, other = embed_grads(src_own, src_other, adj_grad, dst, norm, inner, second_part)
    pack = exchange_dst(pack)
    output, d_dst = call(
        output_kernel, 1, (pack, hop, base, mix1, mix2), [array(128, 384), array(64, 128, dtype=F32)],
        flops=4 * 128 * 384 * 384,
    )
    d_src = jnp.sum(exchange_src(own + swap_cores(other)), axis=0)
    return output, d_dst.T, d_src.T


def solution(mesh):
    blocks = P(("row", "col"), None)
    return jax.shard_map(
        local,
        mesh=mesh,
        in_specs=(blocks, blocks, blocks, P(), P(), P(), blocks),
        out_specs=(blocks, blocks, blocks),
        check_vma=False,
    )
```

```python
import jax
import jax.numpy as jnp
from jax import lax
from jax.experimental import pallas as pl
from jax.experimental.pallas import tpu as pltpu
from jax.sharding import PartitionSpec as P

BF16 = jnp.bfloat16
F32 = jnp.float32
GROUP = 8
MIB = 1024 * 1024
VMEM_BYTES = 28 * MIB

SAME_CORE = [[2 * chip + core for chip in range(8)] for core in range(2)]
OTHER_CORE = [(i, i ^ 1) for i in range(16)]


def dot_nn(a, b):
    return lax.dot_general(a, b, (((1,), (0,)), ((), ())), preferred_element_type=F32)


def dot_nt(a, b):
    return lax.dot_general(a, b, (((1,), (1,)), ((), ())), preferred_element_type=F32)


def dot_tn(a, b):
    return lax.dot_general(a, b, (((0,), (0,)), ((), ())), preferred_element_type=F32)


def exchange_dst(blocks):
    return lax.all_to_all(blocks, "row", 0, 0)


def exchange_src(blocks):
    return lax.all_to_all(blocks, "col", 0, 0, axis_index_groups=SAME_CORE)


def swap_cores(blocks):
    return lax.ppermute(blocks, "col", OTHER_CORE)


def array(*shape, dtype=BF16):
    return jax.ShapeDtypeStruct(shape, dtype)


def whole(a):
    return pl.BlockSpec(a.shape, lambda *_: (0,) * len(a.shape))


def by_step(a):
    return pl.BlockSpec((a.shape[0] // 2,) + a.shape[1:], lambda i, *_: (i,) + (0,) * (len(a.shape) - 1))


def call(kernel, steps, ins, outs, scratch=(), flops=0, exps=0, kinds=None, vmem=VMEM_BYTES):
    kinds = kinds or {}
    sizes = [a.size * a.dtype.itemsize for a in list(ins) + list(outs)]
    specs = [kinds.get(i, whole)(a) for i, a in enumerate(list(ins) + list(outs))]
    return pl.pallas_call(
        kernel,
        grid=(steps,),
        in_specs=specs[: len(ins)],
        out_specs=specs[len(ins) :],
        out_shape=outs,
        scratch_shapes=scratch,
        compiler_params=pltpu.CompilerParams(vmem_limit_bytes=vmem),
        cost_estimate=pl.CostEstimate(flops=flops, bytes_accessed=sum(sizes), transcendentals=exps),
    )(*ins)


def at_step(step):
    return pl.when(pl.program_id(0) == step)


def pick(own_ref, other_ref):
    return jnp.where(pl.program_id(0) == 0, own_ref[...], other_ref[...])


def put(own_ref, other_ref, block, value):
    @at_step(0)
    def _():
        own_ref[block] = value

    @at_step(1)
    def _():
        other_ref[block] = value


def accumulate(total, part):
    @at_step(0)
    def _():
        total[...] = part

    @at_step(1)
    def _():
        total[...] += part


def side_by_side(blocks):
    return jnp.concatenate([blocks[b] for b in range(GROUP)], axis=1)


def nodes(block):
    return slice(128 * block, 128 * block + 128)


def series_of(packed):
    return jnp.concatenate([packed[b, 0:128, :] for b in range(GROUP)], axis=0)


def src_of(packed):
    pieces = [packed[:, 128:160, 0:128], packed[:, 128:160, 128:256]]
    return side_by_side(jnp.concatenate(pieces, axis=1))


def mixing(weight):
    size, chan = 384, weight.shape[0]
    place = lax.broadcasted_iota(jnp.int32, (size, chan), 0) % chan
    repeat = jnp.where(place == lax.broadcasted_iota(jnp.int32, (size, chan), 1), 1.0, 0.0).astype(BF16)
    tiled = dot_nt(dot_nn(repeat, weight).astype(BF16), repeat)
    rows = lax.broadcasted_iota(jnp.int32, (size, size), 0) // chan
    cols = lax.broadcasted_iota(jnp.int32, (size, size), 1) // chan
    return jnp.where(rows == cols, tiled, 0.0).astype(BF16)


def prepare_kernel(
    dst_ref, src_ref, series_ref, self_ref, hop1_ref, hop2_ref, cotangent_ref,
    src_out, dst_out, first_out, base_out, mix1_out, mix2_out,
):
    mix1, mix2 = mixing(hop1_ref[...]), mixing(hop2_ref[...])
    cotangent = cotangent_ref[...]
    second = dot_nt(mix2, cotangent).astype(BF16)
    for block in range(GROUP):
        src_out[block, 0:128, :] = series_ref[...]
        src_out[block, 128:160, 0:128] = src_ref[0:32, :]
        src_out[block, 128:160, 128:256] = src_ref[32:64, :]
        src_out[block, 128:160, 256:384] = jnp.zeros((32, 128), BF16)
        dst_out[block, 0:384, :] = second
        dst_out[block, 384:448, :] = dst_ref[...]
    first_out[...] = dot_nt(mix1, cotangent)
    base_out[...] = dot_nn(series_ref[...], mixing(self_ref[...]))
    mix1_out[...] = mix1
    mix2_out[...] = mix2


def prepare(*ins):
    outs = [
        array(GROUP, 160, 384),
        array(GROUP, 448, 128),
        array(384, 128, dtype=F32),
        array(128, 384, dtype=F32),
        array(384, 384),
        array(384, 384),
    ]
    return call(prepare_kernel, 1, ins, outs, flops=3 * 2 * 128 * 384 * 384, vmem=60 * MIB)


def stats_kernel(own_ref, other_ref, dst_ref, out_ref, state, dst):
    @at_step(0)
    def _():
        state[...] = jnp.zeros_like(state)
        dst[...] = side_by_side(dst_ref[:, 384:448, :])

    lifted = jnp.maximum(dot_tn(src_of(pick(own_ref, other_ref)), dst[...]), 0.0)
    old = state[0:1, :]
    new = jnp.maximum(old, jnp.max(lifted, axis=0, keepdims=True))
    total = jnp.sum(jnp.exp(lifted - new), axis=0, keepdims=True)
    state[1:2, :] = state[1:2, :] * jnp.exp(old - new) + total
    state[0:1, :] = new

    @at_step(1)
    def _():
        out_ref[...] = jnp.broadcast_to(state[...][None], out_ref.shape)


def softmax_stats(own, other, dst):
    rows = dst.shape[0] * 128
    scratch = [pltpu.VMEM((2, rows), F32), pltpu.VMEM((64, rows), BF16)]
    outs = [array(GROUP, 2, rows, dtype=F32)]
    size = 2 * rows * rows
    return call(stats_kernel, 2, (own, other, dst), outs, scratch, 128 * size, size)[0]


def weights_of(src, dst, norm_ref):
    scores = dot_tn(src, dst)
    weights = jnp.exp(jnp.maximum(scores, 0.0) - norm_ref[0:1, :]) * norm_ref[1:2, :]
    return scores, weights


def hops_kernel(
    own_ref, other_ref, dst_ref, stats_ref, norm_ref, hop_ref, own_out, other_out, total, dst, second
):
    @at_step(0)
    def _():
        peak = stats_ref[0, 0:1, :]
        for d in range(1, GROUP):
            peak = jnp.maximum(peak, stats_ref[d, 0:1, :])
        row_sum = jnp.zeros_like(peak)
        for d in range(GROUP):
            row_sum += stats_ref[d, 1:2, :] * jnp.exp(stats_ref[d, 0:1, :] - peak)
        norm_ref[0:1, :] = peak
        norm_ref[1:2, :] = 1.0 / row_sum
        second[...] = side_by_side(dst_ref[:, 0:384, :])
        dst[...] = side_by_side(dst_ref[:, 384:448, :])

    packed = pick(own_ref, other_ref)
    adjacency = weights_of(src_of(packed), dst[...], norm_ref)[1].astype(BF16)
    carried = dot_nt(second[...], adjacency).astype(BF16)
    for block in range(GROUP):
        put(own_out, other_out, block, carried[:, nodes(block)])
    accumulate(total, dot_tn(series_of(packed), adjacency))

    @at_step(1)
    def _():
        for block in range(GROUP):
            hop_ref[block] = total[:, nodes(block)].astype(BF16)


def first_hops(own, other, dst, stats):
    rows = dst.shape[0] * 128
    outs = [array(2, rows, dtype=F32)] + [array(GROUP, 384, 128)] * 3
    scratch = [pltpu.VMEM((384, rows), F32), pltpu.VMEM((64, rows), BF16), pltpu.VMEM((384, rows), BF16)]
    size = 2 * rows * rows
    return call(hops_kernel, 2, (own, other, dst, stats), outs, scratch, 2 * 832 * size, size)


def sum_of(pack_ref, start, stop):
    total = pack_ref[0, start:stop, :].astype(F32)
    for d in range(1, GROUP):
        total += pack_ref[d, start:stop, :].astype(F32)
    return total


def join_kernel(hop_ref, own_ref, other_ref, hop_out, pack_out):
    hop = sum_of(hop_ref, 0, 384).T.astype(BF16)
    hop_out[...] = hop
    for block in range(GROUP):
        carried = own_ref[block].astype(F32) + other_ref[block].astype(F32)
        pack_out[block, 0:384, :] = carried.astype(BF16)
        for part in range(3):
            pack_out[block, 384 + 128 * part : 512 + 128 * part, :] = hop[:, nodes(part)]


def split_kernel(pack_ref, mixed_ref, first_out, hop_out):
    grad = (mixed_ref[...] + sum_of(pack_ref, 0, 384)).astype(BF16)
    for block in range(GROUP):
        first_out[block] = grad
        for part in range(3):
            hop_out[nodes(block), nodes(part)] = pack_ref[block, 384 + 128 * part : 512 + 128 * part, :]


def second_kernel(own_ref, other_ref, hop_own_ref, hop_other_ref, dst_ref, norm_ref, out_ref, total, dst):
    @at_step(0)
    def _():
        dst[...] = side_by_side(dst_ref[:, 384:448, :])

    src = src_of(pick(own_ref, other_ref))
    adjacency = weights_of(src, dst[...], norm_ref)[1].astype(BF16)
    accumulate(total, dot_tn(pick(hop_own_ref, hop_other_ref), adjacency))

    @at_step(1)
    def _():
        for block in range(GROUP):
            out_ref[block] = total[:, nodes(block)].astype(BF16)


def second_hop(*ins):
    rows = ins[4].shape[0] * 128
    scratch = [pltpu.VMEM((384, rows), F32), pltpu.VMEM((64, rows), BF16)]
    size = 2 * rows * rows
    return call(second_kernel, 2, ins, [array(GROUP, 384, 128)], scratch, 896 * size, size)[0]


def three_terms(value):
    high = value.astype(BF16).astype(F32)
    middle = (value - high).astype(BF16).astype(F32)
    return [high, middle, value - high - middle]


SECOND, ABOVE, BELOW, INNER, SHIFT, LAST = 0, 384, 448, 512, 536, 544


def grad_kernel(
    own_ref, other_ref, hop_own_ref, hop_other_ref, dst_ref, norm_ref, first_ref, second_ref,
    pack_ref, masked_ref, shift_ref, own_out, other_out, inner, mass, above, below, dst, grads, adj, wide,
):
    step = pl.program_id(0)
    half = step % 2

    @at_step(0)
    def _():
        dst[...] = side_by_side(dst_ref[:, 384:448, :])
        grads[0:384, :] = side_by_side(dst_ref[:, 0:384, :])
        grads[384:768, :] = side_by_side(first_ref)

    packed = jnp.where(half == 0, own_ref[...], other_ref[...])
    src = src_of(packed)

    @pl.when(step < 2)
    def _():
        scores, weights = weights_of(src, dst[...], norm_ref)
        hop = jnp.where(half == 0, hop_own_ref[...], hop_other_ref[...])
        adj_grad = dot_nn(jnp.concatenate([hop, series_of(packed)], axis=1), grads[...])
        adj[half] = adj_grad
        wide[half] = jnp.where(scores > 0.0, weights, 0.0)
        total = jnp.sum(weights * adj_grad, axis=0, keepdims=True)
        weight = jnp.sum(weights, axis=0, keepdims=True)
        inner[...] = jnp.where(step == 0, total, inner[...] + total)
        mass[...] = jnp.where(step == 0, weight, mass[...] + weight)

    @pl.when(step >= 2)
    def _():
        shift = jnp.where(mass[...] > 1e-30, inner[...] / jnp.maximum(mass[...], 1e-30), 0.0)
        masked = wide[half]
        graded = (masked * (adj[half] - shift)).astype(BF16)
        masked = masked.astype(BF16)
        masked_ref[...] = masked
        up, low = dot_nn(src, graded), dot_nn(src, masked)
        above[...] = jnp.where(step == 2, up, above[...] + up)
        below[...] = jnp.where(step == 2, low, below[...] + low)
        d_src = dot_nt(dst[...], graded)

        @pl.when(half == 0)
        def _():
            for block in range(GROUP):
                own_out[block] = d_src[:, nodes(block)]

        @pl.when(half == 1)
        def _():
            shift_ref[...] = shift
            for block in range(GROUP):
                other_out[block] = d_src[:, nodes(block)]
            sums = [term[:, nodes(block)] for term in three_terms(inner[...]) for block in range(GROUP)]
            sums = jnp.concatenate(sums, axis=0)
            shifts = jnp.concatenate(three_terms(shift), axis=0)
            for block in range(GROUP):
                tail = jnp.concatenate([sums, shifts[:, nodes(block)], jnp.zeros((5, 128), F32)], axis=0)
                pack_ref[block, SECOND:ABOVE, :] = second_ref[block]
                pack_ref[block, ABOVE:BELOW, :] = above[:, nodes(block)].astype(BF16)
                pack_ref[block, BELOW:INNER, :] = below[:, nodes(block)].astype(BF16)
                pack_ref[block, INNER:LAST, :] = tail.astype(BF16)


def embed_grads(*ins):
    rows = ins[4].shape[0] * 128
    outs = [
        array(GROUP, LAST, 128),
        array(2 * rows, rows),
        array(1, rows, dtype=F32),
        array(GROUP, 64, 128, dtype=F32),
        array(GROUP, 64, 128, dtype=F32),
    ]
    scratch = [
        pltpu.VMEM((1, rows), F32),
        pltpu.VMEM((1, rows), F32),
        pltpu.VMEM((64, rows), F32),
        pltpu.VMEM((64, rows), F32),
        pltpu.VMEM((64, rows), BF16),
        pltpu.VMEM((768, rows), BF16),
        pltpu.VMEM((2, rows, rows), F32),
        pltpu.VMEM((2, rows, rows), F32),
    ]

    def second_pass(a):
        return pl.BlockSpec((a.shape[0] // 2, a.shape[1]), lambda i: (jnp.maximum(i - 2, 0), 0))

    size = 2 * rows * rows
    return call(
        grad_kernel, 4, ins, outs, scratch, 2 * 1024 * size, size, kinds={len(ins) + 1: second_pass}, vmem=46 * MIB
    )


def inner_of(pack_ref):
    terms = sum_of(pack_ref, INNER, LAST)
    return terms[0:8] + (terms[8:16] + terms[16:24])


def src_kernel(masked_ref, dst_ref, pack_ref, shift_ref, own_ref, other_ref, own_out, other_out, scaled):
    @at_step(0)
    def _():
        inner = inner_of(pack_ref)
        for block in range(GROUP):
            change = shift_ref[:, nodes(block)] - inner[block : block + 1, :]
            scaled[:, nodes(block)] = (dst_ref[block, 384:448, :].astype(F32) * change).astype(BF16)

    part = dot_nt(scaled[...], masked_ref[...])

    @at_step(0)
    def _():
        for block in range(GROUP):
            own_out[block] = own_ref[block] + part[:, nodes(block)]

    @at_step(1)
    def _():
        for block in range(GROUP):
            other_out[block] = other_ref[block] + part[:, nodes(block)]


def src_grads(*ins):
    src, rows = ins[0].shape
    outs = [array(GROUP, 64, 128, dtype=F32), array(GROUP, 64, 128, dtype=F32)]
    scratch = [pltpu.VMEM((64, rows), BF16)]
    return call(src_kernel, 2, ins, outs, scratch, 128 * src * rows, kinds={0: by_step})


def output_kernel(pack_ref, hop_ref, base_ref, mix1_ref, mix2_ref, out_ref, d_dst_ref):
    second = sum_of(pack_ref, SECOND, ABOVE).T.astype(BF16)
    mixed = base_ref[...] + dot_nn(hop_ref[...], mix1_ref[...]) + dot_nn(second, mix2_ref[...])
    out_ref[...] = mixed.astype(BF16)
    me = lax.axis_index("row")
    inner = inner_of(pack_ref)
    places = lax.broadcasted_iota(jnp.int32, inner.shape, 0)
    inner = jnp.sum(jnp.where(places == me, inner, 0.0), axis=0, keepdims=True)
    d_dst = jnp.zeros((64, 128), F32)
    for d in range(GROUP):
        tail = pack_ref[d, INNER:LAST, :].astype(F32)
        shift = tail[24:25] + (tail[25:26] + tail[26:27])
        above, below = pack_ref[d, ABOVE:BELOW, :].astype(F32), pack_ref[d, BELOW:INNER, :].astype(F32)
        d_dst += above + (shift - inner) * below
    d_dst_ref[...] = d_dst


def local(dst_embed, src_embed, series, w_self, w_hop1, w_hop2, cotangent):
    src_own, dst, first_mixed, base, mix1, mix2 = prepare(
        dst_embed.T, src_embed.T, series, w_self, w_hop1, w_hop2, cotangent
    )
    src_own = exchange_src(src_own)
    src_other = swap_cores(src_own)
    dst = exchange_dst(dst)
    stats = exchange_dst(softmax_stats(src_own, src_other, dst))

    norm, hop, own, other = first_hops(src_own, src_other, dst, stats)
    hop = exchange_dst(hop)
    hop, pack = call(
        join_kernel, 1, (hop, own, swap_cores(other)), [array(128, 384), array(GROUP, 768, 128)]
    )
    pack = exchange_src(pack)
    first, hop_own = call(
        split_kernel, 1, (pack, first_mixed), [array(GROUP, 384, 128), array(GROUP * 128, 384)]
    )
    hop_other = swap_cores(hop_own)
    first = exchange_dst(first)

    second = second_hop(src_own, src_other, hop_own, hop_other, dst, norm)
    pack, masked, shift, own, other = embed_grads(
        src_own, src_other, hop_own, hop_other, dst, norm, first, second
    )
    pack = exchange_dst(pack)
    own, other = src_grads(masked, dst, pack, shift, own, other)
    output, d_dst = call(
        output_kernel, 1, (pack, hop, base, mix1, mix2), [array(128, 384), array(64, 128, dtype=F32)],
        flops=4 * 128 * 384 * 384,
    )
    d_src = jnp.sum(exchange_src(own + swap_cores(other)), axis=0)
    return output, d_dst.T, d_src.T


def solution(mesh):
    blocks = P(("row", "col"), None)
    return jax.shard_map(
        local,
        mesh=mesh,
        in_specs=(blocks, blocks, blocks, P(), P(), P(), blocks),
        out_specs=(blocks, blocks, blocks),
        check_vma=False,
    )
```

```python
import jax
import jax.numpy as jnp
from jax import lax
from jax.experimental import pallas as pl
from jax.experimental.pallas import tpu as pltpu
from jax.sharding import PartitionSpec as P

BF16 = jnp.bfloat16
F32 = jnp.float32
GROUP = 8
MIB = 1024 * 1024
VMEM_BYTES = 28 * MIB

SAME_CORE = [[2 * chip + core for chip in range(8)] for core in range(2)]
OTHER_CORE = [(i, i ^ 1) for i in range(16)]


def dot_nn(a, b):
    return lax.dot_general(a, b, (((1,), (0,)), ((), ())), preferred_element_type=F32)


def dot_nt(a, b):
    return lax.dot_general(a, b, (((1,), (1,)), ((), ())), preferred_element_type=F32)


def dot_tn(a, b):
    return lax.dot_general(a, b, (((0,), (0,)), ((), ())), preferred_element_type=F32)


def exchange_dst(blocks):
    return lax.all_to_all(blocks, "row", 0, 0)


def exchange_src(blocks):
    return lax.all_to_all(blocks, "col", 0, 0, axis_index_groups=SAME_CORE)


def swap_cores(blocks):
    return lax.ppermute(blocks, "col", OTHER_CORE)


def array(*shape, dtype=BF16):
    return jax.ShapeDtypeStruct(shape, dtype)


def whole(a):
    return pl.BlockSpec(a.shape, lambda *_: (0,) * len(a.shape))


def by_step(a):
    return pl.BlockSpec((a.shape[0] // 2,) + a.shape[1:], lambda i, *_: (i,) + (0,) * (len(a.shape) - 1))


def call(kernel, steps, ins, outs, scratch=(), flops=0, exps=0, kinds=None, vmem=VMEM_BYTES):
    kinds = kinds or {}
    sizes = [a.size * a.dtype.itemsize for a in list(ins) + list(outs)]
    specs = [kinds.get(i, whole)(a) for i, a in enumerate(list(ins) + list(outs))]
    return pl.pallas_call(
        kernel,
        grid=(steps,),
        in_specs=specs[: len(ins)],
        out_specs=specs[len(ins) :],
        out_shape=outs,
        scratch_shapes=scratch,
        compiler_params=pltpu.CompilerParams(vmem_limit_bytes=vmem),
        cost_estimate=pl.CostEstimate(flops=flops, bytes_accessed=sum(sizes), transcendentals=exps),
    )(*ins)


def at_step(step):
    return pl.when(pl.program_id(0) == step)


def pick(own_ref, other_ref):
    return jnp.where(pl.program_id(0) == 0, own_ref[...], other_ref[...])


def put(own_ref, other_ref, block, value):
    @at_step(0)
    def _():
        own_ref[block] = value

    @at_step(1)
    def _():
        other_ref[block] = value


def accumulate(total, part):
    @at_step(0)
    def _():
        total[...] = part

    @at_step(1)
    def _():
        total[...] += part


def side_by_side(blocks):
    return jnp.concatenate([blocks[b] for b in range(GROUP)], axis=1)


def nodes(block):
    return slice(128 * block, 128 * block + 128)


def series_of(packed):
    return jnp.concatenate([packed[b, 0:128, :] for b in range(GROUP)], axis=0)


def src_of(packed):
    pieces = [packed[:, 128:160, 0:128], packed[:, 128:160, 128:256]]
    return side_by_side(jnp.concatenate(pieces, axis=1))


def mixing(weight):
    size, chan = 384, weight.shape[0]
    place = lax.broadcasted_iota(jnp.int32, (size, chan), 0) % chan
    repeat = jnp.where(place == lax.broadcasted_iota(jnp.int32, (size, chan), 1), 1.0, 0.0).astype(BF16)
    tiled = dot_nt(dot_nn(repeat, weight).astype(BF16), repeat)
    rows = lax.broadcasted_iota(jnp.int32, (size, size), 0) // chan
    cols = lax.broadcasted_iota(jnp.int32, (size, size), 1) // chan
    return jnp.where(rows == cols, tiled, 0.0).astype(BF16)


def source_kernel(src_ref, series_ref, src_out):
    src_out[:, 0:128, :] = jnp.broadcast_to(series_ref[...][None], (GROUP, 128, 384))
    for block in range(GROUP):
        src_out[block, 128:160, 0:128] = src_ref[0:32, :]
        src_out[block, 128:160, 128:256] = src_ref[32:64, :]
        src_out[block, 128:160, 256:384] = jnp.zeros((32, 128), BF16)


def prepare_kernel(
    dst_ref, series_ref, self_ref, hop1_ref, hop2_ref, cotangent_ref, dst_out, first_out, base_out, mix1_out, mix2_out
):
    mix1, mix2 = mixing(hop1_ref[...]), mixing(hop2_ref[...])
    cotangent = cotangent_ref[...]
    second = dot_nt(mix2, cotangent).astype(BF16)
    for block in range(GROUP):
        dst_out[block, 0:384, :] = second
        dst_out[block, 384:448, :] = dst_ref[...]
    first_out[...] = dot_nt(mix1, cotangent)
    base_out[...] = dot_nn(series_ref[...], mixing(self_ref[...]))
    mix1_out[...] = mix1
    mix2_out[...] = mix2


def prepare(*ins):
    outs = [
        array(GROUP, 448, 128),
        array(384, 128, dtype=F32),
        array(128, 384, dtype=F32),
        array(384, 384),
        array(384, 384),
    ]
    return call(prepare_kernel, 1, ins, outs, flops=3 * 2 * 128 * 384 * 384, vmem=60 * MIB)


def stats_kernel(own_ref, other_ref, dst_ref, out_ref, state, dst):
    @at_step(0)
    def _():
        state[...] = jnp.zeros_like(state)
        dst[...] = side_by_side(dst_ref[:, 384:448, :])

    lifted = jnp.maximum(dot_tn(src_of(pick(own_ref, other_ref)), dst[...]), 0.0)
    old = state[0:1, :]
    new = jnp.maximum(old, jnp.max(lifted, axis=0, keepdims=True))
    total = jnp.sum(jnp.exp(lifted - new), axis=0, keepdims=True)
    state[1:2, :] = state[1:2, :] * jnp.exp(old - new) + total
    state[0:1, :] = new

    @at_step(1)
    def _():
        out_ref[...] = jnp.broadcast_to(state[...][None], out_ref.shape)


def softmax_stats(own, other, dst):
    rows = dst.shape[0] * 128
    scratch = [pltpu.VMEM((2, rows), F32), pltpu.VMEM((64, rows), BF16)]
    outs = [array(GROUP, 2, rows, dtype=F32)]
    size = 2 * rows * rows
    return call(stats_kernel, 2, (own, other, dst), outs, scratch, 128 * size, size)[0]


def weights_of(src, dst, norm_ref):
    scores = dot_tn(src, dst)
    weights = jnp.exp(jnp.maximum(scores, 0.0) - norm_ref[0:1, :]) * norm_ref[1:2, :]
    return scores, weights


def hops_kernel(
    own_ref, other_ref, dst_ref, stats_ref, norm_ref, hop_ref, own_out, other_out, total, dst, second
):
    @at_step(0)
    def _():
        peak = stats_ref[0, 0:1, :]
        for d in range(1, GROUP):
            peak = jnp.maximum(peak, stats_ref[d, 0:1, :])
        row_sum = jnp.zeros_like(peak)
        for d in range(GROUP):
            row_sum += stats_ref[d, 1:2, :] * jnp.exp(stats_ref[d, 0:1, :] - peak)
        norm_ref[0:1, :] = peak
        norm_ref[1:2, :] = 1.0 / row_sum
        second[...] = side_by_side(dst_ref[:, 0:384, :])
        dst[...] = side_by_side(dst_ref[:, 384:448, :])

    packed = pick(own_ref, other_ref)
    adjacency = weights_of(src_of(packed), dst[...], norm_ref)[1].astype(BF16)
    carried = dot_nt(second[...], adjacency).astype(BF16)
    for block in range(GROUP):
        put(own_out, other_out, block, carried[:, nodes(block)])
    accumulate(total, dot_tn(series_of(packed), adjacency))

    @at_step(1)
    def _():
        for block in range(GROUP):
            hop_ref[block] = total[:, nodes(block)].astype(BF16)


def first_hops(own, other, dst, stats):
    rows = dst.shape[0] * 128
    outs = [array(2, rows, dtype=F32)] + [array(GROUP, 384, 128)] * 3
    scratch = [pltpu.VMEM((384, rows), F32), pltpu.VMEM((64, rows), BF16), pltpu.VMEM((384, rows), BF16)]
    size = 2 * rows * rows
    return call(hops_kernel, 2, (own, other, dst, stats), outs, scratch, 2 * 832 * size, size)


def sum_of(pack_ref, start, stop):
    total = pack_ref[0, start:stop, :].astype(F32)
    for d in range(1, GROUP):
        total += pack_ref[d, start:stop, :].astype(F32)
    return total


def join_kernel(hop_ref, own_ref, other_ref, hop_out, pack_out):
    hop = sum_of(hop_ref, 0, 384).T.astype(BF16)
    hop_out[...] = hop
    for block in range(GROUP):
        carried = own_ref[block].astype(F32) + other_ref[block].astype(F32)
        pack_out[block, 0:384, :] = carried.astype(BF16)
        for part in range(3):
            pack_out[block, 384 + 128 * part : 512 + 128 * part, :] = hop[:, nodes(part)]


def split_kernel(pack_ref, mixed_ref, first_out, hop_out):
    grad = (mixed_ref[...] + sum_of(pack_ref, 0, 384)).astype(BF16)
    for block in range(GROUP):
        first_out[block] = grad
        for part in range(3):
            hop_out[nodes(block), nodes(part)] = pack_ref[block, 384 + 128 * part : 512 + 128 * part, :]


def three_terms(value):
    high = value.astype(BF16).astype(F32)
    middle = (value - high).astype(BF16).astype(F32)
    return [high, middle, value - high - middle]


SECOND, ABOVE, BELOW, INNER, SHIFT, LAST = 0, 384, 448, 512, 536, 544


def grad_kernel(
    own_ref, other_ref, hop_own_ref, hop_other_ref, dst_ref, norm_ref, first_ref,
    pack_ref, shift_ref, own_out, other_out, inner, mass, above, below, dst, grads, adj, wide, second,
):
    step = pl.program_id(0)
    half = step % 2

    @at_step(0)
    def _():
        dst[...] = side_by_side(dst_ref[:, 384:448, :])
        grads[0:384, :] = side_by_side(dst_ref[:, 0:384, :])
        grads[384:768, :] = side_by_side(first_ref)

    packed = jnp.where(half == 0, own_ref[...], other_ref[...])
    src = src_of(packed)

    @pl.when(step < 2)
    def _():
        scores, weights = weights_of(src, dst[...], norm_ref)
        hop = jnp.where(half == 0, hop_own_ref[...], hop_other_ref[...])
        adj_grad = dot_nn(jnp.concatenate([hop, series_of(packed)], axis=1), grads[...])
        adj[half] = adj_grad
        wide[half] = jnp.where(scores > 0.0, weights, 0.0)
        hop_part = dot_tn(hop, weights.astype(BF16))
        second[...] = jnp.where(step == 0, hop_part, second[...] + hop_part)
        total = jnp.sum(weights * adj_grad, axis=0, keepdims=True)
        weight = jnp.sum(weights, axis=0, keepdims=True)
        inner[...] = jnp.where(step == 0, total, inner[...] + total)
        mass[...] = jnp.where(step == 0, weight, mass[...] + weight)

    @pl.when(step >= 2)
    def _():
        shift = jnp.where(mass[...] > 1e-30, inner[...] / jnp.maximum(mass[...], 1e-30), 0.0)
        masked = wide[half]
        graded = (masked * (adj[half] - shift)).astype(BF16)
        masked = masked.astype(BF16)
        up, low = dot_nn(src, graded), dot_nn(src, masked)
        above[...] = jnp.where(step == 2, up, above[...] + up)
        below[...] = jnp.where(step == 2, low, below[...] + low)
        d_src = dot_nt(dst[...], graded)

        @pl.when(half == 0)
        def _():
            for block in range(GROUP):
                own_out[block] = d_src[:, nodes(block)]

        @pl.when(half == 1)
        def _():
            shift_ref[...] = shift
            for block in range(GROUP):
                other_out[block] = d_src[:, nodes(block)]
            sums = [term[:, nodes(block)] for term in three_terms(inner[...]) for block in range(GROUP)]
            sums = jnp.concatenate(sums, axis=0)
            shifts = jnp.concatenate(three_terms(shift), axis=0)
            for block in range(GROUP):
                tail = jnp.concatenate([sums, shifts[:, nodes(block)], jnp.zeros((5, 128), F32)], axis=0)
                pack_ref[block, SECOND:ABOVE, :] = second[:, nodes(block)].astype(BF16)
                pack_ref[block, ABOVE:BELOW, :] = above[:, nodes(block)].astype(BF16)
                pack_ref[block, BELOW:INNER, :] = below[:, nodes(block)].astype(BF16)
                pack_ref[block, INNER:LAST, :] = tail.astype(BF16)


def embed_grads(*ins):
    rows = ins[4].shape[0] * 128
    outs = [
        array(GROUP, LAST, 128),
        array(1, rows, dtype=F32),
        array(GROUP, 64, 128, dtype=F32),
        array(GROUP, 64, 128, dtype=F32),
    ]
    scratch = [
        pltpu.VMEM((1, rows), F32),
        pltpu.VMEM((1, rows), F32),
        pltpu.VMEM((64, rows), F32),
        pltpu.VMEM((64, rows), F32),
        pltpu.VMEM((64, rows), BF16),
        pltpu.VMEM((768, rows), BF16),
        pltpu.VMEM((2, rows, rows), F32),
        pltpu.VMEM((2, rows, rows), F32),
        pltpu.VMEM((384, rows), F32),
    ]

    size = 2 * rows * rows
    return call(
        grad_kernel, 4, ins, outs, scratch, 2 * 1408 * size, size, vmem=46 * MIB
    )


def inner_of(pack_ref):
    terms = sum_of(pack_ref, INNER, LAST)
    return terms[0:8] + (terms[8:16] + terms[16:24])


def src_kernel(
    own_ref, other_ref, dst_ref, norm_ref, pack_ref, shift_ref, own_part, other_part, own_out, other_out, scaled, dst
):
    @at_step(0)
    def _():
        dst[...] = side_by_side(dst_ref[:, 384:448, :])
        inner = inner_of(pack_ref)
        for block in range(GROUP):
            change = shift_ref[:, nodes(block)] - inner[block : block + 1, :]
            scaled[:, nodes(block)] = (dst[:, nodes(block)].astype(F32) * change).astype(BF16)

    scores, weights = weights_of(src_of(pick(own_ref, other_ref)), dst[...], norm_ref)
    part = dot_nt(scaled[...], jnp.where(scores > 0.0, weights, 0.0).astype(BF16))

    @at_step(0)
    def _():
        for block in range(GROUP):
            own_out[block] = own_part[block] + part[:, nodes(block)]

    @at_step(1)
    def _():
        for block in range(GROUP):
            other_out[block] = other_part[block] + part[:, nodes(block)]


def src_grads(*ins):
    rows = ins[2].shape[0] * 128
    outs = [array(GROUP, 64, 128, dtype=F32), array(GROUP, 64, 128, dtype=F32)]
    scratch = [pltpu.VMEM((64, rows), BF16), pltpu.VMEM((64, rows), BF16)]
    size = 2 * rows * rows
    return call(src_kernel, 2, ins, outs, scratch, 256 * size, size)


def output_kernel(pack_ref, hop_ref, base_ref, mix1_ref, mix2_ref, out_ref, d_dst_ref):
    second = sum_of(pack_ref, SECOND, ABOVE).T.astype(BF16)
    mixed = base_ref[...] + dot_nn(hop_ref[...], mix1_ref[...]) + dot_nn(second, mix2_ref[...])
    out_ref[...] = mixed.astype(BF16)
    me = lax.axis_index("row")
    inner = inner_of(pack_ref)
    places = lax.broadcasted_iota(jnp.int32, inner.shape, 0)
    inner = jnp.sum(jnp.where(places == me, inner, 0.0), axis=0, keepdims=True)
    d_dst = jnp.zeros((64, 128), F32)
    for d in range(GROUP):
        tail = pack_ref[d, INNER:LAST, :].astype(F32)
        shift = tail[24:25] + (tail[25:26] + tail[26:27])
        above, below = pack_ref[d, ABOVE:BELOW, :].astype(F32), pack_ref[d, BELOW:INNER, :].astype(F32)
        d_dst += above + (shift - inner) * below
    d_dst_ref[...] = d_dst


def local(dst_embed, src_embed, series, w_self, w_hop1, w_hop2, cotangent):
    src_own = call(source_kernel, 1, (src_embed.T, series), [array(GROUP, 160, 384)], vmem=60 * MIB)[0]
    src_own = exchange_src(src_own)
    dst, first_mixed, base, mix1, mix2 = prepare(dst_embed.T, series, w_self, w_hop1, w_hop2, cotangent)
    src_other = swap_cores(src_own)
    dst = exchange_dst(dst)
    stats = exchange_dst(softmax_stats(src_own, src_other, dst))

    norm, hop, own, other = first_hops(src_own, src_other, dst, stats)
    hop = exchange_dst(hop)
    hop, pack = call(
        join_kernel, 1, (hop, own, swap_cores(other)), [array(128, 384), array(GROUP, 768, 128)]
    )
    pack = exchange_src(pack)
    first, hop_own = call(
        split_kernel, 1, (pack, first_mixed), [array(GROUP, 384, 128), array(GROUP * 128, 384)]
    )
    hop_other = swap_cores(hop_own)
    first = exchange_dst(first)

    pack, shift, own, other = embed_grads(src_own, src_other, hop_own, hop_other, dst, norm, first)
    pack = exchange_dst(pack)
    own, other = src_grads(src_own, src_other, dst, norm, pack, shift, own, other)
    output, d_dst = call(
        output_kernel, 1, (pack, hop, base, mix1, mix2), [array(128, 384), array(64, 128, dtype=F32)],
        flops=4 * 128 * 384 * 384,
    )
    d_src = jnp.sum(exchange_src(own + swap_cores(other)), axis=0)
    return output, d_dst.T, d_src.T


def solution(mesh):
    blocks = P(("row", "col"), None)
    return jax.shard_map(
        local,
        mesh=mesh,
        in_specs=(blocks, blocks, blocks, P(), P(), P(), blocks),
        out_specs=(blocks, blocks, blocks),
        check_vma=False,
    )
```

```python
import jax
import jax.numpy as jnp
from jax import lax
from jax.experimental import pallas as pl
from jax.experimental.pallas import tpu as pltpu
from jax.sharding import PartitionSpec as P

BF16 = jnp.bfloat16
F32 = jnp.float32
GROUP = 8
MIB = 1024 * 1024
VMEM_BYTES = 28 * MIB

SAME_CORE = [[2 * chip + core for chip in range(8)] for core in range(2)]
OTHER_CORE = [(i, i ^ 1) for i in range(16)]


def dot_nn(a, b):
    return lax.dot_general(a, b, (((1,), (0,)), ((), ())), preferred_element_type=F32)


def dot_nt(a, b):
    return lax.dot_general(a, b, (((1,), (1,)), ((), ())), preferred_element_type=F32)


def dot_tn(a, b):
    return lax.dot_general(a, b, (((0,), (0,)), ((), ())), preferred_element_type=F32)


def exchange_dst(blocks):
    return lax.all_to_all(blocks, "row", 0, 0)


def exchange_src(blocks):
    return lax.all_to_all(blocks, "col", 0, 0, axis_index_groups=SAME_CORE)


def swap_cores(blocks):
    return lax.ppermute(blocks, "col", OTHER_CORE)


def to_chip(blocks, x_step, z_step):
    pairs = []
    for i in range(16):
        x, z, core = i // 4, i // 2 % 2, i % 2
        pairs.append((i, (x + x_step) % 4 * 4 + (z + z_step) % 2 * 2 + core))
    return lax.ppermute(blocks, "col", pairs)


def gather_src(block):
    pair = jnp.stack([block, to_chip(block, 0, 1)])
    pairs = [pair] + [to_chip(pair, dx, 0) for dx in range(1, 4)]
    return jnp.concatenate(pairs), jnp.concatenate([swap_cores(p) for p in pairs])


def array(*shape, dtype=BF16):
    return jax.ShapeDtypeStruct(shape, dtype)


def whole(a):
    return pl.BlockSpec(a.shape, lambda *_: (0,) * len(a.shape))


def by_step(a):
    return pl.BlockSpec((a.shape[0] // 2,) + a.shape[1:], lambda i, *_: (i,) + (0,) * (len(a.shape) - 1))


def call(kernel, steps, ins, outs, scratch=(), flops=0, exps=0, kinds=None, vmem=VMEM_BYTES):
    kinds = kinds or {}
    sizes = [a.size * a.dtype.itemsize for a in list(ins) + list(outs)]
    specs = [kinds.get(i, whole)(a) for i, a in enumerate(list(ins) + list(outs))]
    return pl.pallas_call(
        kernel,
        grid=(steps,),
        in_specs=specs[: len(ins)],
        out_specs=specs[len(ins) :],
        out_shape=outs,
        scratch_shapes=scratch,
        compiler_params=pltpu.CompilerParams(vmem_limit_bytes=vmem),
        cost_estimate=pl.CostEstimate(flops=flops, bytes_accessed=sum(sizes), transcendentals=exps),
    )(*ins)


def at_step(step):
    return pl.when(pl.program_id(0) == step)


def pick(own_ref, other_ref):
    return jnp.where(pl.program_id(0) == 0, own_ref[...], other_ref[...])


def put(own_ref, other_ref, block, value):
    @at_step(0)
    def _():
        own_ref[block] = value

    @at_step(1)
    def _():
        other_ref[block] = value


def accumulate(total, part):
    @at_step(0)
    def _():
        total[...] = part

    @at_step(1)
    def _():
        total[...] += part


def side_by_side(blocks):
    return jnp.concatenate([blocks[b] for b in range(GROUP)], axis=1)


def nodes(block):
    return slice(128 * block, 128 * block + 128)


def series_of(packed):
    return jnp.concatenate([packed[b, 0:128, :] for b in range(GROUP)], axis=0)


def src_of(packed):
    pieces = [packed[:, 128:160, 0:128], packed[:, 128:160, 128:256]]
    return side_by_side(jnp.concatenate(pieces, axis=1))


def mixing(weight):
    size, chan = 384, weight.shape[0]
    place = lax.broadcasted_iota(jnp.int32, (size, chan), 0) % chan
    repeat = jnp.where(place == lax.broadcasted_iota(jnp.int32, (size, chan), 1), 1.0, 0.0).astype(BF16)
    tiled = dot_nt(dot_nn(repeat, weight).astype(BF16), repeat)
    rows = lax.broadcasted_iota(jnp.int32, (size, size), 0) // chan
    cols = lax.broadcasted_iota(jnp.int32, (size, size), 1) // chan
    return jnp.where(rows == cols, tiled, 0.0).astype(BF16)


def source_kernel(src_ref, series_ref, src_out):
    src_out[0:128, :] = series_ref[...]
    src_out[128:160, 0:128] = src_ref[0:32, :]
    src_out[128:160, 128:256] = src_ref[32:64, :]
    src_out[128:160, 256:384] = jnp.zeros((32, 128), BF16)


def prepare_kernel(
    dst_ref, series_ref, self_ref, hop1_ref, hop2_ref, cotangent_ref, dst_out, first_out, base_out, mix1_out, mix2_out
):
    mix1, mix2 = mixing(hop1_ref[...]), mixing(hop2_ref[...])
    cotangent = cotangent_ref[...]
    second = dot_nt(mix2, cotangent).astype(BF16)
    for block in range(GROUP):
        dst_out[block, 0:384, :] = second
        dst_out[block, 384:448, :] = dst_ref[...]
    first_out[...] = dot_nt(mix1, cotangent)
    base_out[...] = dot_nn(series_ref[...], mixing(self_ref[...]))
    mix1_out[...] = mix1
    mix2_out[...] = mix2


def prepare(*ins):
    outs = [
        array(GROUP, 448, 128),
        array(384, 128, dtype=F32),
        array(128, 384, dtype=F32),
        array(384, 384),
        array(384, 384),
    ]
    return call(prepare_kernel, 1, ins, outs, flops=3 * 2 * 128 * 384 * 384, vmem=60 * MIB)


def stats_kernel(own_ref, other_ref, dst_ref, out_ref, state, dst):
    @at_step(0)
    def _():
        state[...] = jnp.zeros_like(state)
        dst[...] = side_by_side(dst_ref[:, 384:448, :])

    lifted = jnp.maximum(dot_tn(src_of(pick(own_ref, other_ref)), dst[...]), 0.0)
    old = state[0:1, :]
    new = jnp.maximum(old, jnp.max(lifted, axis=0, keepdims=True))
    total = jnp.sum(jnp.exp(lifted - new), axis=0, keepdims=True)
    state[1:2, :] = state[1:2, :] * jnp.exp(old - new) + total
    state[0:1, :] = new

    @at_step(1)
    def _():
        out_ref[...] = jnp.broadcast_to(state[...][None], out_ref.shape)


def softmax_stats(own, other, dst):
    rows = dst.shape[0] * 128
    scratch = [pltpu.VMEM((2, rows), F32), pltpu.VMEM((64, rows), BF16)]
    outs = [array(GROUP, 2, rows, dtype=F32)]
    size = 2 * rows * rows
    return call(stats_kernel, 2, (own, other, dst), outs, scratch, 128 * size, size)[0]


def weights_of(src, dst, norm_ref):
    scores = dot_tn(src, dst)
    weights = jnp.exp(jnp.maximum(scores, 0.0) - norm_ref[0:1, :]) * norm_ref[1:2, :]
    return scores, weights


def hops_kernel(
    own_ref, other_ref, dst_ref, stats_ref, norm_ref, hop_ref, own_out, other_out, total, dst, second
):
    @at_step(0)
    def _():
        peak = stats_ref[0, 0:1, :]
        for d in range(1, GROUP):
            peak = jnp.maximum(peak, stats_ref[d, 0:1, :])
        row_sum = jnp.zeros_like(peak)
        for d in range(GROUP):
            row_sum += stats_ref[d, 1:2, :] * jnp.exp(stats_ref[d, 0:1, :] - peak)
        norm_ref[0:1, :] = peak
        norm_ref[1:2, :] = 1.0 / row_sum
        second[...] = side_by_side(dst_ref[:, 0:384, :])
        dst[...] = side_by_side(dst_ref[:, 384:448, :])

    packed = pick(own_ref, other_ref)
    adjacency = weights_of(src_of(packed), dst[...], norm_ref)[1].astype(BF16)
    carried = dot_nt(second[...], adjacency).astype(BF16)
    for block in range(GROUP):
        put(own_out, other_out, block, carried[:, nodes(block)])
    accumulate(total, dot_tn(series_of(packed), adjacency))

    @at_step(1)
    def _():
        for block in range(GROUP):
            hop_ref[block] = total[:, nodes(block)].astype(BF16)


def first_hops(own, other, dst, stats):
    rows = dst.shape[0] * 128
    outs = [array(2, rows, dtype=F32)] + [array(GROUP, 384, 128)] * 3
    scratch = [pltpu.VMEM((384, rows), F32), pltpu.VMEM((64, rows), BF16), pltpu.VMEM((384, rows), BF16)]
    size = 2 * rows * rows
    return call(hops_kernel, 2, (own, other, dst, stats), outs, scratch, 2 * 832 * size, size)


def sum_of(pack_ref, start, stop):
    total = pack_ref[0, start:stop, :].astype(F32)
    for d in range(1, GROUP):
        total += pack_ref[d, start:stop, :].astype(F32)
    return total


def cores_kernel(own_ref, other_ref, *outs):
    for place, out in enumerate(outs):
        pair = slice(2 * place, 2 * place + 2)
        out[...] = (own_ref[pair].astype(F32) + other_ref[pair].astype(F32)).astype(BF16)


def join_kernel(hop_ref, a_ref, b_ref, c_ref, d_ref, hop_out, mine_out, other_out):
    def total(place):
        parts = [ref[place].astype(F32) for ref in (a_ref, b_ref, c_ref, d_ref)]
        return (parts[0] + parts[1]) + (parts[2] + parts[3])

    other_out[...] = total(1).astype(BF16)
    hop_out[...] = sum_of(hop_ref, 0, 384).T.astype(BF16)
    mine_out[...] = total(0)


def first_grad_kernel(mixed_ref, mine_ref, other_ref, out_ref):
    grad = (mixed_ref[...] + (mine_ref[...] + other_ref[...].astype(F32))).astype(BF16)
    for block in range(GROUP):
        out_ref[block] = grad


def three_terms(value):
    high = value.astype(BF16).astype(F32)
    middle = (value - high).astype(BF16).astype(F32)
    return [high, middle, value - high - middle]


SECOND, ABOVE, BELOW, INNER, SHIFT, LAST = 0, 384, 448, 512, 536, 544


def grad_kernel(
    own_ref, other_ref, hop_own_ref, hop_other_ref, dst_ref, norm_ref, first_ref,
    pack_ref, shift_ref, own_out, other_out, inner, mass, above, below, dst, grads, adj, wide, second,
):
    step = pl.program_id(0)
    half = step % 2

    @at_step(0)
    def _():
        dst[...] = side_by_side(dst_ref[:, 384:448, :])
        grads[0:384, :] = side_by_side(dst_ref[:, 0:384, :])
        grads[384:768, :] = side_by_side(first_ref)

    packed = jnp.where(half == 0, own_ref[...], other_ref[...])
    src = src_of(packed)

    @pl.when(step < 2)
    def _():
        scores, weights = weights_of(src, dst[...], norm_ref)
        hop = jnp.where(half == 0, hop_own_ref[...], hop_other_ref[...])
        adj_grad = dot_nn(jnp.concatenate([hop, series_of(packed)], axis=1), grads[...])
        adj[half] = adj_grad
        wide[half] = jnp.where(scores > 0.0, weights, 0.0)
        hop_part = dot_tn(hop, weights.astype(BF16))
        second[...] = jnp.where(step == 0, hop_part, second[...] + hop_part)
        total = jnp.sum(weights * adj_grad, axis=0, keepdims=True)
        weight = jnp.sum(weights, axis=0, keepdims=True)
        inner[...] = jnp.where(step == 0, total, inner[...] + total)
        mass[...] = jnp.where(step == 0, weight, mass[...] + weight)

    @pl.when(step >= 2)
    def _():
        shift = jnp.where(mass[...] > 1e-30, inner[...] / jnp.maximum(mass[...], 1e-30), 0.0)
        masked = wide[half]
        graded = (masked * (adj[half] - shift)).astype(BF16)
        masked = masked.astype(BF16)
        up, low = dot_nn(src, graded), dot_nn(src, masked)
        above[...] = jnp.where(step == 2, up, above[...] + up)
        below[...] = jnp.where(step == 2, low, below[...] + low)
        d_src = dot_nt(dst[...], graded)

        @pl.when(half == 0)
        def _():
            for block in range(GROUP):
                own_out[block] = d_src[:, nodes(block)]

        @pl.when(half == 1)
        def _():
            shift_ref[...] = shift
            for block in range(GROUP):
                other_out[block] = d_src[:, nodes(block)]
            sums = [term[:, nodes(block)] for term in three_terms(inner[...]) for block in range(GROUP)]
            sums = jnp.concatenate(sums, axis=0)
            shifts = jnp.concatenate(three_terms(shift), axis=0)
            for block in range(GROUP):
                tail = jnp.concatenate([sums, shifts[:, nodes(block)], jnp.zeros((5, 128), F32)], axis=0)
                pack_ref[block, SECOND:ABOVE, :] = second[:, nodes(block)].astype(BF16)
                pack_ref[block, ABOVE:BELOW, :] = above[:, nodes(block)].astype(BF16)
                pack_ref[block, BELOW:INNER, :] = below[:, nodes(block)].astype(BF16)
                pack_ref[block, INNER:LAST, :] = tail.astype(BF16)


def embed_grads(*ins):
    rows = ins[4].shape[0] * 128
    outs = [
        array(GROUP, LAST, 128),
        array(1, rows, dtype=F32),
        array(GROUP, 64, 128, dtype=F32),
        array(GROUP, 64, 128, dtype=F32),
    ]
    scratch = [
        pltpu.VMEM((1, rows), F32),
        pltpu.VMEM((1, rows), F32),
        pltpu.VMEM((64, rows), F32),
        pltpu.VMEM((64, rows), F32),
        pltpu.VMEM((64, rows), BF16),
        pltpu.VMEM((768, rows), BF16),
        pltpu.VMEM((2, rows, rows), F32),
        pltpu.VMEM((2, rows, rows), F32),
        pltpu.VMEM((384, rows), F32),
    ]

    size = 2 * rows * rows
    return call(
        grad_kernel, 4, ins, outs, scratch, 2 * 1408 * size, size, vmem=46 * MIB
    )


def inner_of(pack_ref):
    terms = sum_of(pack_ref, INNER, LAST)
    return terms[0:8] + (terms[8:16] + terms[16:24])


def src_kernel(
    own_ref, other_ref, dst_ref, norm_ref, pack_ref, shift_ref, own_part, other_part, own_out, other_out, scaled, dst
):
    @at_step(0)
    def _():
        dst[...] = side_by_side(dst_ref[:, 384:448, :])
        inner = inner_of(pack_ref)
        for block in range(GROUP):
            change = shift_ref[:, nodes(block)] - inner[block : block + 1, :]
            scaled[:, nodes(block)] = (dst[:, nodes(block)].astype(F32) * change).astype(BF16)

    scores, weights = weights_of(src_of(pick(own_ref, other_ref)), dst[...], norm_ref)
    part = dot_nt(scaled[...], jnp.where(scores > 0.0, weights, 0.0).astype(BF16))

    me = lax.axis_index("col")
    for block in range(GROUP):
        place = (me // 4 + 4 - block // 2) % 4 * 2 + (me // 2 + block) % 2

        @at_step(0)
        def _(block=block, place=place):
            own_out[place] = own_part[block] + part[:, nodes(block)]

        @at_step(1)
        def _(block=block, place=place):
            other_out[place] = other_part[block] + part[:, nodes(block)]


def src_grads(*ins):
    rows = ins[2].shape[0] * 128
    outs = [array(GROUP, 64, 128, dtype=F32), array(GROUP, 64, 128, dtype=F32)]
    scratch = [pltpu.VMEM((64, rows), BF16), pltpu.VMEM((64, rows), BF16)]
    size = 2 * rows * rows
    return call(src_kernel, 2, ins, outs, scratch, 256 * size, size)


def output_kernel(pack_ref, hop_ref, base_ref, mix1_ref, mix2_ref, out_ref, d_dst_ref):
    second = sum_of(pack_ref, SECOND, ABOVE).T.astype(BF16)
    mixed = base_ref[...] + dot_nn(hop_ref[...], mix1_ref[...]) + dot_nn(second, mix2_ref[...])
    out_ref[...] = mixed.astype(BF16)
    me = lax.axis_index("row")
    inner = inner_of(pack_ref)
    places = lax.broadcasted_iota(jnp.int32, inner.shape, 0)
    inner = jnp.sum(jnp.where(places == me, inner, 0.0), axis=0, keepdims=True)
    d_dst = jnp.zeros((64, 128), F32)
    for d in range(GROUP):
        tail = pack_ref[d, INNER:LAST, :].astype(F32)
        shift = tail[24:25] + (tail[25:26] + tail[26:27])
        above, below = pack_ref[d, ABOVE:BELOW, :].astype(F32), pack_ref[d, BELOW:INNER, :].astype(F32)
        d_dst += above + (shift - inner) * below
    d_dst_ref[...] = d_dst


def local(dst_embed, src_embed, series, w_self, w_hop1, w_hop2, cotangent):
    src = call(source_kernel, 1, (src_embed.T, series), [array(160, 384)], vmem=60 * MIB)[0]
    src_own, src_other = gather_src(src)
    dst, first_mixed, base, mix1, mix2 = prepare(dst_embed.T, series, w_self, w_hop1, w_hop2, cotangent)
    dst = exchange_dst(dst)
    stats = exchange_dst(softmax_stats(src_own, src_other, dst))

    norm, hop, own, other = first_hops(src_own, src_other, dst, stats)
    hop = exchange_dst(hop)
    pairs = call(cores_kernel, 1, (own, swap_cores(other)), [array(2, 384, 128)] * 4)
    pairs = [pairs[0]] + [to_chip(pairs[dx], -dx, 0) for dx in range(1, 4)]
    hop, mine, rest = call(
        join_kernel, 1, (hop, *pairs), [array(128, 384), array(384, 128, dtype=F32), array(384, 128)]
    )
    rest = to_chip(rest, 0, 1)
    first = call(first_grad_kernel, 1, (first_mixed, mine, rest), [array(GROUP, 384, 128)])[0]
    first = exchange_dst(first)
    hop_own, hop_other = (half.reshape(-1, 384) for half in gather_src(hop))

    pack, shift, own, other = embed_grads(src_own, src_other, hop_own, hop_other, dst, norm, first)
    pack = exchange_dst(pack)
    own, other = src_grads(src_own, src_other, dst, norm, pack, shift, own, other)
    output, d_dst = call(
        output_kernel, 1, (pack, hop, base, mix1, mix2), [array(128, 384), array(64, 128, dtype=F32)],
        flops=4 * 128 * 384 * 384,
    )
    d_src = jnp.sum(exchange_src(own + swap_cores(other)), axis=0)
    return output, d_dst.T, d_src.T


def solution(mesh):
    blocks = P(("row", "col"), None)
    return jax.shard_map(
        local,
        mesh=mesh,
        in_specs=(blocks, blocks, blocks, P(), P(), P(), blocks),
        out_specs=(blocks, blocks, blocks),
        check_vma=False,
    )
```

```python
import jax
import jax.numpy as jnp
from jax import lax
from jax.experimental import pallas as pl
from jax.experimental.pallas import tpu as pltpu
from jax.sharding import PartitionSpec as P

BF16 = jnp.bfloat16
F32 = jnp.float32
GROUP = 8
MIB = 1024 * 1024
VMEM_BYTES = 28 * MIB

SAME_CORE = [[2 * chip + core for chip in range(8)] for core in range(2)]
OTHER_CORE = [(i, i ^ 1) for i in range(16)]


def dot_nn(a, b):
    return lax.dot_general(a, b, (((1,), (0,)), ((), ())), preferred_element_type=F32)


def dot_nt(a, b):
    return lax.dot_general(a, b, (((1,), (1,)), ((), ())), preferred_element_type=F32)


def dot_tn(a, b):
    return lax.dot_general(a, b, (((0,), (0,)), ((), ())), preferred_element_type=F32)


def exchange_dst(blocks):
    return lax.all_to_all(blocks, "row", 0, 0)


def exchange_src(blocks):
    return lax.all_to_all(blocks, "col", 0, 0, axis_index_groups=SAME_CORE)


def swap_cores(blocks):
    return lax.ppermute(blocks, "col", OTHER_CORE)


def to_chip(blocks, x_step, z_step):
    pairs = []
    for i in range(16):
        x, z, core = i // 4, i // 2 % 2, i % 2
        pairs.append((i, (x + x_step) % 4 * 4 + (z + z_step) % 2 * 2 + core))
    return lax.ppermute(blocks, "col", pairs)


def to_row(blocks, y_step, z_step):
    pairs = [(i, (i // 4 + z_step) % 2 * 4 + (i + y_step) % 4) for i in range(8)]
    return lax.ppermute(blocks, "row", pairs)


def gather_src(block):
    pair = jnp.stack([block, to_chip(block, 0, 1)])
    pairs = [pair] + [to_chip(pair, dx, 0) for dx in range(1, 4)]
    return pairs, [swap_cores(p) for p in pairs]


def array(*shape, dtype=BF16):
    return jax.ShapeDtypeStruct(shape, dtype)


def whole(a):
    return pl.BlockSpec(a.shape, lambda *_: (0,) * len(a.shape))


def by_step(a):
    return pl.BlockSpec((a.shape[0] // 2,) + a.shape[1:], lambda i, *_: (i,) + (0,) * (len(a.shape) - 1))


def call(kernel, steps, ins, outs, scratch=(), flops=0, exps=0, kinds=None, vmem=VMEM_BYTES):
    kinds = kinds or {}
    sizes = [a.size * a.dtype.itemsize for a in list(ins) + list(outs)]
    specs = [kinds.get(i, whole)(a) for i, a in enumerate(list(ins) + list(outs))]
    return pl.pallas_call(
        kernel,
        grid=(steps,),
        in_specs=specs[: len(ins)],
        out_specs=specs[len(ins) :],
        out_shape=outs,
        scratch_shapes=scratch,
        compiler_params=pltpu.CompilerParams(vmem_limit_bytes=vmem),
        cost_estimate=pl.CostEstimate(flops=flops, bytes_accessed=sum(sizes), transcendentals=exps),
    )(*ins)


def at_step(step):
    return pl.when(pl.program_id(0) == step)


def pick(own_ref, other_ref):
    return jnp.where(pl.program_id(0) == 0, own_ref[...], other_ref[...])


def put(own_ref, other_ref, block, value):
    @at_step(0)
    def _():
        own_ref[block] = value

    @at_step(1)
    def _():
        other_ref[block] = value


def accumulate(total, part):
    @at_step(0)
    def _():
        total[...] = part

    @at_step(1)
    def _():
        total[...] += part


def side_by_side(blocks):
    return jnp.concatenate([blocks[b] for b in range(GROUP)], axis=1)


def nodes(block):
    return slice(128 * block, 128 * block + 128)


def series_of(packed):
    return jnp.concatenate([packed[b, 0:128, :] for b in range(GROUP)], axis=0)


def src_of(packed):
    pieces = [packed[:, 128:160, 0:128], packed[:, 128:160, 128:256]]
    return side_by_side(jnp.concatenate(pieces, axis=1))


def mixing(weight):
    size, chan = 384, weight.shape[0]
    place = lax.broadcasted_iota(jnp.int32, (size, chan), 0) % chan
    repeat = jnp.where(place == lax.broadcasted_iota(jnp.int32, (size, chan), 1), 1.0, 0.0).astype(BF16)
    tiled = dot_nt(dot_nn(repeat, weight).astype(BF16), repeat)
    rows = lax.broadcasted_iota(jnp.int32, (size, size), 0) // chan
    cols = lax.broadcasted_iota(jnp.int32, (size, size), 1) // chan
    return jnp.where(rows == cols, tiled, 0.0).astype(BF16)


def source_kernel(src_ref, series_ref, src_out):
    src_out[0:128, :] = series_ref[...]
    src_out[128:160, 0:128] = src_ref[0:32, :]
    src_out[128:160, 128:256] = src_ref[32:64, :]
    src_out[128:160, 256:384] = jnp.zeros((32, 128), BF16)


def second_grad_kernel(dst_ref, hop2_ref, cotangent_ref, dst_out, mix2_out):
    mix2 = mixing(hop2_ref[...])
    second = dot_nt(mix2, cotangent_ref[...]).astype(BF16)
    for block in range(GROUP):
        dst_out[block, 0:384, :] = second
        dst_out[block, 384:448, :] = dst_ref[...]
    mix2_out[...] = mix2


def mixed_kernel(series_ref, self_ref, hop1_ref, cotangent_ref, first_out, base_out, mix1_out):
    mix1 = mixing(hop1_ref[...])
    first_out[...] = dot_nt(mix1, cotangent_ref[...])
    base_out[...] = dot_nn(series_ref[...], mixing(self_ref[...]))
    mix1_out[...] = mix1


def stats_kernel(own_ref, other_ref, dst_ref, out_ref, state, dst):
    @at_step(0)
    def _():
        state[...] = jnp.zeros_like(state)
        dst[...] = side_by_side(dst_ref[:, 384:448, :])

    lifted = jnp.maximum(dot_tn(src_of(pick(own_ref, other_ref)), dst[...]), 0.0)
    old = state[0:1, :]
    new = jnp.maximum(old, jnp.max(lifted, axis=0, keepdims=True))
    total = jnp.sum(jnp.exp(lifted - new), axis=0, keepdims=True)
    state[1:2, :] = state[1:2, :] * jnp.exp(old - new) + total
    state[0:1, :] = new

    @at_step(1)
    def _():
        out_ref[...] = jnp.broadcast_to(state[...][None], out_ref.shape)


def softmax_stats(own, other, dst):
    rows = dst.shape[0] * 128
    scratch = [pltpu.VMEM((2, rows), F32), pltpu.VMEM((64, rows), BF16)]
    outs = [array(GROUP, 2, rows, dtype=F32)]
    size = 2 * rows * rows
    return call(stats_kernel, 2, (own, other, dst), outs, scratch, 128 * size, size)[0]


def weights_of(src, dst, norm_ref):
    scores = dot_tn(src, dst)
    weights = jnp.exp(jnp.maximum(scores, 0.0) - norm_ref[0:1, :]) * norm_ref[1:2, :]
    return scores, weights


def hops_kernel(
    own_ref, other_ref, dst_ref, stats_ref, norm_ref, hop_ref, own_out, other_out, total, dst, second
):
    @at_step(0)
    def _():
        peak = stats_ref[0, 0:1, :]
        for d in range(1, GROUP):
            peak = jnp.maximum(peak, stats_ref[d, 0:1, :])
        row_sum = jnp.zeros_like(peak)
        for d in range(GROUP):
            row_sum += stats_ref[d, 1:2, :] * jnp.exp(stats_ref[d, 0:1, :] - peak)
        norm_ref[0:1, :] = peak
        norm_ref[1:2, :] = 1.0 / row_sum
        second[...] = side_by_side(dst_ref[:, 0:384, :])
        dst[...] = side_by_side(dst_ref[:, 384:448, :])

    packed = pick(own_ref, other_ref)
    adjacency = weights_of(src_of(packed), dst[...], norm_ref)[1].astype(BF16)
    carried = dot_nt(second[...], adjacency).astype(BF16)
    for block in range(GROUP):
        put(own_out, other_out, block, carried[:, nodes(block)])
    accumulate(total, dot_tn(series_of(packed), adjacency))

    @at_step(1)
    def _():
        for block in range(GROUP):
            hop_ref[block] = total[:, nodes(block)].astype(BF16)


def first_hops(own, other, dst, stats):
    rows = dst.shape[0] * 128
    outs = [array(2, rows, dtype=F32)] + [array(GROUP, 384, 128)] * 3
    scratch = [pltpu.VMEM((384, rows), F32), pltpu.VMEM((64, rows), BF16), pltpu.VMEM((384, rows), BF16)]
    size = 2 * rows * rows
    return call(hops_kernel, 2, (own, other, dst, stats), outs, scratch, 2 * 832 * size, size)


def sum_of(pack_ref, start, stop):
    total = pack_ref[0, start:stop, :].astype(F32)
    for d in range(1, GROUP):
        total += pack_ref[d, start:stop, :].astype(F32)
    return total


def cores_kernel(own_ref, other_ref, *outs):
    for place, out in enumerate(outs):
        pair = slice(2 * place, 2 * place + 2)
        out[...] = (own_ref[pair].astype(F32) + other_ref[pair].astype(F32)).astype(BF16)


def totals(place, *refs):
    parts = [ref[place].astype(F32) for ref in refs]
    return (parts[0] + parts[1]) + (parts[2] + parts[3])


def join_kernel(hop_ref, a_ref, b_ref, c_ref, d_ref, hop_out, mine_out, other_out):
    other_out[...] = totals(1, a_ref, b_ref, c_ref, d_ref).astype(BF16)
    hop_out[...] = sum_of(hop_ref, 0, 384).T.astype(BF16)
    mine_out[...] = totals(0, a_ref, b_ref, c_ref, d_ref)


def first_grad_kernel(mixed_ref, mine_ref, other_ref, out_ref):
    grad = (mixed_ref[...] + (mine_ref[...] + other_ref[...].astype(F32))).astype(BF16)
    for block in range(GROUP):
        out_ref[block] = grad


def three_terms(value):
    high = value.astype(BF16).astype(F32)
    middle = (value - high).astype(BF16).astype(F32)
    return [high, middle, value - high - middle]


ABOVE, BELOW, INNER, LAST = 0, 64, 128, 160


def grad_kernel(own_ref, other_ref, *refs):
    hop_own, hop_other, (dst_ref, norm_ref, first_ref) = refs[0:4], refs[4:8], refs[8:11]
    (pack_ref, shift_ref, own_out, other_out), second_out = refs[11:15], refs[15:19]
    inner, mass, above, below, dst, grads, adj, wide, second = refs[19:]
    step = pl.program_id(0)
    half = step % 2

    @at_step(0)
    def _():
        dst[...] = side_by_side(dst_ref[:, 384:448, :])
        grads[0:384, :] = side_by_side(dst_ref[:, 0:384, :])
        grads[384:768, :] = side_by_side(first_ref)

    packed = jnp.where(half == 0, own_ref[...], other_ref[...])
    src = src_of(packed)

    @pl.when(step < 2)
    def _():
        scores, weights = weights_of(src, dst[...], norm_ref)
        pieces = [jnp.where(half == 0, a[...], b[...]) for a, b in zip(hop_own, hop_other)]
        hop = jnp.concatenate(pieces).reshape(GROUP * 128, 384)
        adj_grad = dot_nn(jnp.concatenate([hop, series_of(packed)], axis=1), grads[...])
        adj[half] = adj_grad
        wide[half] = jnp.where(scores > 0.0, weights, 0.0)
        hop_part = dot_tn(hop, weights.astype(BF16))
        second[...] = jnp.where(step == 0, hop_part, second[...] + hop_part)
        total = jnp.sum(weights * adj_grad, axis=0, keepdims=True)
        weight = jnp.sum(weights, axis=0, keepdims=True)
        inner[...] = jnp.where(step == 0, total, inner[...] + total)
        mass[...] = jnp.where(step == 0, weight, mass[...] + weight)

    @pl.when(step >= 2)
    def _():
        shift = jnp.where(mass[...] > 1e-30, inner[...] / jnp.maximum(mass[...], 1e-30), 0.0)
        masked = wide[half]
        graded = (masked * (adj[half] - shift)).astype(BF16)
        masked = masked.astype(BF16)
        up, low = dot_nn(src, graded), dot_nn(src, masked)
        above[...] = jnp.where(step == 2, up, above[...] + up)
        below[...] = jnp.where(step == 2, low, below[...] + low)
        d_src = dot_nt(dst[...], graded)

        @pl.when(half == 0)
        def _():
            for block in range(GROUP):
                own_out[block] = d_src[:, nodes(block)]

        @pl.when(half == 1)
        def _():
            shift_ref[...] = shift
            for block in range(GROUP):
                other_out[block] = d_src[:, nodes(block)]
            sums = [term[:, nodes(block)] for term in three_terms(inner[...]) for block in range(GROUP)]
            sums = jnp.concatenate(sums, axis=0)
            shifts = jnp.concatenate(three_terms(shift), axis=0)
            for block in range(GROUP):
                tail = jnp.concatenate([sums, shifts[:, nodes(block)], jnp.zeros((5, 128), F32)], axis=0)
                pack_ref[block, ABOVE:BELOW, :] = above[:, nodes(block)].astype(BF16)
                pack_ref[block, BELOW:INNER, :] = below[:, nodes(block)].astype(BF16)
                pack_ref[block, INNER:LAST, :] = tail.astype(BF16)
            me = lax.axis_index("row")
            for block in range(GROUP):
                owner = (me // 4 + block) % 2 * 4 + (me + block // 2) % 4
                part = second[:, pl.ds(pl.multiple_of(owner * 128, 128), 128)]
                second_out[block // 2][block % 2] = part.astype(BF16)


def embed_grads(*ins):
    rows = GROUP * 128
    outs = [
        array(GROUP, LAST, 128),
        array(1, rows, dtype=F32),
        array(GROUP, 64, 128, dtype=F32),
        array(GROUP, 64, 128, dtype=F32),
    ] + [array(2, 384, 128)] * 4
    scratch = [
        pltpu.VMEM((1, rows), F32),
        pltpu.VMEM((1, rows), F32),
        pltpu.VMEM((64, rows), F32),
        pltpu.VMEM((64, rows), F32),
        pltpu.VMEM((64, rows), BF16),
        pltpu.VMEM((768, rows), BF16),
        pltpu.VMEM((2, rows, rows), F32),
        pltpu.VMEM((2, rows, rows), F32),
        pltpu.VMEM((384, rows), F32),
    ]

    size = 2 * rows * rows
    return call(
        grad_kernel, 4, ins, outs, scratch, 2 * 1408 * size, size, vmem=60 * MIB
    )


def inner_of(pack_ref):
    terms = sum_of(pack_ref, INNER, LAST)
    return terms[0:8] + (terms[8:16] + terms[16:24])


def src_kernel(
    own_ref, other_ref, dst_ref, norm_ref, pack_ref, shift_ref, own_part, other_part, a_ref, b_ref, c_ref, d_ref,
    own_out, other_out, mine_out, rest_out, scaled, dst,
):
    @at_step(0)
    def _():
        rest_out[...] = totals(1, a_ref, b_ref, c_ref, d_ref).astype(BF16)
        mine_out[...] = totals(0, a_ref, b_ref, c_ref, d_ref)
        dst[...] = side_by_side(dst_ref[:, 384:448, :])
        inner = inner_of(pack_ref)
        for block in range(GROUP):
            change = shift_ref[:, nodes(block)] - inner[block : block + 1, :]
            scaled[:, nodes(block)] = (dst[:, nodes(block)].astype(F32) * change).astype(BF16)

    scores, weights = weights_of(src_of(pick(own_ref, other_ref)), dst[...], norm_ref)
    part = dot_nt(scaled[...], jnp.where(scores > 0.0, weights, 0.0).astype(BF16))

    me = lax.axis_index("col")
    for block in range(GROUP):
        place = (me // 4 + 4 - block // 2) % 4 * 2 + (me // 2 + block) % 2

        @at_step(0)
        def _(block=block, place=place):
            own_out[place] = own_part[block] + part[:, nodes(block)]

        @at_step(1)
        def _(block=block, place=place):
            other_out[place] = other_part[block] + part[:, nodes(block)]


def src_grads(*ins):
    rows = ins[2].shape[0] * 128
    outs = [
        array(GROUP, 64, 128, dtype=F32),
        array(GROUP, 64, 128, dtype=F32),
        array(384, 128, dtype=F32),
        array(384, 128),
    ]
    scratch = [pltpu.VMEM((64, rows), BF16), pltpu.VMEM((64, rows), BF16)]
    size = 2 * rows * rows
    return call(src_kernel, 2, ins, outs, scratch, 256 * size, size, vmem=60 * MIB)


def output_kernel(pack_ref, mine_ref, rest_ref, hop_ref, base_ref, mix1_ref, mix2_ref, out_ref, d_dst_ref):
    second = (mine_ref[...] + rest_ref[...].astype(F32)).T.astype(BF16)
    mixed = base_ref[...] + dot_nn(hop_ref[...], mix1_ref[...]) + dot_nn(second, mix2_ref[...])
    out_ref[...] = mixed.astype(BF16)
    me = lax.axis_index("row")
    inner = inner_of(pack_ref)
    places = lax.broadcasted_iota(jnp.int32, inner.shape, 0)
    inner = jnp.sum(jnp.where(places == me, inner, 0.0), axis=0, keepdims=True)
    d_dst = jnp.zeros((64, 128), F32)
    for d in range(GROUP):
        tail = pack_ref[d, INNER:LAST, :].astype(F32)
        shift = tail[24:25] + (tail[25:26] + tail[26:27])
        above, below = pack_ref[d, ABOVE:BELOW, :].astype(F32), pack_ref[d, BELOW:INNER, :].astype(F32)
        d_dst += above + (shift - inner) * below
    d_dst_ref[...] = d_dst


def local(dst_embed, src_embed, series, w_self, w_hop1, w_hop2, cotangent):
    src = call(source_kernel, 1, (src_embed.T, series), [array(160, 384)], vmem=60 * MIB)[0]
    src_own, src_other = (jnp.concatenate(pairs) for pairs in gather_src(src))
    dst, mix2 = call(
        second_grad_kernel, 1, (dst_embed.T, w_hop2, cotangent), [array(GROUP, 448, 128), array(384, 384)], vmem=60 * MIB
    )
    first_mixed, base, mix1 = call(
        mixed_kernel, 1, (series, w_self, w_hop1, cotangent),
        [array(384, 128, dtype=F32), array(128, 384, dtype=F32), array(384, 384)],
    )
    dst = exchange_dst(dst)
    stats = exchange_dst(softmax_stats(src_own, src_other, dst))

    norm, hop, own, other = first_hops(src_own, src_other, dst, stats)
    hop = exchange_dst(hop)
    pairs = call(cores_kernel, 1, (own, swap_cores(other)), [array(2, 384, 128)] * 4)
    pairs = [pairs[0]] + [to_chip(pairs[dx], -dx, 0) for dx in range(1, 4)]
    hop, mine, rest = call(
        join_kernel, 1, (hop, *pairs), [array(128, 384), array(384, 128, dtype=F32), array(384, 128)]
    )
    rest = to_chip(rest, 0, 1)
    first = call(first_grad_kernel, 1, (first_mixed, mine, rest), [array(GROUP, 384, 128)])[0]
    first = exchange_dst(first)
    hop_own, hop_other = gather_src(hop)

    pack, shift, own, other, *pairs = embed_grads(src_own, src_other, *hop_own, *hop_other, dst, norm, first)
    pack = exchange_dst(pack)
    pairs = [pairs[0]] + [to_row(pairs[dy], dy, 0) for dy in range(1, 4)]
    own, other, mine, rest = src_grads(src_own, src_other, dst, norm, pack, shift, own, other, *pairs)
    rest = to_row(rest, 0, 1)
    output, d_dst = call(
        output_kernel, 1, (pack, mine, rest, hop, base, mix1, mix2), [array(128, 384), array(64, 128, dtype=F32)],
        flops=4 * 128 * 384 * 384,
    )
    d_src = jnp.sum(exchange_src(own + swap_cores(other)), axis=0)
    return output, d_dst.T, d_src.T


def solution(mesh):
    blocks = P(("row", "col"), None)
    return jax.shard_map(
        local,
        mesh=mesh,
        in_specs=(blocks, blocks, blocks, P(), P(), P(), blocks),
        out_specs=(blocks, blocks, blocks),
        check_vma=False,
    )
```

```python
import jax
import jax.numpy as jnp
from jax import lax
from jax.experimental import pallas as pl
from jax.experimental.pallas import tpu as pltpu
from jax.sharding import PartitionSpec as P

BF16 = jnp.bfloat16
F32 = jnp.float32
GROUP = 8
MIB = 1024 * 1024
VMEM_BYTES = 28 * MIB

SAME_CORE = [[2 * chip + core for chip in range(8)] for core in range(2)]
OTHER_CORE = [(i, i ^ 1) for i in range(16)]


def dot_nn(a, b):
    return lax.dot_general(a, b, (((1,), (0,)), ((), ())), preferred_element_type=F32)


def dot_nt(a, b):
    return lax.dot_general(a, b, (((1,), (1,)), ((), ())), preferred_element_type=F32)


def dot_tn(a, b):
    return lax.dot_general(a, b, (((0,), (0,)), ((), ())), preferred_element_type=F32)


def exchange_dst(blocks):
    return lax.all_to_all(blocks, "row", 0, 0)


def exchange_src(blocks):
    return lax.all_to_all(blocks, "col", 0, 0, axis_index_groups=SAME_CORE)


def swap_cores(blocks):
    return lax.ppermute(blocks, "col", OTHER_CORE)


def to_chip(blocks, x_step, z_step):
    pairs = []
    for i in range(16):
        x, z, core = i // 4, i // 2 % 2, i % 2
        pairs.append((i, (x + x_step) % 4 * 4 + (z + z_step) % 2 * 2 + core))
    return lax.ppermute(blocks, "col", pairs)


def gather_src(pair):
    pairs = [pair] + [to_chip(pair, dx, 0) for dx in range(1, 4)]
    return pairs, [swap_cores(p) for p in pairs]


def array(*shape, dtype=BF16):
    return jax.ShapeDtypeStruct(shape, dtype)


def whole(a):
    return pl.BlockSpec(a.shape, lambda *_: (0,) * len(a.shape))


def by_step(a):
    return pl.BlockSpec((a.shape[0] // 2,) + a.shape[1:], lambda i, *_: (i,) + (0,) * (len(a.shape) - 1))


def call(kernel, steps, ins, outs, scratch=(), flops=0, exps=0, kinds=None, vmem=VMEM_BYTES):
    kinds = kinds or {}
    sizes = [a.size * a.dtype.itemsize for a in list(ins) + list(outs)]
    specs = [kinds.get(i, whole)(a) for i, a in enumerate(list(ins) + list(outs))]
    return pl.pallas_call(
        kernel,
        grid=(steps,),
        in_specs=specs[: len(ins)],
        out_specs=specs[len(ins) :],
        out_shape=outs,
        scratch_shapes=scratch,
        compiler_params=pltpu.CompilerParams(vmem_limit_bytes=vmem),
        cost_estimate=pl.CostEstimate(flops=flops, bytes_accessed=sum(sizes), transcendentals=exps),
    )(*ins)


def at_step(step):
    return pl.when(pl.program_id(0) == step)


def pick(own_ref, other_ref):
    return jnp.where(pl.program_id(0) == 0, own_ref[...], other_ref[...])


def put(own_ref, other_ref, block, value):
    @at_step(0)
    def _():
        own_ref[block] = value

    @at_step(1)
    def _():
        other_ref[block] = value


def accumulate(total, part):
    @at_step(0)
    def _():
        total[...] = part

    @at_step(1)
    def _():
        total[...] += part


def side_by_side(blocks):
    return jnp.concatenate([blocks[b] for b in range(GROUP)], axis=1)


def nodes(block):
    return slice(128 * block, 128 * block + 128)


def series_of(packed):
    return jnp.concatenate([packed[b, 0:128, :] for b in range(GROUP)], axis=0)


def src_of(packed):
    pieces = [packed[:, 128:160, 0:128], packed[:, 128:160, 128:256]]
    return side_by_side(jnp.concatenate(pieces, axis=1))


def mixing(weight):
    size, chan = 384, weight.shape[0]
    place = lax.broadcasted_iota(jnp.int32, (size, chan), 0) % chan
    repeat = jnp.where(place == lax.broadcasted_iota(jnp.int32, (size, chan), 1), 1.0, 0.0).astype(BF16)
    tiled = dot_nt(dot_nn(repeat, weight).astype(BF16), repeat)
    rows = lax.broadcasted_iota(jnp.int32, (size, size), 0) // chan
    cols = lax.broadcasted_iota(jnp.int32, (size, size), 1) // chan
    return jnp.where(rows == cols, tiled, 0.0).astype(BF16)


def source_kernel(src_ref, series_ref, src_out):
    src_out[0:128, :] = series_ref[...]
    src_out[128:160, 0:128] = src_ref[0:32, :]
    src_out[128:160, 128:256] = src_ref[32:64, :]
    src_out[128:160, 256:384] = jnp.zeros((32, 128), BF16)


def prepare_kernel(
    dst_ref, series_ref, self_ref, hop1_ref, hop2_ref, cotangent_ref, dst_out, first_out, base_out, mix1_out, mix2_out
):
    mix1, mix2 = mixing(hop1_ref[...]), mixing(hop2_ref[...])
    cotangent = cotangent_ref[...]
    second = dot_nt(mix2, cotangent).astype(BF16)
    for block in range(GROUP):
        dst_out[block, 0:384, :] = second
        dst_out[block, 384:448, :] = dst_ref[...]
    first_out[...] = dot_nt(mix1, cotangent)
    base_out[...] = dot_nn(series_ref[...], mixing(self_ref[...]))
    mix1_out[...] = mix1
    mix2_out[...] = mix2


def prepare(*ins):
    outs = [
        array(GROUP, 448, 128),
        array(384, 128, dtype=F32),
        array(128, 384, dtype=F32),
        array(384, 384),
        array(384, 384),
    ]
    return call(prepare_kernel, 1, ins, outs, flops=3 * 2 * 128 * 384 * 384, vmem=60 * MIB)


def stats_kernel(own_ref, other_ref, dst_ref, out_ref, state, dst):
    @at_step(0)
    def _():
        state[...] = jnp.zeros_like(state)
        dst[...] = side_by_side(dst_ref[:, 384:448, :])

    lifted = jnp.maximum(dot_tn(src_of(pick(own_ref, other_ref)), dst[...]), 0.0)
    old = state[0:1, :]
    new = jnp.maximum(old, jnp.max(lifted, axis=0, keepdims=True))
    total = jnp.sum(jnp.exp(lifted - new), axis=0, keepdims=True)
    state[1:2, :] = state[1:2, :] * jnp.exp(old - new) + total
    state[0:1, :] = new

    @at_step(1)
    def _():
        out_ref[...] = jnp.broadcast_to(state[...][None], out_ref.shape)


def softmax_stats(own, other, dst):
    rows = dst.shape[0] * 128
    scratch = [pltpu.VMEM((2, rows), F32), pltpu.VMEM((64, rows), BF16)]
    outs = [array(GROUP, 2, rows, dtype=F32)]
    size = 2 * rows * rows
    return call(stats_kernel, 2, (own, other, dst), outs, scratch, 128 * size, size)[0]


def weights_of(src, dst, norm_ref):
    scores = dot_tn(src, dst)
    weights = jnp.exp(jnp.maximum(scores, 0.0) - norm_ref[0:1, :]) * norm_ref[1:2, :]
    return scores, weights


def hops_kernel(
    own_ref, other_ref, dst_ref, stats_ref, norm_ref, hop_ref, own_out, other_out, total, dst, second
):
    @at_step(0)
    def _():
        peak = stats_ref[0, 0:1, :]
        for d in range(1, GROUP):
            peak = jnp.maximum(peak, stats_ref[d, 0:1, :])
        row_sum = jnp.zeros_like(peak)
        for d in range(GROUP):
            row_sum += stats_ref[d, 1:2, :] * jnp.exp(stats_ref[d, 0:1, :] - peak)
        norm_ref[0:1, :] = peak
        norm_ref[1:2, :] = 1.0 / row_sum
        second[...] = side_by_side(dst_ref[:, 0:384, :])
        dst[...] = side_by_side(dst_ref[:, 384:448, :])

    packed = pick(own_ref, other_ref)
    adjacency = weights_of(src_of(packed), dst[...], norm_ref)[1].astype(BF16)
    carried = dot_nt(second[...], adjacency).astype(BF16)
    for block in range(GROUP):
        put(own_out, other_out, block, carried[:, nodes(block)])
    accumulate(total, dot_tn(series_of(packed), adjacency))

    @at_step(1)
    def _():
        for block in range(GROUP):
            hop_ref[block] = total[:, nodes(block)].astype(BF16)


def first_hops(own, other, dst, stats):
    rows = dst.shape[0] * 128
    outs = [array(2, rows, dtype=F32)] + [array(GROUP, 384, 128)] * 3
    scratch = [pltpu.VMEM((384, rows), F32), pltpu.VMEM((64, rows), BF16), pltpu.VMEM((384, rows), BF16)]
    size = 2 * rows * rows
    return call(hops_kernel, 2, (own, other, dst, stats), outs, scratch, 2 * 832 * size, size)


def sum_of(pack_ref, start, stop):
    total = pack_ref[0, start:stop, :].astype(F32)
    for d in range(1, GROUP):
        total += pack_ref[d, start:stop, :].astype(F32)
    return total


def cores_kernel(own_ref, other_ref, *outs):
    for place, out in enumerate(outs):
        pair = slice(2 * place, 2 * place + 2)
        out[...] = (own_ref[pair].astype(F32) + other_ref[pair].astype(F32)).astype(BF16)


def join_kernel(hop_ref, a_ref, b_ref, c_ref, d_ref, hop_out, mine_out, other_out):
    def total(place):
        parts = [ref[place].astype(F32) for ref in (a_ref, b_ref, c_ref, d_ref)]
        return (parts[0] + parts[1]) + (parts[2] + parts[3])

    other_out[...] = total(1).astype(BF16)
    hop_out[...] = sum_of(hop_ref, 0, 384).T.astype(BF16)
    mine_out[...] = total(0)


def first_grad_kernel(mixed_ref, mine_ref, other_ref, hop_ref, next_ref, out_ref, pair_ref):
    pair_ref[0] = hop_ref[...]
    pair_ref[1] = next_ref[...]
    grad = (mixed_ref[...] + (mine_ref[...] + other_ref[...].astype(F32))).astype(BF16)
    for block in range(GROUP):
        out_ref[block] = grad


def three_terms(value):
    high = value.astype(BF16).astype(F32)
    middle = (value - high).astype(BF16).astype(F32)
    return [high, middle, value - high - middle]


SECOND, ABOVE, BELOW, INNER, SHIFT, LAST = 0, 384, 448, 512, 536, 544


def grad_kernel(own_ref, other_ref, *refs):
    hop_own, hop_other, (dst_ref, norm_ref, first_ref) = refs[0:4], refs[4:8], refs[8:11]
    pack_ref, shift_ref, own_out, other_out = refs[11:15]
    inner, mass, above, below, dst, grads, adj, wide, second = refs[15:]
    step = pl.program_id(0)
    half = step % 2

    @at_step(0)
    def _():
        dst[...] = side_by_side(dst_ref[:, 384:448, :])
        grads[0:384, :] = side_by_side(dst_ref[:, 0:384, :])
        grads[384:768, :] = side_by_side(first_ref)

    packed = jnp.where(half == 0, own_ref[...], other_ref[...])
    src = src_of(packed)

    @pl.when(step < 2)
    def _():
        scores, weights = weights_of(src, dst[...], norm_ref)
        pieces = [jnp.where(half == 0, a[...], b[...]) for a, b in zip(hop_own, hop_other)]
        hop = jnp.concatenate(pieces).reshape(GROUP * 128, 384)
        adj_grad = dot_nn(jnp.concatenate([hop, series_of(packed)], axis=1), grads[...])
        adj[half] = adj_grad
        wide[half] = jnp.where(scores > 0.0, weights, 0.0)
        hop_part = dot_tn(hop, weights.astype(BF16))
        second[...] = jnp.where(step == 0, hop_part, second[...] + hop_part)
        total = jnp.sum(weights * adj_grad, axis=0, keepdims=True)
        weight = jnp.sum(weights, axis=0, keepdims=True)
        inner[...] = jnp.where(step == 0, total, inner[...] + total)
        mass[...] = jnp.where(step == 0, weight, mass[...] + weight)

    @pl.when(step >= 2)
    def _():
        shift = jnp.where(mass[...] > 1e-30, inner[...] / jnp.maximum(mass[...], 1e-30), 0.0)
        masked = wide[half]
        graded = (masked * (adj[half] - shift)).astype(BF16)
        masked = masked.astype(BF16)
        up, low = dot_nn(src, graded), dot_nn(src, masked)
        above[...] = jnp.where(step == 2, up, above[...] + up)
        below[...] = jnp.where(step == 2, low, below[...] + low)
        d_src = dot_nt(dst[...], graded)

        @pl.when(half == 0)
        def _():
            for block in range(GROUP):
                own_out[block] = d_src[:, nodes(block)]

        @pl.when(half == 1)
        def _():
            shift_ref[...] = shift
            for block in range(GROUP):
                other_out[block] = d_src[:, nodes(block)]
            sums = [term[:, nodes(block)] for term in three_terms(inner[...]) for block in range(GROUP)]
            sums = jnp.concatenate(sums, axis=0)
            shifts = jnp.concatenate(three_terms(shift), axis=0)
            for block in range(GROUP):
                tail = jnp.concatenate([sums, shifts[:, nodes(block)], jnp.zeros((5, 128), F32)], axis=0)
                pack_ref[block, SECOND:ABOVE, :] = second[:, nodes(block)].astype(BF16)
                pack_ref[block, ABOVE:BELOW, :] = above[:, nodes(block)].astype(BF16)
                pack_ref[block, BELOW:INNER, :] = below[:, nodes(block)].astype(BF16)
                pack_ref[block, INNER:LAST, :] = tail.astype(BF16)


def embed_grads(*ins):
    rows = GROUP * 128
    outs = [
        array(GROUP, LAST, 128),
        array(1, rows, dtype=F32),
        array(GROUP, 64, 128, dtype=F32),
        array(GROUP, 64, 128, dtype=F32),
    ]
    scratch = [
        pltpu.VMEM((1, rows), F32),
        pltpu.VMEM((1, rows), F32),
        pltpu.VMEM((64, rows), F32),
        pltpu.VMEM((64, rows), F32),
        pltpu.VMEM((64, rows), BF16),
        pltpu.VMEM((768, rows), BF16),
        pltpu.VMEM((2, rows, rows), F32),
        pltpu.VMEM((2, rows, rows), F32),
        pltpu.VMEM((384, rows), F32),
    ]

    size = 2 * rows * rows
    return call(
        grad_kernel, 4, ins, outs, scratch, 2 * 1408 * size, size, vmem=46 * MIB
    )


def inner_of(pack_ref):
    terms = sum_of(pack_ref, INNER, LAST)
    return terms[0:8] + (terms[8:16] + terms[16:24])


def src_kernel(
    own_ref, other_ref, dst_ref, norm_ref, pack_ref, shift_ref, own_part, other_part, own_out, other_out, scaled, dst
):
    @at_step(0)
    def _():
        dst[...] = side_by_side(dst_ref[:, 384:448, :])
        inner = inner_of(pack_ref)
        for block in range(GROUP):
            change = shift_ref[:, nodes(block)] - inner[block : block + 1, :]
            scaled[:, nodes(block)] = (dst[:, nodes(block)].astype(F32) * change).astype(BF16)

    scores, weights = weights_of(src_of(pick(own_ref, other_ref)), dst[...], norm_ref)
    part = dot_nt(scaled[...], jnp.where(scores > 0.0, weights, 0.0).astype(BF16))

    me = lax.axis_index("col")
    for block in range(GROUP):
        place = (me // 4 + 4 - block // 2) % 4 * 2 + (me // 2 + block) % 2

        @at_step(0)
        def _(block=block, place=place):
            own_out[place] = own_part[block] + part[:, nodes(block)]

        @at_step(1)
        def _(block=block, place=place):
            other_out[place] = other_part[block] + part[:, nodes(block)]


def src_grads(*ins):
    rows = ins[2].shape[0] * 128
    outs = [array(GROUP, 64, 128, dtype=F32), array(GROUP, 64, 128, dtype=F32)]
    scratch = [pltpu.VMEM((64, rows), BF16), pltpu.VMEM((64, rows), BF16)]
    size = 2 * rows * rows
    return call(src_kernel, 2, ins, outs, scratch, 256 * size, size)


def output_kernel(pack_ref, hop_ref, base_ref, mix1_ref, mix2_ref, out_ref, d_dst_ref):
    second = sum_of(pack_ref, SECOND, ABOVE).T.astype(BF16)
    mixed = base_ref[...] + dot_nn(hop_ref[...], mix1_ref[...]) + dot_nn(second, mix2_ref[...])
    out_ref[...] = mixed.astype(BF16)
    me = lax.axis_index("row")
    inner = inner_of(pack_ref)
    places = lax.broadcasted_iota(jnp.int32, inner.shape, 0)
    inner = jnp.sum(jnp.where(places == me, inner, 0.0), axis=0, keepdims=True)
    d_dst = jnp.zeros((64, 128), F32)
    for d in range(GROUP):
        tail = pack_ref[d, INNER:LAST, :].astype(F32)
        shift = tail[24:25] + (tail[25:26] + tail[26:27])
        above, below = pack_ref[d, ABOVE:BELOW, :].astype(F32), pack_ref[d, BELOW:INNER, :].astype(F32)
        d_dst += above + (shift - inner) * below
    d_dst_ref[...] = d_dst


def local(dst_embed, src_embed, series, w_self, w_hop1, w_hop2, cotangent):
    src = call(source_kernel, 1, (src_embed.T, series), [array(160, 384)], vmem=60 * MIB)[0]
    src_own, src_other = (jnp.concatenate(p) for p in gather_src(jnp.stack([src, to_chip(src, 0, 1)])))
    dst, first_mixed, base, mix1, mix2 = prepare(dst_embed.T, series, w_self, w_hop1, w_hop2, cotangent)
    dst = exchange_dst(dst)
    stats = exchange_dst(softmax_stats(src_own, src_other, dst))

    norm, hop, own, other = first_hops(src_own, src_other, dst, stats)
    hop = exchange_dst(hop)
    pairs = call(cores_kernel, 1, (own, swap_cores(other)), [array(2, 384, 128)] * 4)
    pairs = [pairs[0]] + [to_chip(pairs[dx], -dx, 0) for dx in range(1, 4)]
    hop, mine, rest = call(
        join_kernel, 1, (hop, *pairs), [array(128, 384), array(384, 128, dtype=F32), array(384, 128)]
    )
    rest = to_chip(rest, 0, 1)
    first, hop_pair = call(
        first_grad_kernel, 1, (first_mixed, mine, rest, hop, to_chip(hop, 0, 1)),
        [array(GROUP, 384, 128), array(2, 128, 384)],
    )
    first = exchange_dst(first)
    hop_own, hop_other = gather_src(hop_pair)

    pack, shift, own, other = embed_grads(src_own, src_other, *hop_own, *hop_other, dst, norm, first)
    pack = exchange_dst(pack)
    own, other = src_grads(src_own, src_other, dst, norm, pack, shift, own, other)
    output, d_dst = call(
        output_kernel, 1, (pack, hop, base, mix1, mix2), [array(128, 384), array(64, 128, dtype=F32)],
        flops=4 * 128 * 384 * 384,
    )
    d_src = jnp.sum(exchange_src(own + swap_cores(other)), axis=0)
    return output, d_dst.T, d_src.T


def solution(mesh):
    blocks = P(("row", "col"), None)
    return jax.shard_map(
        local,
        mesh=mesh,
        in_specs=(blocks, blocks, blocks, P(), P(), P(), blocks),
        out_specs=(blocks, blocks, blocks),
        check_vma=False,
    )
```

```python
import jax
import jax.numpy as jnp
from jax import lax
from jax.experimental import pallas as pl
from jax.experimental.pallas import tpu as pltpu
from jax.sharding import PartitionSpec as P

BF16 = jnp.bfloat16
F32 = jnp.float32
GROUP = 8
MIB = 1024 * 1024
VMEM_BYTES = 28 * MIB

SAME_CORE = [[2 * chip + core for chip in range(8)] for core in range(2)]
OTHER_CORE = [(i, i ^ 1) for i in range(16)]


def dot_nn(a, b):
    return lax.dot_general(a, b, (((1,), (0,)), ((), ())), preferred_element_type=F32)


def dot_nt(a, b):
    return lax.dot_general(a, b, (((1,), (1,)), ((), ())), preferred_element_type=F32)


def dot_tn(a, b):
    return lax.dot_general(a, b, (((0,), (0,)), ((), ())), preferred_element_type=F32)


def exchange_dst(blocks):
    return lax.all_to_all(blocks, "row", 0, 0)


def exchange_src(blocks):
    return lax.all_to_all(blocks, "col", 0, 0, axis_index_groups=SAME_CORE)


def swap_cores(blocks):
    return lax.ppermute(blocks, "col", OTHER_CORE)


def to_chip(blocks, x_step, z_step):
    pairs = []
    for i in range(16):
        x, z, core = i // 4, i // 2 % 2, i % 2
        pairs.append((i, (x + x_step) % 4 * 4 + (z + z_step) % 2 * 2 + core))
    return lax.ppermute(blocks, "col", pairs)


def gather_src(pair):
    pairs = [pair] + [to_chip(pair, dx, 0) for dx in range(1, 4)]
    return pairs, [swap_cores(p) for p in pairs]


def array(*shape, dtype=BF16):
    return jax.ShapeDtypeStruct(shape, dtype)


def whole(a):
    return pl.BlockSpec(a.shape, lambda *_: (0,) * len(a.shape))


def by_step(a):
    return pl.BlockSpec((a.shape[0] // 2,) + a.shape[1:], lambda i, *_: (i,) + (0,) * (len(a.shape) - 1))


def call(kernel, steps, ins, outs, scratch=(), flops=0, exps=0, kinds=None, vmem=VMEM_BYTES):
    kinds = kinds or {}
    sizes = [a.size * a.dtype.itemsize for a in list(ins) + list(outs)]
    specs = [kinds.get(i, whole)(a) for i, a in enumerate(list(ins) + list(outs))]
    return pl.pallas_call(
        kernel,
        grid=(steps,),
        in_specs=specs[: len(ins)],
        out_specs=specs[len(ins) :],
        out_shape=outs,
        scratch_shapes=scratch,
        compiler_params=pltpu.CompilerParams(vmem_limit_bytes=vmem),
        cost_estimate=pl.CostEstimate(flops=flops, bytes_accessed=sum(sizes), transcendentals=exps),
    )(*ins)


def at_step(step):
    return pl.when(pl.program_id(0) == step)


def pick(own_ref, other_ref):
    return jnp.where(pl.program_id(0) == 0, own_ref[...], other_ref[...])


def put(own_ref, other_ref, block, value):
    @at_step(0)
    def _():
        own_ref[block] = value

    @at_step(1)
    def _():
        other_ref[block] = value


def accumulate(total, part):
    @at_step(0)
    def _():
        total[...] = part

    @at_step(1)
    def _():
        total[...] += part


def side_by_side(blocks):
    return jnp.concatenate([blocks[b] for b in range(GROUP)], axis=1)


def nodes(block):
    return slice(128 * block, 128 * block + 128)


def series_of(packed):
    return jnp.concatenate([packed[b, 0:128, :] for b in range(GROUP)], axis=0)


def src_of(packed):
    pieces = [packed[:, 128:160, 0:128], packed[:, 128:160, 128:256]]
    return side_by_side(jnp.concatenate(pieces, axis=1))


def mixing(weight):
    size, chan = 384, weight.shape[0]
    place = lax.broadcasted_iota(jnp.int32, (size, chan), 0) % chan
    repeat = jnp.where(place == lax.broadcasted_iota(jnp.int32, (size, chan), 1), 1.0, 0.0).astype(BF16)
    tiled = dot_nt(dot_nn(repeat, weight).astype(BF16), repeat)
    rows = lax.broadcasted_iota(jnp.int32, (size, size), 0) // chan
    cols = lax.broadcasted_iota(jnp.int32, (size, size), 1) // chan
    return jnp.where(rows == cols, tiled, 0.0).astype(BF16)


def source_kernel(src_ref, series_ref, src_out):
    src_out[0:128, :] = series_ref[...]
    src_out[128:160, 0:128] = src_ref[0:32, :]
    src_out[128:160, 128:256] = src_ref[32:64, :]
    src_out[128:160, 256:384] = jnp.zeros((32, 128), BF16)


def prepare_kernel(
    dst_ref, series_ref, self_ref, hop1_ref, hop2_ref, cotangent_ref, dst_out, first_out, base_out, mix1_out, mix2_out
):
    mix1, mix2 = mixing(hop1_ref[...]), mixing(hop2_ref[...])
    cotangent = cotangent_ref[...]
    second = dot_nt(mix2, cotangent).astype(BF16)
    for block in range(GROUP):
        dst_out[block, 0:384, :] = second
        dst_out[block, 384:448, :] = dst_ref[...]
    first_out[...] = dot_nt(mix1, cotangent)
    base_out[...] = dot_nn(series_ref[...], mixing(self_ref[...]))
    mix1_out[...] = mix1
    mix2_out[...] = mix2


def prepare(*ins):
    outs = [
        array(GROUP, 448, 128),
        array(384, 128, dtype=F32),
        array(128, 384, dtype=F32),
        array(384, 384),
        array(384, 384),
    ]
    return call(prepare_kernel, 1, ins, outs, flops=3 * 2 * 128 * 384 * 384, vmem=60 * MIB)


def stats_kernel(own_ref, other_ref, dst_ref, out_ref, state, dst):
    @at_step(0)
    def _():
        state[...] = jnp.zeros_like(state)
        dst[...] = side_by_side(dst_ref[:, 384:448, :])

    lifted = jnp.maximum(dot_tn(src_of(pick(own_ref, other_ref)), dst[...]), 0.0)
    old = state[0:1, :]
    new = jnp.maximum(old, jnp.max(lifted, axis=0, keepdims=True))
    total = jnp.sum(jnp.exp(lifted - new), axis=0, keepdims=True)
    state[1:2, :] = state[1:2, :] * jnp.exp(old - new) + total
    state[0:1, :] = new

    @at_step(1)
    def _():
        out_ref[...] = jnp.broadcast_to(state[...][None], out_ref.shape)


def softmax_stats(own, other, dst):
    rows = dst.shape[0] * 128
    scratch = [pltpu.VMEM((2, rows), F32), pltpu.VMEM((64, rows), BF16)]
    outs = [array(GROUP, 2, rows, dtype=F32)]
    size = 2 * rows * rows
    return call(stats_kernel, 2, (own, other, dst), outs, scratch, 128 * size, size)[0]


def weights_of(src, dst, norm_ref):
    scores = dot_tn(src, dst)
    weights = jnp.exp(jnp.maximum(scores, 0.0) - norm_ref[0:1, :]) * norm_ref[1:2, :]
    return scores, weights


def hops_kernel(
    own_ref, other_ref, dst_ref, stats_ref, norm_ref, hop_ref, own_out, other_out, total, dst, second
):
    @at_step(0)
    def _():
        peak = stats_ref[0, 0:1, :]
        for d in range(1, GROUP):
            peak = jnp.maximum(peak, stats_ref[d, 0:1, :])
        row_sum = jnp.zeros_like(peak)
        for d in range(GROUP):
            row_sum += stats_ref[d, 1:2, :] * jnp.exp(stats_ref[d, 0:1, :] - peak)
        norm_ref[0:1, :] = peak
        norm_ref[1:2, :] = 1.0 / row_sum
        second[...] = side_by_side(dst_ref[:, 0:384, :])
        dst[...] = side_by_side(dst_ref[:, 384:448, :])

    packed = pick(own_ref, other_ref)
    adjacency = weights_of(src_of(packed), dst[...], norm_ref)[1].astype(BF16)
    carried = dot_nt(second[...], adjacency).astype(BF16)
    for block in range(GROUP):
        put(own_out, other_out, block, carried[:, nodes(block)])
    accumulate(total, dot_tn(series_of(packed), adjacency))

    @at_step(1)
    def _():
        for block in range(GROUP):
            hop_ref[block] = total[:, nodes(block)].astype(BF16)


def first_hops(own, other, dst, stats):
    rows = dst.shape[0] * 128
    outs = [array(2, rows, dtype=F32)] + [array(GROUP, 384, 128)] * 3
    scratch = [pltpu.VMEM((384, rows), F32), pltpu.VMEM((64, rows), BF16), pltpu.VMEM((384, rows), BF16)]
    size = 2 * rows * rows
    return call(hops_kernel, 2, (own, other, dst, stats), outs, scratch, 2 * 832 * size, size)


def sum_of(pack_ref, start, stop):
    total = pack_ref[0, start:stop, :].astype(F32)
    for d in range(1, GROUP):
        total += pack_ref[d, start:stop, :].astype(F32)
    return total


def cores_kernel(own_ref, other_ref, *outs):
    for place, out in enumerate(outs):
        pair = slice(2 * place, 2 * place + 2)
        out[...] = (own_ref[pair].astype(F32) + other_ref[pair].astype(F32)).astype(BF16)


def join_kernel(hop_ref, a_ref, b_ref, c_ref, d_ref, hop_out, mine_out, other_out):
    def total(place):
        parts = [ref[place].astype(F32) for ref in (a_ref, b_ref, c_ref, d_ref)]
        return (parts[0] + parts[1]) + (parts[2] + parts[3])

    other_out[...] = total(1).astype(BF16)
    hop_out[...] = sum_of(hop_ref, 0, 384).T.astype(BF16)
    mine_out[...] = total(0)


def first_grad_kernel(mixed_ref, mine_ref, other_ref, hop_ref, next_ref, out_ref, pair_ref):
    pair_ref[0] = hop_ref[...]
    pair_ref[1] = next_ref[...]
    grad = (mixed_ref[...] + (mine_ref[...] + other_ref[...].astype(F32))).astype(BF16)
    for block in range(GROUP):
        out_ref[block] = grad


def three_terms(value):
    high = value.astype(BF16).astype(F32)
    middle = (value - high).astype(BF16).astype(F32)
    return [high, middle, value - high - middle]


SECOND, ABOVE, BELOW, INNER, SHIFT, LAST = 0, 384, 448, 512, 536, 544


def pieces_kernel(*refs):
    for place, ref in enumerate(refs[:-1]):
        refs[-1][256 * place : 256 * place + 256, :] = ref[...].reshape(256, 384)


def grad_kernel(
    own_ref, other_ref, hop_ref, dst_ref, norm_ref, first_ref,
    pack_ref, shift_ref, own_out, other_out, inner, mass, above, below, dst, grads, adj, wide, second,
):
    step = pl.program_id(0)
    half = step % 2

    @at_step(0)
    def _():
        dst[...] = side_by_side(dst_ref[:, 384:448, :])
        grads[0:384, :] = side_by_side(dst_ref[:, 0:384, :])
        grads[384:768, :] = side_by_side(first_ref)

    packed = jnp.where(half == 0, own_ref[...], other_ref[...])
    src = src_of(packed)

    @pl.when(step < 2)
    def _():
        scores, weights = weights_of(src, dst[...], norm_ref)
        hop = hop_ref[...]
        adj_grad = dot_nn(jnp.concatenate([hop, series_of(packed)], axis=1), grads[...])
        adj[half] = adj_grad
        wide[half] = jnp.where(scores > 0.0, weights, 0.0)
        hop_part = dot_tn(hop, weights.astype(BF16))
        second[...] = jnp.where(step == 0, hop_part, second[...] + hop_part)
        total = jnp.sum(weights * adj_grad, axis=0, keepdims=True)
        weight = jnp.sum(weights, axis=0, keepdims=True)
        inner[...] = jnp.where(step == 0, total, inner[...] + total)
        mass[...] = jnp.where(step == 0, weight, mass[...] + weight)

    @pl.when(step >= 2)
    def _():
        shift = jnp.where(mass[...] > 1e-30, inner[...] / jnp.maximum(mass[...], 1e-30), 0.0)
        masked = wide[half]
        graded = (masked * (adj[half] - shift)).astype(BF16)
        masked = masked.astype(BF16)
        up, low = dot_nn(src, graded), dot_nn(src, masked)
        above[...] = jnp.where(step == 2, up, above[...] + up)
        below[...] = jnp.where(step == 2, low, below[...] + low)
        d_src = dot_nt(dst[...], graded)

        @pl.when(half == 0)
        def _():
            for block in range(GROUP):
                own_out[block] = d_src[:, nodes(block)]

        @pl.when(half == 1)
        def _():
            shift_ref[...] = shift
            for block in range(GROUP):
                other_out[block] = d_src[:, nodes(block)]
            sums = [term[:, nodes(block)] for term in three_terms(inner[...]) for block in range(GROUP)]
            sums = jnp.concatenate(sums, axis=0)
            shifts = jnp.concatenate(three_terms(shift), axis=0)
            for block in range(GROUP):
                tail = jnp.concatenate([sums, shifts[:, nodes(block)], jnp.zeros((5, 128), F32)], axis=0)
                pack_ref[block, SECOND:ABOVE, :] = second[:, nodes(block)].astype(BF16)
                pack_ref[block, ABOVE:BELOW, :] = above[:, nodes(block)].astype(BF16)
                pack_ref[block, BELOW:INNER, :] = below[:, nodes(block)].astype(BF16)
                pack_ref[block, INNER:LAST, :] = tail.astype(BF16)


def embed_grads(*ins):
    rows = GROUP * 128
    outs = [
        array(GROUP, LAST, 128),
        array(1, rows, dtype=F32),
        array(GROUP, 64, 128, dtype=F32),
        array(GROUP, 64, 128, dtype=F32),
    ]
    scratch = [
        pltpu.VMEM((1, rows), F32),
        pltpu.VMEM((1, rows), F32),
        pltpu.VMEM((64, rows), F32),
        pltpu.VMEM((64, rows), F32),
        pltpu.VMEM((64, rows), BF16),
        pltpu.VMEM((768, rows), BF16),
        pltpu.VMEM((2, rows, rows), F32),
        pltpu.VMEM((2, rows, rows), F32),
        pltpu.VMEM((384, rows), F32),
    ]


    def first_pass(a):
        return pl.BlockSpec((a.shape[0] // 2, a.shape[1]), lambda i: (jnp.minimum(i, 1), 0))

    size = 2 * rows * rows
    return call(
        grad_kernel, 4, ins, outs, scratch, 2 * 1408 * size, size, kinds={2: first_pass}, vmem=46 * MIB
    )


def inner_of(pack_ref):
    terms = sum_of(pack_ref, INNER, LAST)
    return terms[0:8] + (terms[8:16] + terms[16:24])


def src_kernel(
    own_ref, other_ref, dst_ref, norm_ref, pack_ref, shift_ref, own_part, other_part, own_out, other_out, scaled, dst
):
    @at_step(0)
    def _():
        dst[...] = side_by_side(dst_ref[:, 384:448, :])
        inner = inner_of(pack_ref)
        for block in range(GROUP):
            change = shift_ref[:, nodes(block)] - inner[block : block + 1, :]
            scaled[:, nodes(block)] = (dst[:, nodes(block)].astype(F32) * change).astype(BF16)

    scores, weights = weights_of(src_of(pick(own_ref, other_ref)), dst[...], norm_ref)
    part = dot_nt(scaled[...], jnp.where(scores > 0.0, weights, 0.0).astype(BF16))

    me = lax.axis_index("col")
    for block in range(GROUP):
        place = (me // 4 + 4 - block // 2) % 4 * 2 + (me // 2 + block) % 2

        @at_step(0)
        def _(block=block, place=place):
            own_out[place] = own_part[block] + part[:, nodes(block)]

        @at_step(1)
        def _(block=block, place=place):
            other_out[place] = other_part[block] + part[:, nodes(block)]


def src_grads(*ins):
    rows = ins[2].shape[0] * 128
    outs = [array(GROUP, 64, 128, dtype=F32), array(GROUP, 64, 128, dtype=F32)]
    scratch = [pltpu.VMEM((64, rows), BF16), pltpu.VMEM((64, rows), BF16)]
    size = 2 * rows * rows
    return call(src_kernel, 2, ins, outs, scratch, 256 * size, size)


def output_kernel(pack_ref, hop_ref, base_ref, mix1_ref, mix2_ref, out_ref, d_dst_ref):
    second = sum_of(pack_ref, SECOND, ABOVE).T.astype(BF16)
    mixed = base_ref[...] + dot_nn(hop_ref[...], mix1_ref[...]) + dot_nn(second, mix2_ref[...])
    out_ref[...] = mixed.astype(BF16)
    me = lax.axis_index("row")
    inner = inner_of(pack_ref)
    places = lax.broadcasted_iota(jnp.int32, inner.shape, 0)
    inner = jnp.sum(jnp.where(places == me, inner, 0.0), axis=0, keepdims=True)
    d_dst = jnp.zeros((64, 128), F32)
    for d in range(GROUP):
        tail = pack_ref[d, INNER:LAST, :].astype(F32)
        shift = tail[24:25] + (tail[25:26] + tail[26:27])
        above, below = pack_ref[d, ABOVE:BELOW, :].astype(F32), pack_ref[d, BELOW:INNER, :].astype(F32)
        d_dst += above + (shift - inner) * below
    d_dst_ref[...] = d_dst


def local(dst_embed, src_embed, series, w_self, w_hop1, w_hop2, cotangent):
    src = call(source_kernel, 1, (src_embed.T, series), [array(160, 384)], vmem=60 * MIB)[0]
    src_own, src_other = (jnp.concatenate(p) for p in gather_src(jnp.stack([src, to_chip(src, 0, 1)])))
    dst, first_mixed, base, mix1, mix2 = prepare(dst_embed.T, series, w_self, w_hop1, w_hop2, cotangent)
    dst = exchange_dst(dst)
    stats = exchange_dst(softmax_stats(src_own, src_other, dst))

    norm, hop, own, other = first_hops(src_own, src_other, dst, stats)
    hop = exchange_dst(hop)
    pairs = call(cores_kernel, 1, (own, swap_cores(other)), [array(2, 384, 128)] * 4)
    pairs = [pairs[0]] + [to_chip(pairs[dx], -dx, 0) for dx in range(1, 4)]
    hop, mine, rest = call(
        join_kernel, 1, (hop, *pairs), [array(128, 384), array(384, 128, dtype=F32), array(384, 128)]
    )
    rest = to_chip(rest, 0, 1)
    first, hop_pair = call(
        first_grad_kernel, 1, (first_mixed, mine, rest, hop, to_chip(hop, 0, 1)),
        [array(GROUP, 384, 128), array(2, 128, 384)],
    )
    first = exchange_dst(first)
    hop_own, hop_other = gather_src(hop_pair)
    hop_all = call(pieces_kernel, 1, (*hop_own, *hop_other), [array(2 * GROUP * 128, 384)])[0]

    pack, shift, own, other = embed_grads(src_own, src_other, hop_all, dst, norm, first)
    pack = exchange_dst(pack)
    own, other = src_grads(src_own, src_other, dst, norm, pack, shift, own, other)
    output, d_dst = call(
        output_kernel, 1, (pack, hop, base, mix1, mix2), [array(128, 384), array(64, 128, dtype=F32)],
        flops=4 * 128 * 384 * 384,
    )
    d_src = jnp.sum(exchange_src(own + swap_cores(other)), axis=0)
    return output, d_dst.T, d_src.T


def solution(mesh):
    blocks = P(("row", "col"), None)
    return jax.shard_map(
        local,
        mesh=mesh,
        in_specs=(blocks, blocks, blocks, P(), P(), P(), blocks),
        out_specs=(blocks, blocks, blocks),
        check_vma=False,
    )
```

```python
import jax
import jax.numpy as jnp
from jax import lax
from jax.experimental import pallas as pl
from jax.experimental.pallas import tpu as pltpu
from jax.sharding import PartitionSpec as P

BF16 = jnp.bfloat16
F32 = jnp.float32
GROUP = 8
MIB = 1024 * 1024
VMEM_BYTES = 28 * MIB

SAME_CORE = [[2 * chip + core for chip in range(8)] for core in range(2)]
OTHER_CORE = [(i, i ^ 1) for i in range(16)]


def dot_nn(a, b):
    return lax.dot_general(a, b, (((1,), (0,)), ((), ())), preferred_element_type=F32)


def dot_nt(a, b):
    return lax.dot_general(a, b, (((1,), (1,)), ((), ())), preferred_element_type=F32)


def dot_tn(a, b):
    return lax.dot_general(a, b, (((0,), (0,)), ((), ())), preferred_element_type=F32)


def exchange_dst(blocks):
    return lax.all_to_all(blocks, "row", 0, 0)


def exchange_src(blocks):
    return lax.all_to_all(blocks, "col", 0, 0, axis_index_groups=SAME_CORE)


def swap_cores(blocks):
    return lax.ppermute(blocks, "col", OTHER_CORE)


def to_chip(blocks, x_step, z_step):
    pairs = []
    for i in range(16):
        x, z, core = i // 4, i // 2 % 2, i % 2
        pairs.append((i, (x + x_step) % 4 * 4 + (z + z_step) % 2 * 2 + core))
    return lax.ppermute(blocks, "col", pairs)


def gather_chips(pair):
    return [pair] + [to_chip(pair, dx, 0) for dx in range(1, 4)]


def gather_src(pair):
    pairs = gather_chips(pair)
    return pairs, [swap_cores(p) for p in pairs]


def array(*shape, dtype=BF16):
    return jax.ShapeDtypeStruct(shape, dtype)


def whole(a):
    return pl.BlockSpec(a.shape, lambda *_: (0,) * len(a.shape))


def by_step(a):
    return pl.BlockSpec((a.shape[0] // 2,) + a.shape[1:], lambda i, *_: (i,) + (0,) * (len(a.shape) - 1))


def call(kernel, steps, ins, outs, scratch=(), flops=0, exps=0, kinds=None, vmem=VMEM_BYTES):
    kinds = kinds or {}
    sizes = [a.size * a.dtype.itemsize for a in list(ins) + list(outs)]
    specs = [kinds.get(i, whole)(a) for i, a in enumerate(list(ins) + list(outs))]
    return pl.pallas_call(
        kernel,
        grid=(steps,),
        in_specs=specs[: len(ins)],
        out_specs=specs[len(ins) :],
        out_shape=outs,
        scratch_shapes=scratch,
        compiler_params=pltpu.CompilerParams(vmem_limit_bytes=vmem),
        cost_estimate=pl.CostEstimate(flops=flops, bytes_accessed=sum(sizes), transcendentals=exps),
    )(*ins)


def at_step(step):
    return pl.when(pl.program_id(0) == step)


def pick(own_ref, other_ref):
    return jnp.where(pl.program_id(0) == 0, own_ref[...], other_ref[...])


def put(own_ref, other_ref, block, value):
    @at_step(0)
    def _():
        own_ref[block] = value

    @at_step(1)
    def _():
        other_ref[block] = value


def accumulate(total, part):
    @at_step(0)
    def _():
        total[...] = part

    @at_step(1)
    def _():
        total[...] += part


def side_by_side(blocks):
    return jnp.concatenate([blocks[b] for b in range(GROUP)], axis=1)


def nodes(block):
    return slice(128 * block, 128 * block + 128)


def mixing(weight):
    size, chan = 384, weight.shape[0]
    place = lax.broadcasted_iota(jnp.int32, (size, chan), 0) % chan
    repeat = jnp.where(place == lax.broadcasted_iota(jnp.int32, (size, chan), 1), 1.0, 0.0).astype(BF16)
    tiled = dot_nt(dot_nn(repeat, weight).astype(BF16), repeat)
    rows = lax.broadcasted_iota(jnp.int32, (size, size), 0) // chan
    cols = lax.broadcasted_iota(jnp.int32, (size, size), 1) // chan
    return jnp.where(rows == cols, tiled, 0.0).astype(BF16)


def prepare_kernel(
    dst_ref, series_ref, self_ref, hop1_ref, hop2_ref, cotangent_ref, dst_out, first_out, base_out, mix1_out, mix2_out
):
    mix1, mix2 = mixing(hop1_ref[...]), mixing(hop2_ref[...])
    cotangent = cotangent_ref[...]
    second = dot_nt(mix2, cotangent).astype(BF16)
    for block in range(GROUP):
        dst_out[block, 0:384, :] = second
        dst_out[block, 384:448, :] = dst_ref[...]
    first_out[...] = dot_nt(mix1, cotangent)
    base_out[...] = dot_nn(series_ref[...], mixing(self_ref[...]))
    mix1_out[...] = mix1
    mix2_out[...] = mix2


def prepare(*ins):
    outs = [
        array(GROUP, 448, 128),
        array(384, 128, dtype=F32),
        array(128, 384, dtype=F32),
        array(384, 384),
        array(384, 384),
    ]
    return call(prepare_kernel, 1, ins, outs, flops=3 * 2 * 128 * 384 * 384, vmem=60 * MIB)


def stats_kernel(own_ref, other_ref, dst_ref, out_ref, state, dst):
    @at_step(0)
    def _():
        state[...] = jnp.zeros_like(state)
        dst[...] = side_by_side(dst_ref[:, 384:448, :])

    lifted = jnp.maximum(dot_tn(side_by_side(pick(own_ref, other_ref)), dst[...]), 0.0)
    old = state[0:1, :]
    new = jnp.maximum(old, jnp.max(lifted, axis=0, keepdims=True))
    total = jnp.sum(jnp.exp(lifted - new), axis=0, keepdims=True)
    state[1:2, :] = state[1:2, :] * jnp.exp(old - new) + total
    state[0:1, :] = new

    @at_step(1)
    def _():
        out_ref[...] = jnp.broadcast_to(state[...][None], out_ref.shape)


def softmax_stats(own, other, dst):
    rows = dst.shape[0] * 128
    scratch = [pltpu.VMEM((2, rows), F32), pltpu.VMEM((64, rows), BF16)]
    outs = [array(GROUP, 2, rows, dtype=F32)]
    size = 2 * rows * rows
    return call(stats_kernel, 2, (own, other, dst), outs, scratch, 128 * size, size)[0]


def weights_of(src, dst, norm_ref):
    scores = dot_tn(src, dst)
    weights = jnp.exp(jnp.maximum(scores, 0.0) - norm_ref[0:1, :]) * norm_ref[1:2, :]
    return scores, weights


def hops_kernel(
    own_ref, other_ref, series_own, series_other, dst_ref, stats_ref,
    norm_ref, hop_ref, own_out, other_out, total, dst, second,
):
    @at_step(0)
    def _():
        peak = stats_ref[0, 0:1, :]
        for d in range(1, GROUP):
            peak = jnp.maximum(peak, stats_ref[d, 0:1, :])
        row_sum = jnp.zeros_like(peak)
        for d in range(GROUP):
            row_sum += stats_ref[d, 1:2, :] * jnp.exp(stats_ref[d, 0:1, :] - peak)
        norm_ref[0:1, :] = peak
        norm_ref[1:2, :] = 1.0 / row_sum
        second[...] = side_by_side(dst_ref[:, 0:384, :])
        dst[...] = side_by_side(dst_ref[:, 384:448, :])

    src = side_by_side(pick(own_ref, other_ref))
    adjacency = weights_of(src, dst[...], norm_ref)[1].astype(BF16)
    carried = dot_nt(second[...], adjacency).astype(BF16)
    for block in range(GROUP):
        put(own_out, other_out, block, carried[:, nodes(block)])
    accumulate(total, dot_tn(pick(series_own, series_other), adjacency))

    @at_step(1)
    def _():
        for block in range(GROUP):
            hop_ref[block] = total[:, nodes(block)].astype(BF16)


def first_hops(*ins):
    rows = GROUP * 128
    outs = [array(2, rows, dtype=F32)] + [array(GROUP, 384, 128)] * 3
    scratch = [pltpu.VMEM((384, rows), F32), pltpu.VMEM((64, rows), BF16), pltpu.VMEM((384, rows), BF16)]
    size = 2 * rows * rows
    return call(hops_kernel, 2, ins, outs, scratch, 2 * 832 * size, size)


def sum_of(pack_ref, start, stop):
    total = pack_ref[0, start:stop, :].astype(F32)
    for d in range(1, GROUP):
        total += pack_ref[d, start:stop, :].astype(F32)
    return total


def cores_kernel(own_ref, other_ref, *outs):
    for place, out in enumerate(outs):
        pair = slice(2 * place, 2 * place + 2)
        out[...] = (own_ref[pair].astype(F32) + other_ref[pair].astype(F32)).astype(BF16)


def join_kernel(hop_ref, a_ref, b_ref, c_ref, d_ref, hop_out, mine_out, other_out):
    def total(place):
        parts = [ref[place].astype(F32) for ref in (a_ref, b_ref, c_ref, d_ref)]
        return (parts[0] + parts[1]) + (parts[2] + parts[3])

    other_out[...] = total(1).astype(BF16)
    hop_out[...] = sum_of(hop_ref, 0, 384).T.astype(BF16)
    mine_out[...] = total(0)


def first_grad_kernel(mixed_ref, mine_ref, other_ref, hop_ref, next_ref, out_ref, pair_ref):
    pair_ref[0] = hop_ref[...]
    pair_ref[1] = next_ref[...]
    grad = (mixed_ref[...] + (mine_ref[...] + other_ref[...].astype(F32))).astype(BF16)
    for block in range(GROUP):
        out_ref[block] = grad


def three_terms(value):
    high = value.astype(BF16).astype(F32)
    middle = (value - high).astype(BF16).astype(F32)
    return [high, middle, value - high - middle]


SECOND, ABOVE, BELOW, INNER, SHIFT, LAST = 0, 384, 448, 512, 536, 544


def pieces_kernel(*refs):
    for place, ref in enumerate(refs[:-1]):
        refs[-1][256 * place : 256 * place + 256, :] = ref[...].reshape(256, 384)


def after_kernel(first_ref, *refs):
    del first_ref
    pieces_kernel(*refs)


def grad_kernel(
    own_ref, other_ref, series_own, series_other, hop_ref, dst_ref, norm_ref, first_ref,
    pack_ref, shift_ref, own_out, other_out, inner, mass, above, below, dst, grads, adj, wide, second,
):
    step = pl.program_id(0)
    half = step % 2

    @at_step(0)
    def _():
        dst[...] = side_by_side(dst_ref[:, 384:448, :])
        grads[0:384, :] = side_by_side(dst_ref[:, 0:384, :])
        grads[384:768, :] = side_by_side(first_ref)

    src = side_by_side(jnp.where(half == 0, own_ref[...], other_ref[...]))

    @pl.when(step < 2)
    def _():
        scores, weights = weights_of(src, dst[...], norm_ref)
        hop = hop_ref[...]
        series = jnp.where(half == 0, series_own[...], series_other[...])
        adj_grad = dot_nn(jnp.concatenate([hop, series], axis=1), grads[...])
        adj[half] = adj_grad
        wide[half] = jnp.where(scores > 0.0, weights, 0.0)
        hop_part = dot_tn(hop, weights.astype(BF16))
        second[...] = jnp.where(step == 0, hop_part, second[...] + hop_part)
        total = jnp.sum(weights * adj_grad, axis=0, keepdims=True)
        weight = jnp.sum(weights, axis=0, keepdims=True)
        inner[...] = jnp.where(step == 0, total, inner[...] + total)
        mass[...] = jnp.where(step == 0, weight, mass[...] + weight)

    @pl.when(step >= 2)
    def _():
        shift = jnp.where(mass[...] > 1e-30, inner[...] / jnp.maximum(mass[...], 1e-30), 0.0)
        masked = wide[half]
        graded = (masked * (adj[half] - shift)).astype(BF16)
        masked = masked.astype(BF16)
        up, low = dot_nn(src, graded), dot_nn(src, masked)
        above[...] = jnp.where(step == 2, up, above[...] + up)
        below[...] = jnp.where(step == 2, low, below[...] + low)
        d_src = dot_nt(dst[...], graded)

        @pl.when(half == 0)
        def _():
            for block in range(GROUP):
                own_out[block] = d_src[:, nodes(block)]

        @pl.when(half == 1)
        def _():
            shift_ref[...] = shift
            for block in range(GROUP):
                other_out[block] = d_src[:, nodes(block)]
            sums = [term[:, nodes(block)] for term in three_terms(inner[...]) for block in range(GROUP)]
            sums = jnp.concatenate(sums, axis=0)
            shifts = jnp.concatenate(three_terms(shift), axis=0)
            for block in range(GROUP):
                tail = jnp.concatenate([sums, shifts[:, nodes(block)], jnp.zeros((5, 128), F32)], axis=0)
                pack_ref[block, SECOND:ABOVE, :] = second[:, nodes(block)].astype(BF16)
                pack_ref[block, ABOVE:BELOW, :] = above[:, nodes(block)].astype(BF16)
                pack_ref[block, BELOW:INNER, :] = below[:, nodes(block)].astype(BF16)
                pack_ref[block, INNER:LAST, :] = tail.astype(BF16)


def embed_grads(*ins):
    rows = GROUP * 128
    outs = [
        array(GROUP, LAST, 128),
        array(1, rows, dtype=F32),
        array(GROUP, 64, 128, dtype=F32),
        array(GROUP, 64, 128, dtype=F32),
    ]
    scratch = [
        pltpu.VMEM((1, rows), F32),
        pltpu.VMEM((1, rows), F32),
        pltpu.VMEM((64, rows), F32),
        pltpu.VMEM((64, rows), F32),
        pltpu.VMEM((64, rows), BF16),
        pltpu.VMEM((768, rows), BF16),
        pltpu.VMEM((2, rows, rows), F32),
        pltpu.VMEM((2, rows, rows), F32),
        pltpu.VMEM((384, rows), F32),
    ]


    def first_pass(a):
        return pl.BlockSpec((a.shape[0] // 2, a.shape[1]), lambda i: (jnp.minimum(i, 1), 0))

    size = 2 * rows * rows
    return call(
        grad_kernel, 4, ins, outs, scratch, 2 * 1408 * size, size, kinds={4: first_pass}, vmem=46 * MIB
    )


def inner_of(pack_ref):
    terms = sum_of(pack_ref, INNER, LAST)
    return terms[0:8] + (terms[8:16] + terms[16:24])


def src_kernel(
    own_ref, other_ref, dst_ref, norm_ref, pack_ref, shift_ref, own_part, other_part, own_out, other_out, scaled, dst
):
    @at_step(0)
    def _():
        dst[...] = side_by_side(dst_ref[:, 384:448, :])
        inner = inner_of(pack_ref)
        for block in range(GROUP):
            change = shift_ref[:, nodes(block)] - inner[block : block + 1, :]
            scaled[:, nodes(block)] = (dst[:, nodes(block)].astype(F32) * change).astype(BF16)

    scores, weights = weights_of(side_by_side(pick(own_ref, other_ref)), dst[...], norm_ref)
    part = dot_nt(scaled[...], jnp.where(scores > 0.0, weights, 0.0).astype(BF16))

    me = lax.axis_index("col")
    for block in range(GROUP):
        place = (me // 4 + 4 - block // 2) % 4 * 2 + (me // 2 + block) % 2

        @at_step(0)
        def _(block=block, place=place):
            own_out[place] = own_part[block] + part[:, nodes(block)]

        @at_step(1)
        def _(block=block, place=place):
            other_out[place] = other_part[block] + part[:, nodes(block)]


def src_grads(*ins):
    rows = ins[2].shape[0] * 128
    outs = [array(GROUP, 64, 128, dtype=F32), array(GROUP, 64, 128, dtype=F32)]
    scratch = [pltpu.VMEM((64, rows), BF16), pltpu.VMEM((64, rows), BF16)]
    size = 2 * rows * rows
    return call(src_kernel, 2, ins, outs, scratch, 256 * size, size)


def output_kernel(pack_ref, hop_ref, base_ref, mix1_ref, mix2_ref, out_ref, d_dst_ref):
    second = sum_of(pack_ref, SECOND, ABOVE).T.astype(BF16)
    mixed = base_ref[...] + dot_nn(hop_ref[...], mix1_ref[...]) + dot_nn(second, mix2_ref[...])
    out_ref[...] = mixed.astype(BF16)
    me = lax.axis_index("row")
    inner = inner_of(pack_ref)
    places = lax.broadcasted_iota(jnp.int32, inner.shape, 0)
    inner = jnp.sum(jnp.where(places == me, inner, 0.0), axis=0, keepdims=True)
    d_dst = jnp.zeros((64, 128), F32)
    for d in range(GROUP):
        tail = pack_ref[d, INNER:LAST, :].astype(F32)
        shift = tail[24:25] + (tail[25:26] + tail[26:27])
        above, below = pack_ref[d, ABOVE:BELOW, :].astype(F32), pack_ref[d, BELOW:INNER, :].astype(F32)
        d_dst += above + (shift - inner) * below
    d_dst_ref[...] = d_dst


def local(dst_embed, src_embed, series, w_self, w_hop1, w_hop2, cotangent):
    src = src_embed.T
    src_own, src_other = (jnp.concatenate(p) for p in gather_src(jnp.stack([src, to_chip(src, 0, 1)])))
    pieces = gather_chips(jnp.stack([series, to_chip(series, 0, 1)]))
    dst, first_mixed, base, mix1, mix2 = prepare(dst_embed.T, series, w_self, w_hop1, w_hop2, cotangent)
    dst = exchange_dst(dst)
    stats = softmax_stats(src_own, src_other, dst)
    series_own = call(after_kernel, 1, (stats, *pieces), [array(GROUP * 128, 384)])[0]
    series_other = swap_cores(series_own)
    stats = exchange_dst(stats)

    norm, hop, own, other = first_hops(src_own, src_other, series_own, series_other, dst, stats)
    hop = exchange_dst(hop)
    pairs = call(cores_kernel, 1, (own, swap_cores(other)), [array(2, 384, 128)] * 4)
    pairs = [pairs[0]] + [to_chip(pairs[dx], -dx, 0) for dx in range(1, 4)]
    hop, mine, rest = call(
        join_kernel, 1, (hop, *pairs), [array(128, 384), array(384, 128, dtype=F32), array(384, 128)]
    )
    rest = to_chip(rest, 0, 1)
    first, hop_pair = call(
        first_grad_kernel, 1, (first_mixed, mine, rest, hop, to_chip(hop, 0, 1)),
        [array(GROUP, 384, 128), array(2, 128, 384)],
    )
    first = exchange_dst(first)
    hop_own, hop_other = gather_src(hop_pair)
    hop_all = call(pieces_kernel, 1, (*hop_own, *hop_other), [array(2 * GROUP * 128, 384)])[0]

    pack, shift, own, other = embed_grads(
        src_own, src_other, series_own, series_other, hop_all, dst, norm, first
    )
    pack = exchange_dst(pack)
    own, other = src_grads(src_own, src_other, dst, norm, pack, shift, own, other)
    output, d_dst = call(
        output_kernel, 1, (pack, hop, base, mix1, mix2), [array(128, 384), array(64, 128, dtype=F32)],
        flops=4 * 128 * 384 * 384,
    )
    d_src = jnp.sum(exchange_src(own + swap_cores(other)), axis=0)
    return output, d_dst.T, d_src.T


def solution(mesh):
    blocks = P(("row", "col"), None)
    return jax.shard_map(
        local,
        mesh=mesh,
        in_specs=(blocks, blocks, blocks, P(), P(), P(), blocks),
        out_specs=(blocks, blocks, blocks),
        check_vma=False,
    )
```

```python
import jax
import jax.numpy as jnp
from jax import lax
from jax.experimental import pallas as pl
from jax.experimental.pallas import tpu as pltpu
from jax.sharding import PartitionSpec as P

BF16 = jnp.bfloat16
F32 = jnp.float32
GROUP = 8
MIB = 1024 * 1024
VMEM_BYTES = 28 * MIB

SAME_CORE = [[2 * chip + core for chip in range(8)] for core in range(2)]
OTHER_CORE = [(i, i ^ 1) for i in range(16)]


def dot_nn(a, b):
    return lax.dot_general(a, b, (((1,), (0,)), ((), ())), preferred_element_type=F32)


def dot_nt(a, b):
    return lax.dot_general(a, b, (((1,), (1,)), ((), ())), preferred_element_type=F32)


def dot_tn(a, b):
    return lax.dot_general(a, b, (((0,), (0,)), ((), ())), preferred_element_type=F32)


def exchange_dst(blocks):
    return lax.all_to_all(blocks, "row", 0, 0)


def exchange_src(blocks):
    return lax.all_to_all(blocks, "col", 0, 0, axis_index_groups=SAME_CORE)


def swap_cores(blocks):
    return lax.ppermute(blocks, "col", OTHER_CORE)


def to_chip(blocks, x_step, z_step):
    pairs = []
    for i in range(16):
        x, z, core = i // 4, i // 2 % 2, i % 2
        pairs.append((i, (x + x_step) % 4 * 4 + (z + z_step) % 2 * 2 + core))
    return lax.ppermute(blocks, "col", pairs)


def gather_chips(pair):
    return [pair] + [to_chip(pair, dx, 0) for dx in range(1, 4)]


def gather_src(pair):
    pairs = gather_chips(pair)
    return pairs, [swap_cores(p) for p in pairs]


def array(*shape, dtype=BF16):
    return jax.ShapeDtypeStruct(shape, dtype)


def whole(a):
    return pl.BlockSpec(a.shape, lambda *_: (0,) * len(a.shape))


def by_step(a):
    return pl.BlockSpec((a.shape[0] // 2,) + a.shape[1:], lambda i, *_: (i,) + (0,) * (len(a.shape) - 1))


def call(kernel, steps, ins, outs, scratch=(), flops=0, exps=0, kinds=None, vmem=VMEM_BYTES):
    kinds = kinds or {}
    sizes = [a.size * a.dtype.itemsize for a in list(ins) + list(outs)]
    specs = [kinds.get(i, whole)(a) for i, a in enumerate(list(ins) + list(outs))]
    return pl.pallas_call(
        kernel,
        grid=(steps,),
        in_specs=specs[: len(ins)],
        out_specs=specs[len(ins) :],
        out_shape=outs,
        scratch_shapes=scratch,
        compiler_params=pltpu.CompilerParams(vmem_limit_bytes=vmem),
        cost_estimate=pl.CostEstimate(flops=flops, bytes_accessed=sum(sizes), transcendentals=exps),
    )(*ins)


def at_step(step):
    return pl.when(pl.program_id(0) == step)


def pick(own_ref, other_ref):
    return jnp.where(pl.program_id(0) == 0, own_ref[...], other_ref[...])


def put(own_ref, other_ref, block, value):
    @at_step(0)
    def _():
        own_ref[block] = value

    @at_step(1)
    def _():
        other_ref[block] = value


def accumulate(total, part):
    @at_step(0)
    def _():
        total[...] = part

    @at_step(1)
    def _():
        total[...] += part


def side_by_side(blocks):
    return jnp.concatenate([blocks[b] for b in range(GROUP)], axis=1)


def nodes(block):
    return slice(128 * block, 128 * block + 128)


def mixing(weight):
    size, chan = 384, weight.shape[0]
    place = lax.broadcasted_iota(jnp.int32, (size, chan), 0) % chan
    repeat = jnp.where(place == lax.broadcasted_iota(jnp.int32, (size, chan), 1), 1.0, 0.0).astype(BF16)
    tiled = dot_nt(dot_nn(repeat, weight).astype(BF16), repeat)
    rows = lax.broadcasted_iota(jnp.int32, (size, size), 0) // chan
    cols = lax.broadcasted_iota(jnp.int32, (size, size), 1) // chan
    return jnp.where(rows == cols, tiled, 0.0).astype(BF16)


def prepare_kernel(
    dst_ref, series_ref, self_ref, hop1_ref, hop2_ref, cotangent_ref, dst_out, first_out, base_out, mix1_out, mix2_out
):
    mix1, mix2 = mixing(hop1_ref[...]), mixing(hop2_ref[...])
    cotangent = cotangent_ref[...]
    second = dot_nt(mix2, cotangent).astype(BF16)
    for block in range(GROUP):
        dst_out[block, 0:384, :] = second
        dst_out[block, 384:448, :] = dst_ref[...]
    first_out[...] = dot_nt(mix1, cotangent)
    base_out[...] = dot_nn(series_ref[...], mixing(self_ref[...]))
    mix1_out[...] = mix1
    mix2_out[...] = mix2


def prepare(*ins):
    outs = [
        array(GROUP, 448, 128),
        array(384, 128, dtype=F32),
        array(128, 384, dtype=F32),
        array(384, 384),
        array(384, 384),
    ]
    return call(prepare_kernel, 1, ins, outs, flops=3 * 2 * 128 * 384 * 384, vmem=60 * MIB)


def stats_kernel(own_ref, other_ref, dst_ref, out_ref, state, dst):
    @at_step(0)
    def _():
        state[...] = jnp.zeros_like(state)
        dst[...] = side_by_side(dst_ref[:, 384:448, :])

    lifted = jnp.maximum(dot_tn(side_by_side(pick(own_ref, other_ref)), dst[...]), 0.0)
    old = state[0:1, :]
    new = jnp.maximum(old, jnp.max(lifted, axis=0, keepdims=True))
    total = jnp.sum(jnp.exp(lifted - new), axis=0, keepdims=True)
    state[1:2, :] = state[1:2, :] * jnp.exp(old - new) + total
    state[0:1, :] = new

    @at_step(1)
    def _():
        out_ref[...] = jnp.broadcast_to(state[...][None], out_ref.shape)


def softmax_stats(own, other, dst):
    rows = dst.shape[0] * 128
    scratch = [pltpu.VMEM((2, rows), F32), pltpu.VMEM((64, rows), BF16)]
    outs = [array(GROUP, 2, rows, dtype=F32)]
    size = 2 * rows * rows
    return call(stats_kernel, 2, (own, other, dst), outs, scratch, 128 * size, size)[0]


def weights_of(src, dst, norm_ref):
    scores = dot_tn(src, dst)
    weights = jnp.exp(jnp.maximum(scores, 0.0) - norm_ref[0:1, :]) * norm_ref[1:2, :]
    return scores, weights


def hops_kernel(
    own_ref, other_ref, series_own, series_other, dst_ref, stats_ref,
    norm_ref, hop_ref, own_out, other_out, total, dst, second,
):
    @at_step(0)
    def _():
        peak = stats_ref[0, 0:1, :]
        for d in range(1, GROUP):
            peak = jnp.maximum(peak, stats_ref[d, 0:1, :])
        row_sum = jnp.zeros_like(peak)
        for d in range(GROUP):
            row_sum += stats_ref[d, 1:2, :] * jnp.exp(stats_ref[d, 0:1, :] - peak)
        norm_ref[0:1, :] = peak
        norm_ref[1:2, :] = 1.0 / row_sum
        second[...] = side_by_side(dst_ref[:, 0:384, :])
        dst[...] = side_by_side(dst_ref[:, 384:448, :])

    src = side_by_side(pick(own_ref, other_ref))
    adjacency = weights_of(src, dst[...], norm_ref)[1].astype(BF16)
    carried = dot_nt(second[...], adjacency).astype(BF16)
    for block in range(GROUP):
        put(own_out, other_out, block, carried[:, nodes(block)])
    accumulate(total, dot_tn(pick(series_own, series_other), adjacency))

    @at_step(1)
    def _():
        for block in range(GROUP):
            hop_ref[block] = total[:, nodes(block)].astype(BF16)


def first_hops(*ins):
    rows = GROUP * 128
    outs = [array(2, rows, dtype=F32)] + [array(GROUP, 384, 128)] * 3
    scratch = [pltpu.VMEM((384, rows), F32), pltpu.VMEM((64, rows), BF16), pltpu.VMEM((384, rows), BF16)]
    size = 2 * rows * rows
    return call(hops_kernel, 2, ins, outs, scratch, 2 * 832 * size, size)


def sum_of(pack_ref, start, stop):
    total = pack_ref[0, start:stop, :].astype(F32)
    for d in range(1, GROUP):
        total += pack_ref[d, start:stop, :].astype(F32)
    return total


def cores_kernel(own_ref, other_ref, *outs):
    for place, out in enumerate(outs):
        pair = slice(2 * place, 2 * place + 2)
        out[...] = (own_ref[pair].astype(F32) + other_ref[pair].astype(F32)).astype(BF16)


def join_kernel(hop_ref, a_ref, b_ref, c_ref, d_ref, mixed_ref, hop_out, mine_out, next_out):
    def total(place):
        parts = [ref[place].astype(F32) for ref in (a_ref, b_ref, c_ref, d_ref)]
        return (parts[0] + parts[1]) + (parts[2] + parts[3])

    hop = sum_of(hop_ref, 0, 384).T.astype(BF16)
    hop_out[...] = hop
    mine_out[...] = mixed_ref[...] + total(0)
    next_out[0:384, :] = total(1).astype(BF16)
    for part in range(3):
        next_out[384 + 128 * part : 512 + 128 * part, :] = hop[:, nodes(part)]


def first_grad_kernel(mine_ref, next_ref, hop_ref, out_ref, pair_ref):
    pair_ref[0] = hop_ref[...]
    for part in range(3):
        pair_ref[1, :, nodes(part)] = next_ref[384 + 128 * part : 512 + 128 * part, :]
    grad = (mine_ref[...] + next_ref[0:384, :].astype(F32)).astype(BF16)
    for block in range(GROUP):
        out_ref[block] = grad


def three_terms(value):
    high = value.astype(BF16).astype(F32)
    middle = (value - high).astype(BF16).astype(F32)
    return [high, middle, value - high - middle]


SECOND, ABOVE, BELOW, INNER, SHIFT, LAST = 0, 384, 448, 512, 536, 544


def pieces_kernel(*refs):
    for place, ref in enumerate(refs[:-1]):
        refs[-1][256 * place : 256 * place + 256, :] = ref[...].reshape(256, 384)


def after_kernel(first_ref, *refs):
    del first_ref
    pieces_kernel(*refs)


def grad_kernel(
    own_ref, other_ref, series_own, series_other, hop_ref, dst_ref, norm_ref, first_ref,
    pack_ref, shift_ref, own_out, other_out, inner, mass, above, below, dst, grads, adj, wide, second,
):
    step = pl.program_id(0)
    half = step % 2

    @at_step(0)
    def _():
        dst[...] = side_by_side(dst_ref[:, 384:448, :])
        grads[0:384, :] = side_by_side(dst_ref[:, 0:384, :])
        grads[384:768, :] = side_by_side(first_ref)

    src = side_by_side(jnp.where(half == 0, own_ref[...], other_ref[...]))

    @pl.when(step < 2)
    def _():
        scores, weights = weights_of(src, dst[...], norm_ref)
        hop = hop_ref[...]
        series = jnp.where(half == 0, series_own[...], series_other[...])
        adj_grad = dot_nn(jnp.concatenate([hop, series], axis=1), grads[...])
        adj[half] = adj_grad
        wide[half] = jnp.where(scores > 0.0, weights, 0.0)
        hop_part = dot_tn(hop, weights.astype(BF16))
        second[...] = jnp.where(step == 0, hop_part, second[...] + hop_part)
        total = jnp.sum(weights * adj_grad, axis=0, keepdims=True)
        weight = jnp.sum(weights, axis=0, keepdims=True)
        inner[...] = jnp.where(step == 0, total, inner[...] + total)
        mass[...] = jnp.where(step == 0, weight, mass[...] + weight)

    @pl.when(step >= 2)
    def _():
        shift = jnp.where(mass[...] > 1e-30, inner[...] / jnp.maximum(mass[...], 1e-30), 0.0)
        masked = wide[half]
        graded = (masked * (adj[half] - shift)).astype(BF16)
        masked = masked.astype(BF16)
        up, low = dot_nn(src, graded), dot_nn(src, masked)
        above[...] = jnp.where(step == 2, up, above[...] + up)
        below[...] = jnp.where(step == 2, low, below[...] + low)
        d_src = dot_nt(dst[...], graded)

        @pl.when(half == 0)
        def _():
            for block in range(GROUP):
                own_out[block] = d_src[:, nodes(block)]

        @pl.when(half == 1)
        def _():
            shift_ref[...] = shift
            for block in range(GROUP):
                other_out[block] = d_src[:, nodes(block)]
            sums = [term[:, nodes(block)] for term in three_terms(inner[...]) for block in range(GROUP)]
            sums = jnp.concatenate(sums, axis=0)
            shifts = jnp.concatenate(three_terms(shift), axis=0)
            for block in range(GROUP):
                tail = jnp.concatenate([sums, shifts[:, nodes(block)], jnp.zeros((5, 128), F32)], axis=0)
                pack_ref[block, SECOND:ABOVE, :] = second[:, nodes(block)].astype(BF16)
                pack_ref[block, ABOVE:BELOW, :] = above[:, nodes(block)].astype(BF16)
                pack_ref[block, BELOW:INNER, :] = below[:, nodes(block)].astype(BF16)
                pack_ref[block, INNER:LAST, :] = tail.astype(BF16)


def embed_grads(*ins):
    rows = GROUP * 128
    outs = [
        array(GROUP, LAST, 128),
        array(1, rows, dtype=F32),
        array(GROUP, 64, 128, dtype=F32),
        array(GROUP, 64, 128, dtype=F32),
    ]
    scratch = [
        pltpu.VMEM((1, rows), F32),
        pltpu.VMEM((1, rows), F32),
        pltpu.VMEM((64, rows), F32),
        pltpu.VMEM((64, rows), F32),
        pltpu.VMEM((64, rows), BF16),
        pltpu.VMEM((768, rows), BF16),
        pltpu.VMEM((2, rows, rows), F32),
        pltpu.VMEM((2, rows, rows), F32),
        pltpu.VMEM((384, rows), F32),
    ]


    def first_pass(a):
        return pl.BlockSpec((a.shape[0] // 2, a.shape[1]), lambda i: (jnp.minimum(i, 1), 0))

    size = 2 * rows * rows
    return call(
        grad_kernel, 4, ins, outs, scratch, 2 * 1408 * size, size, kinds={4: first_pass}, vmem=46 * MIB
    )


def inner_of(pack_ref):
    terms = sum_of(pack_ref, INNER, LAST)
    return terms[0:8] + (terms[8:16] + terms[16:24])


def src_kernel(
    own_ref, other_ref, dst_ref, norm_ref, pack_ref, shift_ref, own_part, other_part, own_out, other_out, scaled, dst
):
    @at_step(0)
    def _():
        dst[...] = side_by_side(dst_ref[:, 384:448, :])
        inner = inner_of(pack_ref)
        for block in range(GROUP):
            change = shift_ref[:, nodes(block)] - inner[block : block + 1, :]
            scaled[:, nodes(block)] = (dst[:, nodes(block)].astype(F32) * change).astype(BF16)

    scores, weights = weights_of(side_by_side(pick(own_ref, other_ref)), dst[...], norm_ref)
    part = dot_nt(scaled[...], jnp.where(scores > 0.0, weights, 0.0).astype(BF16))

    me = lax.axis_index("col")
    for block in range(GROUP):
        place = (me // 4 + 4 - block // 2) % 4 * 2 + (me // 2 + block) % 2

        @at_step(0)
        def _(block=block, place=place):
            own_out[place] = own_part[block] + part[:, nodes(block)]

        @at_step(1)
        def _(block=block, place=place):
            other_out[place] = other_part[block] + part[:, nodes(block)]


def src_grads(*ins):
    rows = ins[2].shape[0] * 128
    outs = [array(GROUP, 64, 128, dtype=F32), array(GROUP, 64, 128, dtype=F32)]
    scratch = [pltpu.VMEM((64, rows), BF16), pltpu.VMEM((64, rows), BF16)]
    size = 2 * rows * rows
    return call(src_kernel, 2, ins, outs, scratch, 256 * size, size)


def output_kernel(pack_ref, hop_ref, base_ref, mix1_ref, mix2_ref, out_ref, d_dst_ref):
    second = sum_of(pack_ref, SECOND, ABOVE).T.astype(BF16)
    mixed = base_ref[...] + dot_nn(hop_ref[...], mix1_ref[...]) + dot_nn(second, mix2_ref[...])
    out_ref[...] = mixed.astype(BF16)
    me = lax.axis_index("row")
    inner = inner_of(pack_ref)
    places = lax.broadcasted_iota(jnp.int32, inner.shape, 0)
    inner = jnp.sum(jnp.where(places == me, inner, 0.0), axis=0, keepdims=True)
    d_dst = jnp.zeros((64, 128), F32)
    for d in range(GROUP):
        tail = pack_ref[d, INNER:LAST, :].astype(F32)
        shift = tail[24:25] + (tail[25:26] + tail[26:27])
        above, below = pack_ref[d, ABOVE:BELOW, :].astype(F32), pack_ref[d, BELOW:INNER, :].astype(F32)
        d_dst += above + (shift - inner) * below
    d_dst_ref[...] = d_dst


def local(dst_embed, src_embed, series, w_self, w_hop1, w_hop2, cotangent):
    src = src_embed.T
    src_own, src_other = (jnp.concatenate(p) for p in gather_src(jnp.stack([src, to_chip(src, 0, 1)])))
    pieces = gather_chips(jnp.stack([series, to_chip(series, 0, 1)]))
    dst, first_mixed, base, mix1, mix2 = prepare(dst_embed.T, series, w_self, w_hop1, w_hop2, cotangent)
    dst = exchange_dst(dst)
    stats = softmax_stats(src_own, src_other, dst)
    series_own = call(after_kernel, 1, (stats, *pieces), [array(GROUP * 128, 384)])[0]
    series_other = swap_cores(series_own)
    stats = exchange_dst(stats)

    norm, hop, own, other = first_hops(src_own, src_other, series_own, series_other, dst, stats)
    hop = exchange_dst(hop)
    pairs = call(cores_kernel, 1, (own, swap_cores(other)), [array(2, 384, 128)] * 4)
    pairs = [pairs[0]] + [to_chip(pairs[dx], -dx, 0) for dx in range(1, 4)]
    hop, mine, near = call(
        join_kernel, 1, (hop, *pairs, first_mixed),
        [array(128, 384), array(384, 128, dtype=F32), array(768, 128)],
    )
    first, hop_pair = call(
        first_grad_kernel, 1, (mine, to_chip(near, 0, 1), hop), [array(GROUP, 384, 128), array(2, 128, 384)]
    )
    first = exchange_dst(first)
    hop_own, hop_other = gather_src(hop_pair)
    hop_all = call(pieces_kernel, 1, (*hop_own, *hop_other), [array(2 * GROUP * 128, 384)])[0]

    pack, shift, own, other = embed_grads(
        src_own, src_other, series_own, series_other, hop_all, dst, norm, first
    )
    pack = exchange_dst(pack)
    own, other = src_grads(src_own, src_other, dst, norm, pack, shift, own, other)
    output, d_dst = call(
        output_kernel, 1, (pack, hop, base, mix1, mix2), [array(128, 384), array(64, 128, dtype=F32)],
        flops=4 * 128 * 384 * 384,
    )
    d_src = jnp.sum(exchange_src(own + swap_cores(other)), axis=0)
    return output, d_dst.T, d_src.T


def solution(mesh):
    blocks = P(("row", "col"), None)
    return jax.shard_map(
        local,
        mesh=mesh,
        in_specs=(blocks, blocks, blocks, P(), P(), P(), blocks),
        out_specs=(blocks, blocks, blocks),
        check_vma=False,
    )
```

```python
import jax
import jax.numpy as jnp
from jax import lax
from jax.experimental import pallas as pl
from jax.experimental.pallas import tpu as pltpu
from jax.sharding import PartitionSpec as P

BF16 = jnp.bfloat16
F32 = jnp.float32
GROUP = 8
MIB = 1024 * 1024
VMEM_BYTES = 28 * MIB

OTHER_CORE = [(i, i ^ 1) for i in range(16)]


def dot_nn(a, b):
    return lax.dot_general(a, b, (((1,), (0,)), ((), ())), preferred_element_type=F32)


def dot_nt(a, b):
    return lax.dot_general(a, b, (((1,), (1,)), ((), ())), preferred_element_type=F32)


def dot_tn(a, b):
    return lax.dot_general(a, b, (((0,), (0,)), ((), ())), preferred_element_type=F32)


def exchange_dst(blocks):
    return lax.all_to_all(blocks, "row", 0, 0)


def exchange_col(blocks):
    return lax.all_to_all(blocks, "col", 0, 0)


def swap_cores(blocks):
    return lax.ppermute(blocks, "col", OTHER_CORE)


def to_chip(blocks, x_step, z_step):
    pairs = []
    for i in range(16):
        x, z, core = i // 4, i // 2 % 2, i % 2
        pairs.append((i, (x + x_step) % 4 * 4 + (z + z_step) % 2 * 2 + core))
    return lax.ppermute(blocks, "col", pairs)


def gather_src(block):
    pair = jnp.stack([block, to_chip(block, 0, 1)])
    pairs = [pair] + [to_chip(pair, dx, 0) for dx in range(1, 4)]
    return jnp.concatenate(pairs), jnp.concatenate([swap_cores(p) for p in pairs])


def array(*shape, dtype=BF16):
    return jax.ShapeDtypeStruct(shape, dtype)


def whole(a):
    return pl.BlockSpec(a.shape, lambda *_: (0,) * len(a.shape))


def by_step(a):
    return pl.BlockSpec((a.shape[0] // 2,) + a.shape[1:], lambda i, *_: (i,) + (0,) * (len(a.shape) - 1))


def call(kernel, steps, ins, outs, scratch=(), flops=0, exps=0, kinds=None, vmem=VMEM_BYTES):
    kinds = kinds or {}
    sizes = [a.size * a.dtype.itemsize for a in list(ins) + list(outs)]
    specs = [kinds.get(i, whole)(a) for i, a in enumerate(list(ins) + list(outs))]
    return pl.pallas_call(
        kernel,
        grid=(steps,),
        in_specs=specs[: len(ins)],
        out_specs=specs[len(ins) :],
        out_shape=outs,
        scratch_shapes=scratch,
        compiler_params=pltpu.CompilerParams(vmem_limit_bytes=vmem),
        cost_estimate=pl.CostEstimate(flops=flops, bytes_accessed=sum(sizes), transcendentals=exps),
    )(*ins)


def at_step(step):
    return pl.when(pl.program_id(0) == step)


def pick(own_ref, other_ref):
    return jnp.where(pl.program_id(0) == 0, own_ref[...], other_ref[...])


def put(own_ref, other_ref, block, value):
    @at_step(0)
    def _():
        own_ref[block] = value

    @at_step(1)
    def _():
        other_ref[block] = value


def accumulate(total, part):
    @at_step(0)
    def _():
        total[...] = part

    @at_step(1)
    def _():
        total[...] += part


def side_by_side(blocks):
    return jnp.concatenate([blocks[b] for b in range(GROUP)], axis=1)


def nodes(block):
    return slice(128 * block, 128 * block + 128)


def series_of(packed):
    return jnp.concatenate([packed[b, 0:128, :] for b in range(GROUP)], axis=0)


def src_of(packed):
    pieces = [packed[:, 128:160, 0:128], packed[:, 128:160, 128:256]]
    return side_by_side(jnp.concatenate(pieces, axis=1))


def mixing(weight):
    size, chan = 384, weight.shape[0]
    place = lax.broadcasted_iota(jnp.int32, (size, chan), 0) % chan
    repeat = jnp.where(place == lax.broadcasted_iota(jnp.int32, (size, chan), 1), 1.0, 0.0).astype(BF16)
    tiled = dot_nt(dot_nn(repeat, weight).astype(BF16), repeat)
    rows = lax.broadcasted_iota(jnp.int32, (size, size), 0) // chan
    cols = lax.broadcasted_iota(jnp.int32, (size, size), 1) // chan
    return jnp.where(rows == cols, tiled, 0.0).astype(BF16)


def source_kernel(src_ref, series_ref, src_out):
    src_out[0:128, :] = series_ref[...]
    src_out[128:160, 0:128] = src_ref[0:32, :]
    src_out[128:160, 128:256] = src_ref[32:64, :]
    src_out[128:160, 256:384] = jnp.zeros((32, 128), BF16)


def prepare_kernel(
    dst_ref, series_ref, self_ref, hop1_ref, hop2_ref, cotangent_ref, dst_out, first_out, base_out, mix1_out, mix2_out
):
    mix1, mix2 = mixing(hop1_ref[...]), mixing(hop2_ref[...])
    cotangent = cotangent_ref[...]
    second = dot_nt(mix2, cotangent).astype(BF16)
    for block in range(GROUP):
        dst_out[block, 0:384, :] = second
        dst_out[block, 384:448, :] = dst_ref[...]
    first_out[...] = dot_nt(mix1, cotangent)
    base_out[...] = dot_nn(series_ref[...], mixing(self_ref[...]))
    mix1_out[...] = mix1
    mix2_out[...] = mix2


def prepare(*ins):
    outs = [
        array(GROUP, 448, 128),
        array(384, 128, dtype=F32),
        array(128, 384, dtype=F32),
        array(384, 384),
        array(384, 384),
    ]
    return call(prepare_kernel, 1, ins, outs, flops=3 * 2 * 128 * 384 * 384, vmem=60 * MIB)


def stats_kernel(own_ref, other_ref, dst_ref, out_ref, state, dst):
    @at_step(0)
    def _():
        state[...] = jnp.zeros_like(state)
        dst[...] = side_by_side(dst_ref[:, 384:448, :])

    lifted = jnp.maximum(dot_tn(src_of(pick(own_ref, other_ref)), dst[...]), 0.0)
    old = state[0:1, :]
    new = jnp.maximum(old, jnp.max(lifted, axis=0, keepdims=True))
    total = jnp.sum(jnp.exp(lifted - new), axis=0, keepdims=True)
    state[1:2, :] = state[1:2, :] * jnp.exp(old - new) + total
    state[0:1, :] = new

    @at_step(1)
    def _():
        out_ref[...] = jnp.broadcast_to(state[...][None], out_ref.shape)


def softmax_stats(own, other, dst):
    rows = dst.shape[0] * 128
    scratch = [pltpu.VMEM((2, rows), F32), pltpu.VMEM((64, rows), BF16)]
    outs = [array(GROUP, 2, rows, dtype=F32)]
    size = 2 * rows * rows
    return call(stats_kernel, 2, (own, other, dst), outs, scratch, 128 * size, size)[0]


def weights_of(src, dst, norm_ref):
    scores = dot_tn(src, dst)
    weights = jnp.exp(jnp.maximum(scores, 0.0) - norm_ref[0:1, :]) * norm_ref[1:2, :]
    return scores, weights


def hops_kernel(
    own_ref, other_ref, dst_ref, stats_ref, norm_ref, hop_ref, own_out, other_out, total, dst, second
):
    @at_step(0)
    def _():
        peak = stats_ref[0, 0:1, :]
        for d in range(1, GROUP):
            peak = jnp.maximum(peak, stats_ref[d, 0:1, :])
        row_sum = jnp.zeros_like(peak)
        for d in range(GROUP):
            row_sum += stats_ref[d, 1:2, :] * jnp.exp(stats_ref[d, 0:1, :] - peak)
        norm_ref[0:1, :] = peak
        norm_ref[1:2, :] = 1.0 / row_sum
        second[...] = side_by_side(dst_ref[:, 0:384, :])
        dst[...] = side_by_side(dst_ref[:, 384:448, :])

    packed = pick(own_ref, other_ref)
    adjacency = weights_of(src_of(packed), dst[...], norm_ref)[1].astype(BF16)
    carried = dot_nt(second[...], adjacency).astype(BF16)
    for block in range(GROUP):
        put(own_out, other_out, block, carried[:, nodes(block)])
    accumulate(total, dot_tn(series_of(packed), adjacency))

    @at_step(1)
    def _():
        for block in range(GROUP):
            hop_ref[block] = total[:, nodes(block)].astype(BF16)


def first_hops(own, other, dst, stats):
    rows = dst.shape[0] * 128
    outs = [array(2, rows, dtype=F32)] + [array(GROUP, 384, 128)] * 3
    scratch = [pltpu.VMEM((384, rows), F32), pltpu.VMEM((64, rows), BF16), pltpu.VMEM((384, rows), BF16)]
    size = 2 * rows * rows
    return call(hops_kernel, 2, (own, other, dst, stats), outs, scratch, 2 * 832 * size, size)


def sum_of(pack_ref, start, stop):
    total = pack_ref[0, start:stop, :].astype(F32)
    for d in range(1, GROUP):
        total += pack_ref[d, start:stop, :].astype(F32)
    return total


def cores_kernel(own_ref, other_ref, *outs):
    for place, out in enumerate(outs):
        pair = slice(2 * place, 2 * place + 2)
        out[...] = (own_ref[pair].astype(F32) + other_ref[pair].astype(F32)).astype(BF16)


def join_kernel(hop_ref, a_ref, b_ref, c_ref, d_ref, hop_out, mine_out, other_out):
    def total(place):
        parts = [ref[place].astype(F32) for ref in (a_ref, b_ref, c_ref, d_ref)]
        return (parts[0] + parts[1]) + (parts[2] + parts[3])

    other_out[...] = total(1).astype(BF16)
    hop_out[...] = sum_of(hop_ref, 0, 384).T.astype(BF16)
    mine_out[...] = total(0)


def first_grad_kernel(mixed_ref, mine_ref, other_ref, out_ref):
    grad = (mixed_ref[...] + (mine_ref[...] + other_ref[...].astype(F32))).astype(BF16)
    for block in range(GROUP):
        out_ref[block] = grad


def three_terms(value):
    high = value.astype(BF16).astype(F32)
    middle = (value - high).astype(BF16).astype(F32)
    return [high, middle, value - high - middle]


SECOND, ABOVE, BELOW, INNER, SHIFT, LAST = 0, 384, 448, 512, 536, 544


def grad_kernel(
    own_ref, other_ref, hop_own_ref, hop_other_ref, dst_ref, norm_ref, first_ref,
    pack_ref, shift_ref, own_out, other_out, inner, mass, above, below, dst, grads, adj, wide, second,
):
    step = pl.program_id(0)
    half = step % 2

    @at_step(0)
    def _():
        dst[...] = side_by_side(dst_ref[:, 384:448, :])
        grads[0:384, :] = side_by_side(dst_ref[:, 0:384, :])
        grads[384:768, :] = side_by_side(first_ref)

    packed = jnp.where(half == 0, own_ref[...], other_ref[...])
    src = src_of(packed)

    @pl.when(step < 2)
    def _():
        scores, weights = weights_of(src, dst[...], norm_ref)
        hop = jnp.where(half == 0, hop_own_ref[...], hop_other_ref[...])
        adj_grad = dot_nn(jnp.concatenate([hop, series_of(packed)], axis=1), grads[...])
        adj[half] = adj_grad
        wide[half] = jnp.where(scores > 0.0, weights, 0.0)
        hop_part = dot_tn(hop, weights.astype(BF16))
        second[...] = jnp.where(step == 0, hop_part, second[...] + hop_part)
        total = jnp.sum(weights * adj_grad, axis=0, keepdims=True)
        weight = jnp.sum(weights, axis=0, keepdims=True)
        inner[...] = jnp.where(step == 0, total, inner[...] + total)
        mass[...] = jnp.where(step == 0, weight, mass[...] + weight)

    @pl.when(step >= 2)
    def _():
        shift = jnp.where(mass[...] > 1e-30, inner[...] / jnp.maximum(mass[...], 1e-30), 0.0)
        masked = wide[half]
        graded = (masked * (adj[half] - shift)).astype(BF16)
        masked = masked.astype(BF16)
        up, low = dot_nn(src, graded), dot_nn(src, masked)
        above[...] = jnp.where(step == 2, up, above[...] + up)
        below[...] = jnp.where(step == 2, low, below[...] + low)
        d_src = dot_nt(dst[...], graded)

        @pl.when(half == 0)
        def _():
            for block in range(GROUP):
                own_out[block] = d_src[:, nodes(block)]

        @pl.when(half == 1)
        def _():
            shift_ref[...] = shift
            for block in range(GROUP):
                other_out[block] = d_src[:, nodes(block)]
            sums = [term[:, nodes(block)] for term in three_terms(inner[...]) for block in range(GROUP)]
            sums = jnp.concatenate(sums, axis=0)
            shifts = jnp.concatenate(three_terms(shift), axis=0)
            for block in range(GROUP):
                tail = jnp.concatenate([sums, shifts[:, nodes(block)], jnp.zeros((5, 128), F32)], axis=0)
                pack_ref[block, SECOND:ABOVE, :] = second[:, nodes(block)].astype(BF16)
                pack_ref[block, ABOVE:BELOW, :] = above[:, nodes(block)].astype(BF16)
                pack_ref[block, BELOW:INNER, :] = below[:, nodes(block)].astype(BF16)
                pack_ref[block, INNER:LAST, :] = tail.astype(BF16)


def embed_grads(*ins):
    rows = ins[4].shape[0] * 128
    outs = [
        array(GROUP, LAST, 128),
        array(1, rows, dtype=F32),
        array(GROUP, 64, 128, dtype=F32),
        array(GROUP, 64, 128, dtype=F32),
    ]
    scratch = [
        pltpu.VMEM((1, rows), F32),
        pltpu.VMEM((1, rows), F32),
        pltpu.VMEM((64, rows), F32),
        pltpu.VMEM((64, rows), F32),
        pltpu.VMEM((64, rows), BF16),
        pltpu.VMEM((768, rows), BF16),
        pltpu.VMEM((2, rows, rows), F32),
        pltpu.VMEM((2, rows, rows), F32),
        pltpu.VMEM((384, rows), F32),
    ]

    size = 2 * rows * rows
    return call(
        grad_kernel, 4, ins, outs, scratch, 2 * 1408 * size, size, vmem=46 * MIB
    )


def inner_of(pack_ref):
    terms = sum_of(pack_ref, INNER, LAST)
    return terms[0:8] + (terms[8:16] + terms[16:24])


def src_kernel(
    own_ref, other_ref, dst_ref, norm_ref, pack_ref, shift_ref, own_part, other_part, out_ref, scaled, dst
):
    @at_step(0)
    def _():
        dst[...] = side_by_side(dst_ref[:, 384:448, :])
        inner = inner_of(pack_ref)
        for block in range(GROUP):
            change = shift_ref[:, nodes(block)] - inner[block : block + 1, :]
            scaled[:, nodes(block)] = (dst[:, nodes(block)].astype(F32) * change).astype(BF16)

    scores, weights = weights_of(src_of(pick(own_ref, other_ref)), dst[...], norm_ref)
    part = dot_nt(scaled[...], jnp.where(scores > 0.0, weights, 0.0).astype(BF16))

    me = lax.axis_index("col")
    for block in range(GROUP):
        place = (me // 4 + 4 - block // 2) % 4 * 2 + (me // 2 + block) % 2

        @at_step(0)
        def _(block=block, place=place):
            out_ref[place * 2 + me % 2] = (own_part[block] + part[:, nodes(block)]).astype(BF16)

        @at_step(1)
        def _(block=block, place=place):
            out_ref[place * 2 + 1 - me % 2] = (other_part[block] + part[:, nodes(block)]).astype(BF16)


def src_grads(*ins):
    rows = ins[2].shape[0] * 128
    outs = [array(2 * GROUP, 64, 128)]
    scratch = [pltpu.VMEM((64, rows), BF16), pltpu.VMEM((64, rows), BF16)]
    size = 2 * rows * rows
    return call(src_kernel, 2, ins, outs, scratch, 256 * size, size)[0]


def output_kernel(pack_ref, hop_ref, base_ref, mix1_ref, mix2_ref, out_ref, d_dst_ref):
    second = sum_of(pack_ref, SECOND, ABOVE).T.astype(BF16)
    mixed = base_ref[...] + dot_nn(hop_ref[...], mix1_ref[...]) + dot_nn(second, mix2_ref[...])
    out_ref[...] = mixed.astype(BF16)
    me = lax.axis_index("row")
    inner = inner_of(pack_ref)
    places = lax.broadcasted_iota(jnp.int32, inner.shape, 0)
    inner = jnp.sum(jnp.where(places == me, inner, 0.0), axis=0, keepdims=True)
    d_dst = jnp.zeros((64, 128), F32)
    for d in range(GROUP):
        tail = pack_ref[d, INNER:LAST, :].astype(F32)
        shift = tail[24:25] + (tail[25:26] + tail[26:27])
        above, below = pack_ref[d, ABOVE:BELOW, :].astype(F32), pack_ref[d, BELOW:INNER, :].astype(F32)
        d_dst += above + (shift - inner) * below
    d_dst_ref[...] = d_dst


def local(dst_embed, src_embed, series, w_self, w_hop1, w_hop2, cotangent):
    src = call(source_kernel, 1, (src_embed.T, series), [array(160, 384)], vmem=60 * MIB)[0]
    src_own, src_other = gather_src(src)
    dst, first_mixed, base, mix1, mix2 = prepare(dst_embed.T, series, w_self, w_hop1, w_hop2, cotangent)
    dst = exchange_dst(dst)
    stats = exchange_dst(softmax_stats(src_own, src_other, dst))

    norm, hop, own, other = first_hops(src_own, src_other, dst, stats)
    hop = exchange_dst(hop)
    pairs = call(cores_kernel, 1, (own, swap_cores(other)), [array(2, 384, 128)] * 4)
    pairs = [pairs[0]] + [to_chip(pairs[dx], -dx, 0) for dx in range(1, 4)]
    hop, mine, rest = call(
        join_kernel, 1, (hop, *pairs), [array(128, 384), array(384, 128, dtype=F32), array(384, 128)]
    )
    rest = to_chip(rest, 0, 1)
    first = call(first_grad_kernel, 1, (first_mixed, mine, rest), [array(GROUP, 384, 128)])[0]
    first = exchange_dst(first)
    hop_own, hop_other = (half.reshape(-1, 384) for half in gather_src(hop))

    pack, shift, own, other = embed_grads(src_own, src_other, hop_own, hop_other, dst, norm, first)
    pack = exchange_dst(pack)
    d_src = src_grads(src_own, src_other, dst, norm, pack, shift, own, other)
    output, d_dst = call(
        output_kernel, 1, (pack, hop, base, mix1, mix2), [array(128, 384), array(64, 128, dtype=F32)],
        flops=4 * 128 * 384 * 384,
    )
    d_src = jnp.sum(exchange_col(d_src).astype(F32), axis=0)
    return output, d_dst.T, d_src.T


def solution(mesh):
    blocks = P(("row", "col"), None)
    return jax.shard_map(
        local,
        mesh=mesh,
        in_specs=(blocks, blocks, blocks, P(), P(), P(), blocks),
        out_specs=(blocks, blocks, blocks),
        check_vma=False,
    )
```
